32 devices in a mesh: expert: 4 (over z), context: 2 (over core), dp: 4 (over y, x).
Axes of the slice: x: 2, y: 2, z: 4, core: 2. Of those that a mesh axis runs over, the one named last changes fastest.
Arguments:
- tokens: bfloat16 [4, 1024, 2048], P('dp', ('expert', 'context')), may hold values from -6 to 6
- cotangent: bfloat16 [4, 1024, 2048], P('dp', ('expert', 'context')), may hold values from -6 to 6
- segments: int32 [4, 1024], P('dp'), may hold values from 0 to 2, as said below
- expert_ids: int32 [4, 1024, 4], P('dp', ('expert', 'context')), may hold values from 0 to 7, all different within a row
- slot_order: int32 [4, 8, 512], P('dp', ('expert', 'context')), may hold values from 0 to 511, each once within a row
- gate_weights: float32 [4, 1024, 4], P('dp', ('expert', 'context')), may hold values from 0.1 to 0.4
- qkv_weight: bfloat16 [2048, 6144], P(('expert', 'context', 'dp')), may hold values from -0.125 to 0.125
- qkv_bias: bfloat16 [6144], P(('expert', 'context', 'dp')), may hold values from -4 to 4
- out_weight: bfloat16 [2048, 2048], P(('expert', 'context', 'dp')), may hold values from -2 to 2
- norm_attn: bfloat16 [2048], P(('expert', 'context', 'dp')), may hold values from 0.5 to 1.5
- norm_ffn: bfloat16 [2048], P(('expert', 'context', 'dp')), may hold values from 0.5 to 1.5
- shared_gate_up: bfloat16 [2, 2048, 5632], P(None, ('context', 'dp'), 'expert'), may hold values from -0.125 to 0.125
- shared_down: bfloat16 [5632, 2048], P('expert', ('context', 'dp')), may hold values from -0.15625 to 0.15625
- shared_gate: bfloat16 [2048], P(('expert', 'context', 'dp')), may hold values from -0.125 to 0.125
- expert_gate_up: bfloat16 [8, 2048, 2816], P('expert', ('context', 'dp')), may hold values from -0.125 to 0.125
- expert_down: bfloat16 [8, 1408, 2048], P('expert', ('context', 'dp')), may hold values from -0.3125 to 0.3125
Outputs:
- block_output: bfloat16 [4, 1024, 2048], P('dp', ('expert', 'context'))
- input_grad: float32 [4, 1024, 2048], P('dp', ('expert', 'context'))
- qkv_weight_grad: float32 [2048, 6144], P(('expert', 'context', 'dp'))
- qkv_bias_grad: float32 [6144], P(('expert', 'context', 'dp'))
- out_weight_grad: float32 [2048, 2048], P(('expert', 'context', 'dp'))
- norm_attn_grad: float32 [2048], P(('expert', 'context', 'dp'))
- norm_ffn_grad: float32 [2048], P(('expert', 'context', 'dp'))
- shared_gate_up_grad: float32 [2, 2048, 5632], P(None, ('context', 'dp'), 'expert')
- shared_down_grad: float32 [5632, 2048], P('expert', ('context', 'dp'))
- shared_gate_grad: float32 [2048], P(('expert', 'context', 'dp'))
- expert_gate_up_grad: float32 [8, 2048, 2816], P('expert', ('context', 'dp'))
- expert_down_grad: float32 [8, 1408, 2048], P('expert', ('context', 'dp'))
The draws below stay inside these ranges and needn't reach their ends.
Inputs may be any that keep to these rules, and one draw needn't show every extreme that they name: `segments`: each sequence holds exactly three documents, numbered 0 to 2 in order of position, none empty. `expert_ids`: each row names 4 different experts. `slot_order`: each row is a permutation of the block's 128 * 4 pairs.
All inputs are finite; a program needn't handle non-finite values.
Results may differ from the reference program's by a relative error of at most 0.017.
Values may be sent and summed in bfloat16 or wider, within the bound.
No kernel may reach another device: no remote copies, remote signals or barrier semaphores. Data moves between devices by JAX's collectives and lax.ppermute only.
A program may use at most 640 MiB of HBM per device.

```python
import math
import jax
import jax.numpy as jnp
from jax import lax

D = 2048
HEADS = 16
HEAD_DIM = 128
FF = 1408
FFS = 5632
TOPK = 4
TOK_DEV = 128
EXPERTS = 8
SEQS = 4
SPANS = 8
LEN = 1024
CAP = 72


def draw_segments(key, part):
    key = jax.random.fold_in(key, 7)
    key_low, key_high = jax.random.split(key, 2)
    cut_low = jax.random.randint(key_low, (SEQS, 1), 1, TOK_DEV)
    cut_high = jax.random.randint(key_high, (SEQS, 1), LEN - TOK_DEV + 1, LEN)
    places = jnp.arange(LEN)[None, :]
    total = (places >= cut_low).astype(jnp.int32) + (places >= cut_high).astype(jnp.int32)
    return total.astype(jnp.int32)


def block_scale(rng, shape, cuts, least, high):
    loudness = 1.0
    for axis_at, blocks in cuts:
        draws = jax.random.uniform(jax.random.fold_in(jax.random.fold_in(rng, 6), axis_at), (blocks,), jnp.float32, least / len(cuts), high / len(cuts))
        loudness = loudness * jnp.repeat(jnp.exp(draws), shape[axis_at] // blocks).reshape((-1,) + (1,) * (len(shape) - 1 - axis_at))
    return loudness


def picks_of(stream_key, rows, number_of, top, lift):
    order = jax.random.permutation(jax.random.fold_in(stream_key, 1), number_of)
    pull = order
    for power in range(3):
        pull = pull * pull // number_of
    pull = pull * lift // number_of
    chance = jax.random.randint(jax.random.fold_in(stream_key, 2), (rows, number_of), 0, 4096) + pull
    sure = jax.random.permutation(jax.random.fold_in(stream_key, 3), rows)[jnp.arange(number_of) % rows]
    chance = jnp.where(jnp.arange(rows)[:, None] == sure[None, :], 1 << 14, chance)
    merit = chance * number_of + jnp.arange(number_of)
    return lax.top_k(merit.astype(jnp.int32), top)[1].astype(jnp.int32)


def noise(key, dims, deviation, most, cuts=(), held_as=jnp.bfloat16):
    level = block_scale(key, dims, cuts, -0.22, 0.18) if cuts else 1.0
    array = jax.random.normal(key, dims, jnp.float32) * deviation * level
    return jnp.minimum(jnp.maximum(array, -most), most).astype(held_as)


def setup_inputs(seed: int = 0) -> dict:
    key_of = jax.random.split(jax.random.key(seed), 17)
    tokens = noise(key_of[0], (SEQS, LEN, D), 1.0, 6.0, ((0, 4), (1, 8)))
    cotangent = noise(key_of[1], (SEQS, LEN, D), 1.0, 6.0, ((0, 4), (1, 8)))
    segments = draw_segments(jax.random.fold_in(key_of[16], 71), 0)
    expert_ids = picks_of(key_of[3], SEQS * LEN, EXPERTS, TOPK, 4096).reshape((SEQS, LEN, TOPK))
    slot_order = jax.vmap(lambda own: jax.random.permutation(own, TOK_DEV * TOPK))(jax.random.split(key_of[4], SEQS * SPANS)).reshape((SEQS, SPANS, TOK_DEV * TOPK)).astype(jnp.int32)
    gate_weights = jnp.clip(0.1 + 0.3 * jax.random.uniform(key_of[5], (SEQS, LEN, TOPK), jnp.float32) ** block_scale(key_of[5], (SEQS, LEN, TOPK), ((0, 4), (1, 8)), -0.2, 0.2), 0.1, 0.4)
    qkv_weight = noise(key_of[6], (D, 3 * D), D ** -0.5, 0.125, ((0, 32),))
    qkv_bias = noise(key_of[7], (3 * D,), 0.3, 4.0, ((0, 32),))
    out_weight = noise(key_of[8], (D, D), (max(1, D // 256)) ** -0.5, 2.0, ((0, 32),))
    norm_attn = jnp.clip(1.0 + 0.1 * jax.random.normal(key_of[9], (D,), jnp.float32), 0.5, 1.5).astype(jnp.bfloat16)
    norm_ffn = jnp.clip(1.0 + 0.1 * jax.random.normal(key_of[10], (D,), jnp.float32), 0.5, 1.5).astype(jnp.bfloat16)
    shared_gate_up = noise(key_of[11], (2, D, FFS), D ** -0.5, 0.125, ((1, 8), (2, 4)))
    shared_down = noise(key_of[12], (FFS, D), (FFS // 4) ** -0.5, 0.15625, ((0, 4), (1, 8)))
    shared_gate = noise(key_of[13], (D,), D ** -0.5, 0.125, ((0, 32),))
    expert_gate_up = noise(key_of[14], (EXPERTS, D, 2 * FF), D ** -0.5, 0.125, ((0, 4), (1, 8)))
    expert_down = noise(key_of[15], (EXPERTS, FF, D), (FF // 4) ** -0.5, 0.3125, ((0, 4), (1, 8)))
    return {"tokens": tokens, "cotangent": cotangent, "segments": segments, "expert_ids": expert_ids, "slot_order": slot_order, "gate_weights": gate_weights, "qkv_weight": qkv_weight, "qkv_bias": qkv_bias, "out_weight": out_weight, "norm_attn": norm_attn, "norm_ffn": norm_ffn, "shared_gate_up": shared_gate_up, "shared_down": shared_down, "shared_gate": shared_gate, "expert_gate_up": expert_gate_up, "expert_down": expert_down}


eps_norm = 1e-06
neg_fill = -1e+30
rope_base = 1000000.0
highest_precision = lax.Precision.HIGHEST

@jax.custom_vjp
def low(v):
    return lax.optimization_barrier(v.astype(jnp.bfloat16)).astype(jnp.float32)

@jax.custom_vjp
def lower_backward(v):
    return v

def low_keep(v):
    return (low(v), None)

def low_pass(kept, grad):
    return (grad,)

def back_keep(v):
    return (v, None)

def back_low(kept, grad):
    return (low(grad),)
low.defvjp(low_keep, low_pass)
lower_backward.defvjp(back_keep, back_low)

def rope_tables(positions, half):
    inverse = jnp.exp(jnp.arange(half).astype(jnp.float32) * (-2.0 * math.log(rope_base) / (2 * half)))
    angle = positions.astype(jnp.float32)[:, None] * inverse[None, :]
    return (jnp.cos(angle), jnp.sin(angle))

def rotate(values, cosine, sine):
    half = values.shape[-1] // 2
    front = values[..., :half]
    behind = values[..., half:]
    cosine = cosine[:, None, :]
    sine = sine[:, None, :]
    return jnp.concatenate([front * cosine - behind * sine, behind * cosine + front * sine], axis=-1)

def normalize(values, gain):
    return values * lax.rsqrt(lax.optimization_barrier(jnp.mean(values * values, axis=-1, keepdims=True)) + eps_norm) * gain

def query_block(total, unit):
    size = unit
    while size * 2 <= max(512, unit) and total % (size * 2) == 0:
        size = size * 2
    return size

def route(expert_row, order_row, experts, capacity):
    count = expert_row.shape[0]
    same_expert = expert_row[:, None] == expert_row[None, :]
    earlier = order_row[None, :] < order_row[:, None]
    rank = lax.optimization_barrier(jnp.sum((same_expert & earlier).astype(jnp.int32), axis=1)).astype(jnp.int32)
    kept_pair = rank < capacity
    slot = jnp.where(kept_pair, expert_row * capacity + rank, experts * capacity).astype(jnp.int32)
    source = jnp.full((experts * capacity + 1,), count, jnp.int32).at[slot].set(jnp.arange(count, dtype=jnp.int32))
    source = source[:experts * capacity]
    return (kept_pair, slot, source, source < count)

def reference(tokens, cotangent, segments, expert_ids, slot_order, gate_weights, qkv_weight, qkv_bias, out_weight, norm_attn, norm_ffn, shared_gate_up, shared_down, shared_gate, expert_gate_up, expert_down):
    floats = jnp.float32
    blocks = SEQS * SPANS
    pairs = TOK_DEV * TOPK
    kept_pair, slot, source, filled = jax.vmap(lambda row, order: route(row, order, EXPERTS, CAP))(expert_ids.reshape(blocks, pairs), slot_order.reshape(blocks, pairs))
    slot_token = (jnp.minimum(source, pairs - 1) // TOPK).astype(jnp.int32)
    pair_gate = gate_weights.reshape(blocks, pairs).astype(floats) * kept_pair.astype(floats)
    filled_mask = filled.astype(floats)[..., None]
    cosine, sine = rope_tables(jnp.arange(LEN), HEAD_DIM // 2)
    places = jnp.arange(LEN, dtype=jnp.int32)
    scale = 1.0 / math.sqrt(HEAD_DIM)
    qblock = query_block(LEN, TOK_DEV)
    qcount = LEN // qblock

    def attend(pieces):
        query, key, value, seq_ids = pieces

        def one_block(parts):
            q_part, q_places, q_ids = parts
            visible = (places[None, :] <= q_places[:, None]) & (seq_ids[None, :] == q_ids[:, None])
            scores = jnp.einsum('qhd,khd->hqk', q_part, key, precision=highest_precision)
            scores = lower_backward(scores)
            scores = jnp.where(visible[None], scores, neg_fill)
            probs = low(jax.nn.softmax(scores, axis=-1))
            return jnp.einsum('hqk,khd->qhd', probs, value, precision=highest_precision)
        mixed = lax.map(jax.checkpoint(one_block), (query.reshape(qcount, qblock, HEADS, HEAD_DIM), places.reshape(qcount, qblock), seq_ids.reshape(qcount, qblock)))
        return mixed.reshape(LEN, D)

    def forward(residual_input, query_key_value_weight, query_key_value_bias, output_weight, gain_attn, gain_ffn, shared_up_weight, shared_down_weight, shared_gate_weight, w_expert_up, w_expert_down):
        attention_normed_input = low(normalize(residual_input, gain_attn))
        projected_output = lower_backward(jnp.einsum('wxi,im->wxm', attention_normed_input, query_key_value_weight, precision=highest_precision) + query_key_value_bias)
        query = projected_output[..., :D].reshape(SEQS, LEN, HEADS, HEAD_DIM)
        key = projected_output[..., D:2 * D].reshape(SEQS, LEN, HEADS, HEAD_DIM)
        value = projected_output[..., 2 * D:].reshape(SEQS, LEN, HEADS, HEAD_DIM)
        query = low(rotate(query, cosine, sine) * scale)
        key = low(rotate(key, cosine, sine))
        value = low(value)
        attention_result = lax.map(attend, (query, key, value, segments))
        attention_result = lower_backward(low(attention_result))
        residual_middle = residual_input + lower_backward(jnp.einsum('wxi,im->wxm', attention_result, output_weight, precision=highest_precision))
        feedforward_normed_input = low(normalize(residual_middle, gain_ffn))
        shared_gate_values = lower_backward(jnp.einsum('bzn,nq->bzq', feedforward_normed_input, shared_up_weight[0], precision=highest_precision))
        shared_up_values = lower_backward(jnp.einsum('bzn,nq->bzq', feedforward_normed_input, shared_up_weight[1], precision=highest_precision))
        shared_hidden_state = low(jax.nn.silu(shared_gate_values) * shared_up_values)
        shared_output = lower_backward(jnp.einsum('aqb,br->aqr', shared_hidden_state, shared_down_weight, precision=highest_precision))
        shared_gate_matrix = jax.nn.sigmoid(jnp.einsum('fba,a->fb', feedforward_normed_input, shared_gate_weight, precision=highest_precision))[..., None]
        flat = feedforward_normed_input.reshape(blocks, TOK_DEV, D)
        slot_in = jnp.take_along_axis(flat, slot_token[..., None], axis=1) * filled_mask
        slot_in = lower_backward(slot_in).reshape(blocks, EXPERTS, CAP, D)
        expert_pre = lower_backward(jnp.einsum('becd,edf->becf', slot_in, w_expert_up, precision=highest_precision))
        expert_hidden = low(jax.nn.silu(expert_pre[..., :FF]) * expert_pre[..., FF:])
        expert_out = lower_backward(low(jnp.einsum('becf,efd->becd', expert_hidden, w_expert_down, precision=highest_precision)))
        expert_out = expert_out.reshape(blocks, EXPERTS * CAP, D)
        expert_out = jnp.concatenate([expert_out, jnp.zeros((blocks, 1, D), floats)], axis=1)
        picked = jnp.take_along_axis(expert_out, slot[..., None], axis=1)
        routed = (picked * pair_gate[..., None]).reshape(blocks, TOK_DEV, TOPK, D).sum(axis=2).reshape(SEQS, LEN, D)
        return residual_middle + shared_gate_matrix * shared_output + routed
    primals = (tokens.astype(floats), qkv_weight.astype(floats), qkv_bias.astype(floats), out_weight.astype(floats), norm_attn.astype(floats), norm_ffn.astype(floats), shared_gate_up.astype(floats), shared_down.astype(floats), shared_gate.astype(floats), expert_gate_up.astype(floats), expert_down.astype(floats))
    layer_sum, pullback = jax.vjp(forward, *primals)
    grads = pullback(cotangent.astype(floats))
    return (layer_sum.astype(jnp.bfloat16), grads[0], grads[1], grads[2], grads[3], grads[4], grads[5], grads[6], grads[7], grads[8], grads[9], grads[10])
```

```python
import math

import jax
import jax.numpy as jnp
from jax import lax
from jax.sharding import PartitionSpec as P

HEADS = 16
HEAD_DIM = 128


eps_norm = 1e-06
neg_fill = -1e30
rope_base = 1000000.0
group_heads = 4
floats = jnp.float32
halves = jnp.bfloat16
every = ("expert", "context", "dp")
group = ("expert", "context")


def rope_tables(positions, half):
    inverse = jnp.exp(
        jnp.arange(half).astype(jnp.float32) * (-2.0 * math.log(rope_base) / (2 * half))
    )
    angle = positions.astype(jnp.float32)[:, None] * inverse[None, :]
    return (jnp.cos(angle), jnp.sin(angle))


def rotate(values, cosine, sine):
    half = values.shape[-1] // 2
    front = values[..., :half]
    behind = values[..., half:]
    cosine = cosine[:, None, :]
    sine = sine[:, None, :]
    return jnp.concatenate(
        [front * cosine - behind * sine, behind * cosine + front * sine], axis=-1
    )


def rotate_back(grads, cosine, sine):
    half = grads.shape[-1] // 2
    front = grads[..., :half]
    behind = grads[..., half:]
    cosine = cosine[:, None, :]
    sine = sine[:, None, :]
    return jnp.concatenate(
        [front * cosine + behind * sine, behind * cosine - front * sine], axis=-1
    )


def silu_parts(grad_hidden, gate_pre, up_pre):
    sigma = jax.nn.sigmoid(gate_pre)
    gate_grad = grad_hidden * up_pre * sigma * (1.0 + gate_pre * (1.0 - sigma))
    up_grad = grad_hidden * gate_pre * sigma
    return (gate_grad, up_grad)


def dot(left, right):
    return jnp.dot(left, right, preferred_element_type=floats)


def dot_tn(left, right):
    return lax.dot_general(left, right, (((0,), (0,)), ((), ())), preferred_element_type=floats)


def dot_nt(left, right):
    return lax.dot_general(left, right, (((1,), (1,)), ((), ())), preferred_element_type=floats)


def dp_step(value, step):
    count = lax.axis_size("dp")
    return lax.ppermute(value, "dp", [(i, i ^ step) for i in range(count)])


def other_core(value):
    return lax.ppermute(value, "context", [(0, 1), (1, 0)])


def gather_square(first, second):
    first_x, first_y = dp_step(first, 1), dp_step(first, 2)
    second_y, second_x = dp_step(second, 2), dp_step(second, 1)
    first_far, second_far = dp_step(first_x, 2), dp_step(second_y, 1)
    return [first, first_x, first_y, first_far], [second, second_x, second_y, second_far]


def reduce_square(first, second):
    first_far, first_near = dp_step(first[3], 1), dp_step(first[1], 1)
    second_far, second_near = dp_step(second[3], 2), dp_step(second[2], 2)
    first_pass = (first[2].astype(floats) + first_far.astype(floats)).astype(halves)
    second_pass = (second[1].astype(floats) + second_far.astype(floats)).astype(halves)
    first_last, second_last = dp_step(first_pass, 2), dp_step(second_pass, 1)
    first_sum = first[0].astype(floats) + first_near.astype(floats) + first_last.astype(floats)
    second_sum = second[0].astype(floats) + second_near.astype(floats) + second_last.astype(floats)
    return first_sum, second_sum


def gather_weight(kept, given):
    core = lax.axis_index("context")
    place = lax.axis_index("dp")
    taken = other_core(given)
    near, far = gather_square(kept, taken)
    out = jnp.zeros((2, 4) + kept.shape, kept.dtype)
    zeros = (0,) * kept.ndim
    for step in range(4):
        out = lax.dynamic_update_slice(out, near[step][None, None], (core, place ^ step) + zeros)
        out = lax.dynamic_update_slice(out, far[step][None, None], (1 - core, place ^ step) + zeros)
    return out


def line_gather(block):
    count = lax.axis_size("expert")
    if count != 4:
        return lax.all_gather(block, "expert", axis=0)
    here = lax.axis_index("expert")
    lower = lax.ppermute(block, "expert", [(0, 1), (1, 2), (2, 3)])
    upper = lax.ppermute(block, "expert", [(1, 0), (2, 1), (3, 2)])
    second = lax.ppermute(block, "expert", [(0, 2), (1, 3), (2, 0), (3, 1)])
    third = lax.ppermute(second, "expert", [(2, 3), (1, 0)])
    table = (
        (block, upper, second, third),
        (lower, block, upper, second),
        (second, lower, block, upper),
        (third, second, lower, block),
    )
    rows = []
    for slot in range(4):
        pick = table[3][slot]
        for at in (2, 1, 0):
            pick = jnp.where(here == at, table[at][slot], pick)
        rows.append(pick)
    return jnp.stack(rows)


def group_gather(block):
    if lax.axis_size("expert") != 4:
        return lax.all_gather(block, group, axis=0, tiled=True)
    core = lax.axis_index("context")
    mine = line_gather(block)
    other = other_core(mine)
    both = jnp.stack([jnp.where(core == 0, mine, other), jnp.where(core == 0, other, mine)], axis=1)
    return both.reshape((-1,) + block.shape[1:])


def group_reduce(part):
    count = lax.axis_size("expert")
    if count != 4:
        return lax.psum_scatter(part, group, scatter_dimension=0, tiled=True)
    core = lax.axis_index("context")
    here = lax.axis_index("expert")
    width = part.shape[1]
    view = part.reshape(count, 2, -1, width)
    mine = lax.dynamic_index_in_dim(view, core, 1, keepdims=False)
    other = lax.dynamic_index_in_dim(view, 1 - core, 1, keepdims=False).astype(halves)
    rows = (mine + other_core(other).astype(floats)).astype(halves)

    def of(place):
        return lax.dynamic_index_in_dim(rows, jnp.clip(place, 0, 3), 0, keepdims=False)

    corner = lax.ppermute(of(jnp.where(here == 3, 0, 3)), "expert", [(3, 2), (0, 1)])
    lower = lax.ppermute(of(here + 1), "expert", [(0, 1), (1, 2), (2, 3)])
    upper = lax.ppermute(of(here - 1), "expert", [(1, 0), (2, 1), (3, 2)])
    passed = (of(here ^ 2).astype(floats) + corner.astype(floats)).astype(halves)
    second = lax.ppermute(passed, "expert", [(0, 2), (1, 3), (2, 0), (3, 1)])
    return (
        of(here).astype(floats)
        + lower.astype(floats)
        + upper.astype(floats)
        + second.astype(floats)
    )


def spread(values):
    count = lax.axis_size(every)
    padded = jnp.broadcast_to(values.reshape(1, -1, 128), (count, values.shape[0] // 128, 128))
    got = lax.all_to_all(padded, every, split_axis=0, concat_axis=0, tiled=True)
    return got.reshape(count, -1)


def head_weights(qkv_weight, out_weight):
    count = lax.axis_size(group)
    place = lax.axis_index("dp")
    rows, wide = qkv_weight.shape
    width = wide // 3
    piece = width // count
    cut = qkv_weight.reshape(rows, 3, count, piece).transpose(2, 0, 1, 3).reshape(count, rows, 3 * piece)
    cut = lax.all_to_all(cut, group, split_axis=0, concat_axis=0, tiled=True)
    half = count // 2
    first, second = gather_square(cut[:half], cut[half:])
    weight = jnp.zeros((count, 4, rows, 3 * piece), halves)
    half_rows = rows // 2
    first_out, second_out = gather_square(out_weight[:half_rows], out_weight[half_rows:])
    out = jnp.zeros((4, 2, half_rows, width), halves)
    for step in range(4):
        at = place ^ step
        weight = lax.dynamic_update_slice(weight, first[step][:, None], (0, at, 0, 0))
        weight = lax.dynamic_update_slice(weight, second[step][:, None], (half, at, 0, 0))
        out = lax.dynamic_update_slice(out, first_out[step][None, None], (at, 0, 0, 0))
        out = lax.dynamic_update_slice(out, second_out[step][None, None], (at, 1, 0, 0))
    return weight.reshape(width, 3 * piece), out.reshape(piece, width)


def heads_forward(all_tokens, gain, bias, weights, seq_ids):
    weight, out_rows = weights
    count = lax.axis_size(group)
    index = lax.axis_index(group)
    length, width = all_tokens.shape
    piece = width // count
    heads = piece // HEAD_DIM
    scale = 1.0 / math.sqrt(HEAD_DIM)
    tokens = all_tokens.astype(floats)
    stat = lax.rsqrt(jnp.mean(tokens * tokens, axis=-1, keepdims=True) + eps_norm)
    unit = tokens * stat
    normed = (unit * gain).astype(halves)
    own_bias = lax.dynamic_index_in_dim(bias.reshape(3, count, piece), index, 1, keepdims=False)
    projected = dot(normed, weight) + own_bias.reshape(1, 3 * piece)
    positions = jnp.arange(length, dtype=jnp.int32)
    cosine, sine = rope_tables(positions, HEAD_DIM // 2)
    raw = projected.reshape(length, 3, heads, HEAD_DIM)
    query = (rotate(raw[:, 0], cosine, sine) * scale).astype(halves)
    key = rotate(raw[:, 1], cosine, sine).astype(halves)
    value = raw[:, 2].astype(halves)
    visible = (positions[None, :] <= positions[:, None]) & (seq_ids[None, :] == seq_ids[:, None])
    scores = jnp.einsum("qhd,khd->hqk", query, key, preferred_element_type=floats)
    scores = jnp.where(visible[None], scores, neg_fill)
    top = jnp.max(scores, axis=-1, keepdims=True)
    grown = jnp.exp(scores - top)
    probs = grown / jnp.sum(grown, axis=-1, keepdims=True)
    attended = jnp.einsum("hqk,khd->qhd", probs.astype(halves), value, preferred_element_type=floats)
    attended = attended.reshape(length, piece).astype(halves)
    mixed = group_reduce(dot(attended, out_rows))
    return mixed, (normed, query, key, value, probs, attended, cosine, sine)


def heads_backward(all_tokens, gain, weights, saved, mid_low):
    weight, out_rows = weights
    normed, query, key, value, probs, attended, cosine, sine = saved
    count = lax.axis_size(group)
    index = lax.axis_index(group)
    place = lax.axis_index("dp")
    length, width = all_tokens.shape
    piece = width // count
    heads = piece // HEAD_DIM
    scale = 1.0 / math.sqrt(HEAD_DIM)
    all_mid = group_gather(mid_low)
    attended_grad = dot_nt(all_mid, out_rows).astype(halves).reshape(length, heads, HEAD_DIM)
    prob_grad = jnp.einsum("qhd,khd->hqk", attended_grad, value, preferred_element_type=floats)
    delta = jnp.sum(probs * prob_grad, axis=-1, keepdims=True)
    score_grad = (probs * (prob_grad - delta)).astype(halves)
    query_grad = jnp.einsum("hqk,khd->qhd", score_grad, key, preferred_element_type=floats)
    key_grad = jnp.einsum("hqk,qhd->khd", score_grad, query, preferred_element_type=floats)
    value_grad = jnp.einsum(
        "hqk,qhd->khd", probs.astype(halves), attended_grad, preferred_element_type=floats
    )
    proj_grad = jnp.concatenate(
        [
            rotate_back(query_grad * scale, cosine, sine).reshape(length, piece),
            rotate_back(key_grad, cosine, sine).reshape(length, piece),
            value_grad.reshape(length, piece),
        ],
        axis=-1,
    ).astype(halves)
    weight_part = dot_tn(normed, proj_grad).astype(halves)
    in_part = dot_nt(proj_grad, weight)
    tokens = all_tokens.astype(floats)
    stat = lax.rsqrt(jnp.mean(tokens * tokens, axis=-1, keepdims=True) + eps_norm)
    gain_part = jnp.sum(in_part * (tokens * stat), axis=0)
    bias_part = lax.dynamic_update_slice(
        jnp.zeros((3, count, piece), floats),
        jnp.sum(proj_grad.astype(floats), axis=0).reshape(3, 1, piece),
        (0, index, 0),
    ).reshape(-1)
    attn_in_grad = group_reduce(in_part)
    rows = width // (count * 4)
    half = count // 2
    cut = weight_part.reshape(count, 4, rows, 3 * piece)
    picks = [lax.dynamic_index_in_dim(cut, place ^ step, 1, keepdims=False) for step in range(4)]
    first, second = reduce_square([pick[:half] for pick in picks], [pick[half:] for pick in picks])
    total = jnp.concatenate([first, second]).astype(halves)
    total = lax.all_to_all(total, group, split_axis=0, concat_axis=0, tiled=True)
    qkv_out = (
        total.reshape(count, rows, 3, piece).transpose(1, 2, 0, 3).reshape(rows, 3 * width).astype(floats)
    )
    out_part = dot_tn(attended, all_mid).astype(halves).reshape(4, rows, width)
    picks = [lax.dynamic_index_in_dim(out_part, place ^ step, 0, keepdims=False) for step in range(4)]
    first, second = reduce_square(
        [pick[: rows // 2] for pick in picks], [pick[rows // 2 :] for pick in picks]
    )
    return attn_in_grad, gain_part, bias_part, qkv_out, jnp.concatenate([first, second])


def rows_weights(qkv_weight, out_weight):
    return (
        lax.all_gather(qkv_weight, every, axis=0, tiled=True),
        lax.all_gather(out_weight, every, axis=0, tiled=True),
    )


def rows_forward(own_tokens, gain, bias, weights, seq_ids):
    weight, out_weight = weights
    tok_count, width = own_tokens.shape
    seq_len = seq_ids.shape[0]
    head_groups = HEADS // group_heads
    block_place = lax.axis_index(group)
    positions = block_place * tok_count + jnp.arange(tok_count, dtype=jnp.int32)
    cosine, sine = rope_tables(positions, HEAD_DIM // 2)
    scale = 1.0 / math.sqrt(HEAD_DIM)
    tokens = own_tokens.astype(floats)
    stat = lax.rsqrt(jnp.mean(tokens * tokens, axis=-1, keepdims=True) + eps_norm)
    unit = tokens * stat
    normed = (unit * gain).astype(halves)
    projected = dot(normed, weight) + bias
    raw = projected.reshape(tok_count, 3, HEADS, HEAD_DIM)
    query = (rotate(raw[:, 0], cosine, sine) * scale).astype(halves)
    key = rotate(raw[:, 1], cosine, sine).astype(halves)
    value = raw[:, 2].astype(halves)

    def by_group(array):
        return array.reshape(tok_count, head_groups, group_heads, HEAD_DIM).transpose(1, 0, 2, 3)

    query_groups = by_group(query)
    key_all = lax.all_gather(by_group(key), group, axis=1, tiled=True)
    value_all = lax.all_gather(by_group(value), group, axis=1, tiled=True)
    query_ids = lax.dynamic_slice_in_dim(seq_ids, block_place * tok_count, tok_count)
    key_places = jnp.arange(seq_len, dtype=jnp.int32)
    visible = (key_places[None, :] <= positions[:, None]) & (seq_ids[None, :] == query_ids[:, None])

    def attend_group(pieces):
        q_part, k_part, v_part = pieces
        scores = jnp.einsum("qhd,khd->hqk", q_part, k_part, preferred_element_type=floats)
        scores = jnp.where(visible[None], scores, neg_fill)
        top_score = jnp.max(scores, axis=-1, keepdims=True)
        grown = jnp.exp(scores - top_score)
        total = jnp.sum(grown, axis=-1, keepdims=True)
        probs_low = (grown / total).astype(halves)
        mixed = jnp.einsum("hqk,khd->qhd", probs_low, v_part, preferred_element_type=floats)
        return (mixed, top_score + jnp.log(total))

    mixed_groups, log_totals = lax.map(attend_group, (query_groups, key_all, value_all))
    attended = mixed_groups.transpose(1, 0, 2, 3).reshape(tok_count, width).astype(halves)
    saved = (normed, unit, query_groups, key_all, value_all, log_totals, attended, cosine, sine, visible)
    return dot(attended, out_weight), saved


def rows_backward(weights, saved, mid_low):
    weight, out_weight = weights
    normed, unit, query_groups, key_all, value_all, log_totals, attended, cosine, sine, visible = saved
    tok_count, width = mid_low.shape
    head_groups = HEADS // group_heads
    scale = 1.0 / math.sqrt(HEAD_DIM)
    attended_grad = dot_nt(mid_low, out_weight).astype(halves)
    grad_groups = attended_grad.reshape(tok_count, head_groups, group_heads, HEAD_DIM).transpose(
        1, 0, 2, 3
    )

    def attend_back(pieces):
        q_part, k_part, v_part, g_part, log_part = pieces
        scores = jnp.einsum("qhd,khd->hqk", q_part, k_part, preferred_element_type=floats)
        scores = jnp.where(visible[None], scores, neg_fill)
        probs = jnp.exp(scores - log_part)
        prob_grad = jnp.einsum("qhd,khd->hqk", g_part, v_part, preferred_element_type=floats)
        delta = jnp.sum(probs * prob_grad, axis=-1, keepdims=True)
        score_grad = (probs * (prob_grad - delta)).astype(halves)
        q_grad = jnp.einsum("hqk,khd->qhd", score_grad, k_part, preferred_element_type=floats)
        k_grad = jnp.einsum("hqk,qhd->khd", score_grad, q_part, preferred_element_type=floats)
        v_grad = jnp.einsum(
            "hqk,qhd->khd", probs.astype(halves), g_part, preferred_element_type=floats
        )
        return (q_grad, k_grad, v_grad)

    query_grads, key_grads, value_grads = lax.map(
        attend_back, (query_groups, key_all, value_all, grad_groups, log_totals)
    )
    key_grad = lax.psum_scatter(key_grads, group, scatter_dimension=1, tiled=True)
    value_grad = lax.psum_scatter(value_grads, group, scatter_dimension=1, tiled=True)

    def by_head(array):
        return array.transpose(1, 0, 2, 3).reshape(tok_count, HEADS, HEAD_DIM)

    proj_grad = jnp.concatenate(
        [
            rotate_back(by_head(query_grads) * scale, cosine, sine).reshape(tok_count, width),
            rotate_back(by_head(key_grad), cosine, sine).reshape(tok_count, width),
            by_head(value_grad).reshape(tok_count, width),
        ],
        axis=-1,
    ).astype(halves)
    bias_part = jnp.sum(proj_grad.astype(floats), axis=0)
    attn_in_grad = dot_nt(proj_grad, weight)
    gain_part = jnp.sum(attn_in_grad * unit, axis=0)
    qkv_out = lax.psum_scatter(dot_tn(normed, proj_grad), every, scatter_dimension=0, tiled=True)
    out_out = lax.psum_scatter(dot_tn(attended, mid_low), every, scatter_dimension=0, tiled=True)
    return attn_in_grad, gain_part, bias_part, qkv_out, out_out


def shards(
    tokens,
    cotangent,
    segments,
    expert_ids,
    slot_order,
    gate_weights,
    qkv_weight,
    qkv_bias,
    out_weight,
    norm_attn,
    norm_ffn,
    shared_gate_up,
    shared_down,
    shared_gate,
    expert_gate_up,
    expert_down,
):
    count = lax.axis_size(group)
    devices = lax.axis_size(every)
    core = lax.axis_index("context")
    place = lax.axis_index("dp")
    index = lax.axis_index(group)
    tok_count, width = tokens.shape[1:]
    topk = expert_ids.shape[2]
    pairs = tok_count * topk
    experts = expert_gate_up.shape[0] * lax.axis_size("expert")
    capacity = (9 * pairs + 8 * experts - 1) // (8 * experts)
    length = count * tok_count
    by_heads = HEADS % count == 0

    vectors = [norm_attn, norm_ffn, shared_gate, qkv_bias]
    lengths = [vector.shape[0] for vector in vectors]
    routing = [expert_ids[0].reshape(pairs), slot_order[0, 0], gate_weights[0].reshape(pairs)]
    payload = jnp.concatenate([v.astype(floats) for v in vectors + routing])
    payload = jnp.pad(payload, (0, -payload.shape[0] % 128))
    small = spread(payload)
    at = 0
    gathered = []
    for size in lengths:
        gathered.append(small[:, at : at + size].reshape(-1))
        at += size
    gain_attn, gain_ffn, gate_vector, bias = gathered
    small_own = lax.dynamic_index_in_dim(
        small.reshape(count, devices // count, -1), place, 1, keepdims=False
    )
    routes = [small_own[:, at + i * pairs : at + (i + 1) * pairs] for i in range(3)]
    pair_expert, pair_order, pair_gate = [r.reshape(count, tok_count, topk) for r in routes]

    own_tokens = tokens[0]
    resid_in = own_tokens.astype(floats)
    if by_heads:
        weights = head_weights(qkv_weight, out_weight)
        all_tokens = group_gather(own_tokens)
        mixed, saved = heads_forward(all_tokens, gain_attn, bias, weights, segments[0])
    else:
        weights = rows_weights(qkv_weight, out_weight)
        mixed, saved = rows_forward(own_tokens, gain_attn, bias, weights, segments[0])

    def core_half(array, axis, which):
        size = array.shape[axis] // 2
        return lax.dynamic_slice_in_dim(array, which * size, size, axis)

    def expert_of(array, which):
        return lax.dynamic_index_in_dim(array, which, 0, keepdims=False)

    def gate_up_half(which):
        part = core_half(shared_gate_up, 2, which)
        return jnp.concatenate([part[0], part[1]], axis=-1)

    expert_up = gather_weight(expert_of(expert_gate_up, core), expert_of(expert_gate_up, 1 - core))
    expert_up = expert_up.reshape(width, -1)
    expert_dn = gather_weight(expert_of(expert_down, core), expert_of(expert_down, 1 - core))
    expert_dn = expert_dn.reshape(-1, width)
    ff_width = expert_dn.shape[0]
    shared_up = gather_weight(gate_up_half(core), gate_up_half(1 - core)).reshape(width, -1)
    down_turned = shared_down.T
    shared_dn = gather_weight(core_half(down_turned, 1, core), core_half(down_turned, 1, 1 - core))
    shared_dn = shared_dn.reshape(width, -1)
    hidden_units = shared_dn.shape[1]

    resid_mid = resid_in + mixed
    stat_ffn = lax.rsqrt(jnp.mean(resid_mid * resid_mid, axis=-1, keepdims=True) + eps_norm)
    unit_ffn = resid_mid * stat_ffn
    normed_ffn = (unit_ffn * gain_ffn).astype(halves)
    grad_out = cotangent[0].astype(floats)

    all_grads = group_gather(cotangent[0])
    all_normed = group_gather(normed_ffn)

    chosen = pair_expert == index.astype(floats)
    has_pair = jnp.any(chosen, axis=-1)
    order = jnp.sum(jnp.where(chosen, pair_order, 0.0), axis=-1)
    gate = jnp.sum(jnp.where(chosen, pair_gate, 0.0), axis=-1)
    earlier = has_pair[:, None, :] & (order[:, None, :] < order[:, :, None])
    rank = jnp.sum(earlier.astype(jnp.int32), axis=-1)
    kept = has_pair & (rank < capacity)
    gate = jnp.where(kept, gate, 0.0)
    slots = jnp.arange(capacity, dtype=jnp.int32)
    select = (rank[:, None, :] == slots[None, :, None]) & kept[:, None, :]
    slot_gate = jnp.sum(jnp.where(select, gate[:, None, :], 0.0), axis=-1).reshape(-1, 1)
    select = select.astype(halves)

    def to_slots(rows):
        got = jnp.einsum(
            "brt,btd->brd",
            select,
            rows.reshape(count, tok_count, width),
            preferred_element_type=floats,
        )
        return got.reshape(count * capacity, width)

    def from_slots(rows):
        got = jnp.einsum(
            "brt,brd->btd",
            select,
            rows.reshape(count, capacity, width),
            preferred_element_type=floats,
        )
        return got.reshape(length, width)

    slot_in = to_slots(all_normed).astype(halves)
    slot_grad = (to_slots(all_grads) * slot_gate).astype(halves)
    expert_pre = dot(slot_in, expert_up)
    expert_g, expert_u = expert_pre[:, :ff_width], expert_pre[:, ff_width:]
    expert_hidden = (jax.nn.silu(expert_g) * expert_u).astype(halves)
    hidden_grad = dot_nt(slot_grad, expert_dn)
    expert_pre_grad = jnp.concatenate(
        silu_parts(hidden_grad, expert_g, expert_u), axis=-1
    ).astype(halves)
    expert_out = dot(expert_hidden, expert_dn).astype(halves)
    slot_in_grad = dot_nt(expert_pre_grad, expert_up).astype(halves)

    shared_pre = dot(all_normed, shared_up)
    shared_g, shared_u = shared_pre[:, :hidden_units], shared_pre[:, hidden_units:]
    shared_hidden = (jax.nn.silu(shared_g) * shared_u).astype(halves)
    gate_shared = jax.nn.sigmoid(
        jnp.sum(all_normed.astype(floats) * gate_vector, axis=-1, keepdims=True)
    )
    shared_grad = (gate_shared * all_grads.astype(floats)).astype(halves)
    hidden_grad = dot(shared_grad, shared_dn)
    shared_pre_grad = jnp.concatenate(
        silu_parts(hidden_grad, shared_g, shared_u), axis=-1
    ).astype(halves)
    shared_part = dot_nt(shared_hidden, shared_dn)
    logit_part = jnp.sum(all_grads.astype(floats) * shared_part, axis=-1)

    ffn_part = dot_nt(shared_pre_grad, shared_up) + from_slots(slot_in_grad)
    out_part = gate_shared * shared_part + gate.reshape(length, 1) * from_slots(expert_out)

    logit_sums = lax.all_to_all(
        logit_part.reshape(count, 1, tok_count), group, split_axis=0, concat_axis=0, tiled=True
    )
    own_gate = jax.nn.sigmoid(
        jnp.sum(normed_ffn.astype(floats) * gate_vector, axis=-1, keepdims=True)
    )
    logit_grad = jnp.sum(logit_sums, axis=0).reshape(tok_count, 1) * own_gate * (1.0 - own_gate)
    ffn_grad = group_reduce(ffn_part) + logit_grad * gate_vector
    unit_grad = ffn_grad * gain_ffn
    gain_ffn_part = jnp.sum(ffn_grad * unit_ffn, axis=0)
    gate_vector_part = jnp.sum(logit_grad * normed_ffn.astype(floats), axis=0)
    mid_grad = grad_out + stat_ffn * (
        unit_grad - unit_ffn * jnp.mean(unit_grad * unit_ffn, axis=-1, keepdims=True)
    )
    mid_low = mid_grad.astype(halves)
    layer_sum = resid_mid + group_reduce(out_part)

    def block_of(array, crel, step):
        size = width // 8
        blk = (core ^ crel) * 4 + (place ^ step)
        return lax.dynamic_slice_in_dim(array, blk * size, size, 1)

    def reduce_blocks(block):
        near, far = reduce_square(
            [block(0, step) for step in range(4)], [block(1, step) for step in range(4)]
        )
        return near, other_core(far)

    def in_order(near, far, axis):
        return (
            jnp.where(core == 0, near, far),
            jnp.where(core == 0, far, near),
        )

    expert_down_term = dot_tn(expert_hidden, slot_grad).astype(halves)
    expert_down_term = expert_down_term.reshape(8, -1, width)
    expert_down_out = jnp.stack(
        in_order(
            *reduce_blocks(
                lambda crel, step: lax.dynamic_index_in_dim(
                    expert_down_term, (core ^ crel) * 4 + (place ^ step), 0, keepdims=False
                )
            ),
            0,
        )
    )
    expert_up_out = jnp.stack(
        in_order(
            *reduce_blocks(
                lambda crel, step: dot_tn(block_of(slot_in, crel, step), expert_pre_grad).astype(halves)
            ),
            0,
        )
    )
    lower, upper = in_order(
        *reduce_blocks(
            lambda crel, step: dot_tn(block_of(all_normed, crel, step), shared_pre_grad).astype(halves)
        ),
        0,
    )
    shared_up_out = jnp.concatenate(
        [array.reshape(width // 8, 2, hidden_units).transpose(1, 0, 2) for array in (lower, upper)],
        axis=-1,
    )
    lower, upper = in_order(
        *reduce_blocks(
            lambda crel, step: dot_tn(block_of(shared_grad, crel, step), shared_hidden).astype(halves)
        ),
        0,
    )
    shared_down_out = jnp.concatenate([lower, upper], axis=-1).T

    if by_heads:
        attn_in_grad, gain_attn_part, bias_part, qkv_out, out_weight_out = heads_backward(
            all_tokens, gain_attn, weights, saved, mid_low
        )
    else:
        attn_in_grad, gain_attn_part, bias_part, qkv_out, out_weight_out = rows_backward(
            weights, saved, mid_low
        )
    stat_attn = lax.rsqrt(jnp.mean(resid_in * resid_in, axis=-1, keepdims=True) + eps_norm)
    unit_attn = resid_in * stat_attn
    unit_grad = attn_in_grad * gain_attn
    input_grad = mid_grad + stat_attn * (
        unit_grad - unit_attn * jnp.mean(unit_grad * unit_attn, axis=-1, keepdims=True)
    )

    parts = [gain_attn_part, gain_ffn_part, gate_vector_part, bias_part]
    packed = jnp.concatenate([part.reshape(devices, -1) for part in parts], axis=1)
    total = packed.shape[1]
    packed = jnp.pad(packed, ((0, 0), (0, -total % 128)))
    packed = lax.all_to_all(
        packed.reshape(devices, -1, 128), every, split_axis=0, concat_axis=0, tiled=True
    )
    sums = jnp.sum(packed, axis=0).reshape(-1)
    at = 0
    small_out = []
    for size in lengths:
        small_out.append(sums[at : at + size])
        at += size
    gain_attn_out, gain_ffn_out, gate_vector_out, bias_out = small_out
    return (
        layer_sum.astype(halves)[None],
        input_grad[None],
        qkv_out,
        bias_out,
        out_weight_out,
        gain_attn_out,
        gain_ffn_out,
        shared_up_out,
        shared_down_out,
        gate_vector_out,
        expert_up_out,
        expert_down_out,
    )


def solution(mesh):
    placed = (
        P("dp", ("expert", "context"), None),
        P("dp", ("expert", "context"), None),
        P("dp", None),
        P("dp", ("expert", "context"), None),
        P("dp", ("expert", "context"), None),
        P("dp", ("expert", "context"), None),
        P(("expert", "context", "dp"), None),
        P(("expert", "context", "dp")),
        P(("expert", "context", "dp"), None),
        P(("expert", "context", "dp")),
        P(("expert", "context", "dp")),
        P(None, ("context", "dp"), "expert"),
        P("expert", ("context", "dp")),
        P(("expert", "context", "dp")),
        P("expert", ("context", "dp"), None),
        P("expert", ("context", "dp"), None),
    )
    return jax.shard_map(
        shards,
        mesh=mesh,
        in_specs=placed,
        out_specs=(
            P("dp", ("expert", "context"), None),
            P("dp", ("expert", "context"), None),
            P(("expert", "context", "dp"), None),
            P(("expert", "context", "dp")),
            P(("expert", "context", "dp"), None),
            P(("expert", "context", "dp")),
            P(("expert", "context", "dp")),
            P(None, ("context", "dp"), "expert"),
            P("expert", ("context", "dp")),
            P(("expert", "context", "dp")),
            P("expert", ("context", "dp"), None),
            P("expert", ("context", "dp"), None),
        ),
        check_vma=False,
    )
```

```python
import math

import jax
import jax.numpy as jnp
from jax import lax
from jax.experimental import pallas as pl
from jax.experimental.pallas import tpu as pltpu
from jax.sharding import PartitionSpec as P

HEADS = 16
HEAD_DIM = 128


eps_norm = 1e-06
neg_fill = -1e30
rope_base = 1000000.0
group_heads = 4
floats = jnp.float32
halves = jnp.bfloat16
every = ("expert", "context", "dp")
group = ("expert", "context")


def rope_tables(positions, half):
    inverse = jnp.exp(
        jnp.arange(half).astype(jnp.float32) * (-2.0 * math.log(rope_base) / (2 * half))
    )
    angle = positions.astype(jnp.float32)[:, None] * inverse[None, :]
    return (jnp.cos(angle), jnp.sin(angle))


def rotate(values, cosine, sine):
    half = values.shape[-1] // 2
    front = values[..., :half]
    behind = values[..., half:]
    cosine = cosine[:, None, :]
    sine = sine[:, None, :]
    return jnp.concatenate(
        [front * cosine - behind * sine, behind * cosine + front * sine], axis=-1
    )


def rotate_back(grads, cosine, sine):
    half = grads.shape[-1] // 2
    front = grads[..., :half]
    behind = grads[..., half:]
    cosine = cosine[:, None, :]
    sine = sine[:, None, :]
    return jnp.concatenate(
        [front * cosine + behind * sine, behind * cosine - front * sine], axis=-1
    )


def silu_parts(grad_hidden, gate_pre, up_pre):
    sigma = jax.nn.sigmoid(gate_pre)
    gate_grad = grad_hidden * up_pre * sigma * (1.0 + gate_pre * (1.0 - sigma))
    up_grad = grad_hidden * gate_pre * sigma
    return (gate_grad, up_grad)


def dot(left, right):
    return jnp.dot(left, right, preferred_element_type=floats)


def dot_tn(left, right):
    return lax.dot_general(left, right, (((0,), (0,)), ((), ())), preferred_element_type=floats)


def dot_nt(left, right):
    return lax.dot_general(left, right, (((1,), (1,)), ((), ())), preferred_element_type=floats)


def dp_step(value, step):
    count = lax.axis_size("dp")
    return lax.ppermute(value, "dp", [(i, i ^ step) for i in range(count)])


def other_core(value):
    return lax.ppermute(value, "context", [(0, 1), (1, 0)])


def after(value, *others):
    return lax.optimization_barrier((value,) + others)[0]


def near_blocks(block):
    return dp_step(block, 1), dp_step(block, 2)


def place_blocks(pieces, places, out_shape, views):
    count = len(pieces)

    def kernel(place_ref, *refs):
        blocks, out, held = refs[:count], refs[count], refs[count + 1 : 2 * count + 1]
        in_sems, out_sems = refs[2 * count + 1 :]
        loads = [
            pltpu.make_async_copy(blocks[i], held[i], in_sems.at[i]) for i in range(count)
        ]
        stores = [
            pltpu.make_async_copy(held[i], views[i](out, place_ref[i]), out_sems.at[i])
            for i in range(count)
        ]
        for load in loads:
            load.start()
        for load, store in zip(loads, stores):
            load.wait()
            store.start()
        for store in stores:
            store.wait()

    return pl.pallas_call(
        kernel,
        out_shape=jax.ShapeDtypeStruct(out_shape, pieces[0].dtype),
        in_specs=[pl.BlockSpec(memory_space=pltpu.SMEM)]
        + [pl.BlockSpec(memory_space=pl.ANY)] * len(pieces),
        out_specs=pl.BlockSpec(memory_space=pl.ANY),
        scratch_shapes=[pltpu.VMEM(piece.shape, piece.dtype) for piece in pieces]
        + [
            pltpu.SemaphoreType.DMA((count,)),
            pltpu.SemaphoreType.DMA((count,)),
        ],
        compiler_params=pltpu.CompilerParams(vmem_limit_bytes=32 * 1024 * 1024),
        cost_estimate=pl.CostEstimate(
            flops=0, bytes_accessed=2 * sum(p.size * 2 for p in pieces), transcendentals=0
        ),
    )(jnp.stack(places).astype(jnp.int32), *pieces)


def sum_weight(part):
    rows, wide = part.shape
    return lax.psum_scatter(
        part.reshape(2, rows // 2, wide), "dp", scatter_dimension=1, tiled=True
    )


def both_cores(kept, given):
    core = lax.axis_index("context")
    taken = other_core(given)
    return jnp.stack([jnp.where(core == 0, kept, taken), jnp.where(core == 0, taken, kept)])


def gather_rows(both):
    out = lax.all_gather(both, "dp", axis=1, tiled=True)
    return out.reshape(-1, both.shape[2])


def cores_in_order(blocks):
    core = lax.axis_index("context")
    mine = jnp.where(core == 0, blocks[0], blocks[1])
    other = other_core(jnp.where(core == 0, blocks[1], blocks[0]))
    return jnp.where(core == 0, mine, other), jnp.where(core == 0, other, mine)


def along_expert(blocks):
    return lax.all_to_all(blocks, "expert", split_axis=0, concat_axis=0, tiled=True)


def gather_line(block):
    return along_expert(jnp.broadcast_to(block[None], (lax.axis_size("expert"),) + block.shape))


def gather_cores(mine):
    core = lax.axis_index("context")
    other = other_core(mine)
    both = jnp.stack([jnp.where(core == 0, mine, other), jnp.where(core == 0, other, mine)], axis=1)
    return both.reshape((-1,) + mine.shape[2:])


def group_gather(block):
    return gather_cores(gather_line(block))


def group_reduce(part):
    count = lax.axis_size("expert")
    core = lax.axis_index("context")
    view = part.reshape(count, 2, -1, part.shape[1])
    mine = lax.dynamic_index_in_dim(view, core, 1, keepdims=False)
    other = lax.dynamic_index_in_dim(view, 1 - core, 1, keepdims=False).astype(halves)
    rows = (mine + other_core(other).astype(floats)).astype(halves)
    return jnp.sum(along_expert(rows).astype(floats), axis=0), rows


def spread(values):
    count = lax.axis_size(every)
    padded = jnp.broadcast_to(values.reshape(1, -1, 128), (count, values.shape[0] // 128, 128))
    got = lax.all_to_all(padded, every, split_axis=0, concat_axis=0, tiled=True)
    return got.reshape(count, -1)


def head_cut(qkv_weight, out_weight, vectors):
    count = lax.axis_size(group)
    rows, wide = qkv_weight.shape
    piece = wide // (3 * count)
    cut = qkv_weight.reshape(rows, 3, count, piece).transpose(2, 0, 1, 3).reshape(count, rows, 3 * piece)
    columns = jnp.concatenate([vector.reshape(-1, rows) for vector in vectors]).T
    columns = jnp.pad(columns, ((0, 0), (0, 128 - columns.shape[1])))
    columns = jnp.broadcast_to(columns[None], (count,) + columns.shape)
    cut = jnp.concatenate([cut, columns], axis=-1)
    cut = lax.all_to_all(cut, group, split_axis=0, concat_axis=0, tiled=True)
    out = out_weight.reshape(rows, count, piece).transpose(1, 0, 2)
    return jnp.concatenate([cut, out], axis=-1)


def head_weights(own, x_block, y_block, pins):
    count, rows, wide = own.shape
    place = lax.axis_index("dp")
    half = count // 2
    far_low = dp_step(after(x_block[:half], *pins), 2)
    far_high = dp_step(after(y_block[half:], *pins), 1)
    pieces = [own, x_block, y_block, far_low, far_high]
    places = [place, place ^ 1, place ^ 2, place ^ 3, place ^ 3]
    whole = lambda out, at: out.at[:, at]
    low = lambda out, at: out.at[pl.ds(0, half), at]
    high = lambda out, at: out.at[pl.ds(half, half), at]
    packed = place_blocks(pieces, places, (count, 4, rows, wide), [whole] * 3 + [low, high])
    piece = (wide - 128) // 4
    weight = packed[..., : 3 * piece].reshape(count * 4 * rows, 3 * piece)
    out = packed[..., 3 * piece + 128 :].transpose(1, 2, 0, 3).reshape(4 * rows, count * piece)
    columns = packed[..., 3 * piece : 3 * piece + 6].astype(floats)
    vectors = [columns[..., at].reshape(-1) for at in range(3)]
    vectors.append(columns[..., 3:].transpose(0, 1, 3, 2).reshape(-1))
    return (weight, out), vectors, (far_low, far_high)


def heads_forward(all_tokens, gain, bias, weights, seq_ids, pin):
    weight, out_rows = weights
    count = lax.axis_size(group)
    index = lax.axis_index(group)
    length, width = all_tokens.shape
    piece = width // count
    heads = piece // HEAD_DIM
    scale = 1.0 / math.sqrt(HEAD_DIM)
    tokens = all_tokens.astype(floats)
    stat = lax.rsqrt(jnp.mean(tokens * tokens, axis=-1, keepdims=True) + eps_norm)
    unit = tokens * stat
    normed = (unit * gain).astype(halves)
    own_bias = lax.dynamic_index_in_dim(bias.reshape(3, count, piece), index, 1, keepdims=False)
    projected = dot(normed, weight) + own_bias.reshape(1, 3 * piece)
    positions = jnp.arange(length, dtype=jnp.int32)
    cosine, sine = rope_tables(positions, HEAD_DIM // 2)
    raw = projected.reshape(length, 3, heads, HEAD_DIM)
    query = (rotate(raw[:, 0], cosine, sine) * scale).astype(halves)
    key = rotate(raw[:, 1], cosine, sine).astype(halves)
    value = raw[:, 2].astype(halves)
    visible = (positions[None, :] <= positions[:, None]) & (seq_ids[None, :] == seq_ids[:, None])
    scores = jnp.einsum("qhd,khd->hqk", query, key, preferred_element_type=floats)
    scores = jnp.where(visible[None], scores, neg_fill)
    top = jnp.max(scores, axis=-1, keepdims=True)
    grown = jnp.exp(scores - top)
    probs = grown / jnp.sum(grown, axis=-1, keepdims=True)
    attended = jnp.einsum("hqk,khd->qhd", probs.astype(halves), value, preferred_element_type=floats)
    attended = attended.reshape(length, piece).astype(halves)
    mixed, rows = group_reduce(after(dot(attended, out_rows), *pin))
    return mixed, (normed, query, key, value, probs, attended, cosine, sine), (attended, rows)


def heads_backward(all_tokens, gain, weights, saved, mid_low, pins):
    weight, out_rows = weights
    normed, query, key, value, probs, attended, cosine, sine = saved
    count = lax.axis_size(group)
    index = lax.axis_index(group)
    place = lax.axis_index("dp")
    length, width = all_tokens.shape
    piece = width // count
    heads = piece // HEAD_DIM
    scale = 1.0 / math.sqrt(HEAD_DIM)
    all_mid = gather_cores(after(gather_line(mid_low), pins[0]))
    attended_grad = dot_nt(all_mid, out_rows).astype(halves).reshape(length, heads, HEAD_DIM)
    prob_grad = jnp.einsum("qhd,khd->hqk", attended_grad, value, preferred_element_type=floats)
    delta = jnp.sum(probs * prob_grad, axis=-1, keepdims=True)
    score_grad = (probs * (prob_grad - delta)).astype(halves)
    query_grad = jnp.einsum("hqk,khd->qhd", score_grad, key, preferred_element_type=floats)
    key_grad = jnp.einsum("hqk,qhd->khd", score_grad, query, preferred_element_type=floats)
    value_grad = jnp.einsum(
        "hqk,qhd->khd", probs.astype(halves), attended_grad, preferred_element_type=floats
    )
    proj_grad = jnp.concatenate(
        [
            rotate_back(query_grad * scale, cosine, sine).reshape(length, piece),
            rotate_back(key_grad, cosine, sine).reshape(length, piece),
            value_grad.reshape(length, piece),
        ],
        axis=-1,
    ).astype(halves)
    weight_part = dot_tn(normed, proj_grad).astype(halves)
    in_part = dot_nt(after(proj_grad, pins[1], pins[2]), weight)
    layer_sum, _ = group_reduce(after(pins[3], all_mid))
    tokens = all_tokens.astype(floats)
    stat = lax.rsqrt(jnp.mean(tokens * tokens, axis=-1, keepdims=True) + eps_norm)
    gain_part = jnp.sum(in_part * (tokens * stat), axis=0)
    bias_part = lax.dynamic_update_slice(
        jnp.zeros((3, count, piece), floats),
        jnp.sum(proj_grad.astype(floats), axis=0).reshape(3, 1, piece),
        (0, index, 0),
    ).reshape(-1)
    attn_in_grad, rows_low = group_reduce(after(in_part, layer_sum))
    rows = width // (count * 4)
    cut = weight_part.reshape(count, 4, rows, 3 * piece).transpose(1, 0, 2, 3)
    total = lax.psum_scatter(
        cut.reshape(width, 3 * piece), "dp", scatter_dimension=0, tiled=True
    ).reshape(count, rows, 3 * piece)
    total = lax.all_to_all(total, group, split_axis=0, concat_axis=0, tiled=True)
    qkv_out = (
        total.reshape(count, rows, 3, piece).transpose(1, 2, 0, 3).reshape(rows, 3 * width).astype(floats)
    )
    out_part = dot_tn(attended, all_mid).astype(halves)
    out_out = lax.psum_scatter(out_part, "dp", scatter_dimension=0, tiled=True).astype(floats)
    return attn_in_grad, gain_part, bias_part, qkv_out, out_out, layer_sum, (all_mid, rows_low)


def rows_weights(qkv_weight, out_weight):
    return (
        lax.all_gather(qkv_weight, every, axis=0, tiled=True),
        lax.all_gather(out_weight, every, axis=0, tiled=True),
    )


def rows_forward(own_tokens, gain, bias, weights, seq_ids):
    weight, out_weight = weights
    tok_count, width = own_tokens.shape
    seq_len = seq_ids.shape[0]
    head_groups = HEADS // group_heads
    block_place = lax.axis_index(group)
    positions = block_place * tok_count + jnp.arange(tok_count, dtype=jnp.int32)
    cosine, sine = rope_tables(positions, HEAD_DIM // 2)
    scale = 1.0 / math.sqrt(HEAD_DIM)
    tokens = own_tokens.astype(floats)
    stat = lax.rsqrt(jnp.mean(tokens * tokens, axis=-1, keepdims=True) + eps_norm)
    unit = tokens * stat
    normed = (unit * gain).astype(halves)
    projected = dot(normed, weight) + bias
    raw = projected.reshape(tok_count, 3, HEADS, HEAD_DIM)
    query = (rotate(raw[:, 0], cosine, sine) * scale).astype(halves)
    key = rotate(raw[:, 1], cosine, sine).astype(halves)
    value = raw[:, 2].astype(halves)

    def by_group(array):
        return array.reshape(tok_count, head_groups, group_heads, HEAD_DIM).transpose(1, 0, 2, 3)

    query_groups = by_group(query)
    key_all = lax.all_gather(by_group(key), group, axis=1, tiled=True)
    value_all = lax.all_gather(by_group(value), group, axis=1, tiled=True)
    query_ids = lax.dynamic_slice_in_dim(seq_ids, block_place * tok_count, tok_count)
    key_places = jnp.arange(seq_len, dtype=jnp.int32)
    visible = (key_places[None, :] <= positions[:, None]) & (seq_ids[None, :] == query_ids[:, None])

    def attend_group(pieces):
        q_part, k_part, v_part = pieces
        scores = jnp.einsum("qhd,khd->hqk", q_part, k_part, preferred_element_type=floats)
        scores = jnp.where(visible[None], scores, neg_fill)
        top_score = jnp.max(scores, axis=-1, keepdims=True)
        grown = jnp.exp(scores - top_score)
        total = jnp.sum(grown, axis=-1, keepdims=True)
        probs_low = (grown / total).astype(halves)
        mixed = jnp.einsum("hqk,khd->qhd", probs_low, v_part, preferred_element_type=floats)
        return (mixed, top_score + jnp.log(total))

    mixed_groups, log_totals = lax.map(attend_group, (query_groups, key_all, value_all))
    attended = mixed_groups.transpose(1, 0, 2, 3).reshape(tok_count, width).astype(halves)
    saved = (normed, unit, query_groups, key_all, value_all, log_totals, attended, cosine, sine, visible)
    return dot(attended, out_weight), saved


def rows_backward(weights, saved, mid_low):
    weight, out_weight = weights
    normed, unit, query_groups, key_all, value_all, log_totals, attended, cosine, sine, visible = saved
    tok_count, width = mid_low.shape
    head_groups = HEADS // group_heads
    scale = 1.0 / math.sqrt(HEAD_DIM)
    attended_grad = dot_nt(mid_low, out_weight).astype(halves)
    grad_groups = attended_grad.reshape(tok_count, head_groups, group_heads, HEAD_DIM).transpose(
        1, 0, 2, 3
    )

    def attend_back(pieces):
        q_part, k_part, v_part, g_part, log_part = pieces
        scores = jnp.einsum("qhd,khd->hqk", q_part, k_part, preferred_element_type=floats)
        scores = jnp.where(visible[None], scores, neg_fill)
        probs = jnp.exp(scores - log_part)
        prob_grad = jnp.einsum("qhd,khd->hqk", g_part, v_part, preferred_element_type=floats)
        delta = jnp.sum(probs * prob_grad, axis=-1, keepdims=True)
        score_grad = (probs * (prob_grad - delta)).astype(halves)
        q_grad = jnp.einsum("hqk,khd->qhd", score_grad, k_part, preferred_element_type=floats)
        k_grad = jnp.einsum("hqk,qhd->khd", score_grad, q_part, preferred_element_type=floats)
        v_grad = jnp.einsum(
            "hqk,qhd->khd", probs.astype(halves), g_part, preferred_element_type=floats
        )
        return (q_grad, k_grad, v_grad)

    query_grads, key_grads, value_grads = lax.map(
        attend_back, (query_groups, key_all, value_all, grad_groups, log_totals)
    )
    key_grad = lax.psum_scatter(key_grads, group, scatter_dimension=1, tiled=True)
    value_grad = lax.psum_scatter(value_grads, group, scatter_dimension=1, tiled=True)

    def by_head(array):
        return array.transpose(1, 0, 2, 3).reshape(tok_count, HEADS, HEAD_DIM)

    proj_grad = jnp.concatenate(
        [
            rotate_back(by_head(query_grads) * scale, cosine, sine).reshape(tok_count, width),
            rotate_back(by_head(key_grad), cosine, sine).reshape(tok_count, width),
            by_head(value_grad).reshape(tok_count, width),
        ],
        axis=-1,
    ).astype(halves)
    bias_part = jnp.sum(proj_grad.astype(floats), axis=0)
    attn_in_grad = dot_nt(proj_grad, weight)
    gain_part = jnp.sum(attn_in_grad * unit, axis=0)
    qkv_out = lax.psum_scatter(dot_tn(normed, proj_grad), every, scatter_dimension=0, tiled=True)
    out_out = lax.psum_scatter(dot_tn(attended, mid_low), every, scatter_dimension=0, tiled=True)
    return attn_in_grad, gain_part, bias_part, qkv_out, out_out


def shards(
    tokens,
    cotangent,
    segments,
    expert_ids,
    slot_order,
    gate_weights,
    qkv_weight,
    qkv_bias,
    out_weight,
    norm_attn,
    norm_ffn,
    shared_gate_up,
    shared_down,
    shared_gate,
    expert_gate_up,
    expert_down,
):
    count = lax.axis_size(group)
    devices = lax.axis_size(every)
    core = lax.axis_index("context")
    place = lax.axis_index("dp")
    index = lax.axis_index(group)
    tok_count, width = tokens.shape[1:]
    topk = expert_ids.shape[2]
    pairs = tok_count * topk
    experts = expert_gate_up.shape[0] * lax.axis_size("expert")
    capacity = (9 * pairs + 8 * experts - 1) // (8 * experts)
    length = count * tok_count
    by_heads = HEADS % count == 0

    vectors = [norm_attn, norm_ffn, shared_gate, qkv_bias]
    lengths = [vector.shape[0] for vector in vectors]

    def core_half(array, axis, which):
        size = array.shape[axis] // 2
        return lax.dynamic_slice_in_dim(array, which * size, size, axis)

    def expert_of(array, which):
        return lax.dynamic_index_in_dim(array, which, 0, keepdims=False)

    def gate_up_half(which):
        part = core_half(shared_gate_up, 2, which)
        return jnp.concatenate([part[0], part[1]], axis=-1)

    down_turned = shared_down.T

    own_tokens = tokens[0]
    resid_in = own_tokens.astype(floats)
    ed_first = expert_of(expert_down, core)
    ed_first = lax.all_gather(ed_first, "dp", axis=0)
    ed_second = other_core(expert_of(expert_down, 1 - core))
    su_both = both_cores(gate_up_half(core), gate_up_half(1 - core))
    sd_both = both_cores(core_half(down_turned, 1, core), core_half(down_turned, 1, 1 - core))
    eu_both = both_cores(expert_of(expert_gate_up, core), expert_of(expert_gate_up, 1 - core))

    if by_heads:
        cut = head_cut(qkv_weight, out_weight, vectors)
        marks = (cut,)
        all_tokens = lax.all_gather(after(own_tokens, cut), group, axis=0, tiled=True)
        cut_x, cut_y = near_blocks(cut)
        weights, gathered, previous = head_weights(
            cut, cut_x, cut_y, (ed_second, su_both, sd_both, eu_both)
        )
    else:
        weights = rows_weights(qkv_weight, out_weight)
        payload = jnp.concatenate([vector.astype(floats) for vector in vectors])
        payload = jnp.pad(payload, (0, -payload.shape[0] % 128))
        small = spread(payload)
        gathered = []
        for at, size in enumerate(lengths):
            first = sum(lengths[:at])
            gathered.append(small[:, first : first + size].reshape(-1))
        previous = marks = weights
    gain_attn, gain_ffn, gate_vector, bias = gathered

    routing = [expert_ids[0].reshape(pairs), slot_order[0, 0], gate_weights[0].reshape(pairs)]
    routing = jnp.concatenate([v.astype(floats) for v in routing]).reshape(1, -1, 128)
    routing = jnp.broadcast_to(routing, (count,) + routing.shape[1:])
    routing = lax.all_to_all(after(routing, *marks), group, split_axis=0, concat_axis=0, tiled=True)
    routing = routing.reshape(count, 3, tok_count, topk)
    pair_expert, pair_order, pair_gate = routing[:, 0], routing[:, 1], routing[:, 2]

    ed_second_x, ed_second_y = near_blocks(after(ed_second, *previous))
    ed_split = ed_second.shape[0] // 32 * 16
    ed_far = dp_step(ed_second_x[:ed_split], 2), dp_step(ed_second_y[ed_split:], 1)
    ed_pin = (ed_second_x, ed_second_y) + ed_far
    expert_up = gather_rows(eu_both)
    if by_heads:
        grads_line = gather_line(after(cotangent[0], all_tokens))
        mixed, saved, marks = heads_forward(
            all_tokens, gain_attn, bias, weights, segments[0], (grads_line,) + ed_pin
        )
        all_grads = gather_cores(after(grads_line, mixed))
    else:
        mixed, saved = rows_forward(own_tokens, gain_attn, bias, weights, segments[0])
        all_grads = group_gather(cotangent[0])
        marks = (mixed, mixed)
    shared_up = gather_rows(after(su_both, marks[0]))
    shared_dn = gather_rows(after(sd_both, marks[1]))
    hidden_units = shared_dn.shape[1]
    own_at = lambda out, at: out.at[at]
    firsts = lambda out, at: out.at[pl.ds(at, 4)]
    far_low = lambda out, at: out.at[at, pl.ds(0, ed_split)]
    far_high = lambda out, at: out.at[at, pl.ds(ed_split, ed_second.shape[0] - ed_split)]
    other_at = 4 - 4 * core
    expert_dn = place_blocks(
        [ed_first, ed_second, ed_second_x, ed_second_y, *ed_far],
        [4 * core] + [other_at + (place ^ step) for step in (0, 1, 2, 3, 3)],
        (8,) + ed_second.shape,
        [firsts, own_at, own_at, own_at, far_low, far_high],
    ).reshape(-1, width)
    ff_width = expert_dn.shape[0]

    resid_mid = resid_in + mixed
    stat_ffn = lax.rsqrt(jnp.mean(resid_mid * resid_mid, axis=-1, keepdims=True) + eps_norm)
    unit_ffn = resid_mid * stat_ffn
    normed_ffn = (unit_ffn * gain_ffn).astype(halves)
    grad_out = cotangent[0].astype(floats)

    all_normed = group_gather(normed_ffn)
    chosen = pair_expert == index.astype(floats)
    has_pair = jnp.any(chosen, axis=-1)
    order = jnp.sum(jnp.where(chosen, pair_order, 0.0), axis=-1)
    gate = jnp.sum(jnp.where(chosen, pair_gate, 0.0), axis=-1)
    earlier = has_pair[:, None, :] & (order[:, None, :] < order[:, :, None])
    rank = jnp.sum(earlier.astype(jnp.int32), axis=-1)
    kept = has_pair & (rank < capacity)
    gate = jnp.where(kept, gate, 0.0)
    slots = jnp.arange(capacity, dtype=jnp.int32)
    select = (rank[:, None, :] == slots[None, :, None]) & kept[:, None, :]
    slot_gate = jnp.sum(jnp.where(select, gate[:, None, :], 0.0), axis=-1).reshape(-1, 1)
    select = select.astype(halves)

    def to_slots(rows):
        got = jnp.einsum(
            "brt,btd->brd",
            select,
            rows.reshape(count, tok_count, width),
            preferred_element_type=floats,
        )
        return got.reshape(count * capacity, width)

    def from_slots(rows):
        got = jnp.einsum(
            "brt,brd->btd",
            select,
            rows.reshape(count, capacity, width),
            preferred_element_type=floats,
        )
        return got.reshape(length, width)

    slot_in = to_slots(all_normed).astype(halves)
    slot_grad = (to_slots(all_grads) * slot_gate).astype(halves)
    expert_pre = dot(slot_in, expert_up)
    expert_g, expert_u = expert_pre[:, :ff_width], expert_pre[:, ff_width:]
    expert_hidden = (jax.nn.silu(expert_g) * expert_u).astype(halves)
    hidden_grad = dot_nt(slot_grad, expert_dn)
    expert_pre_grad = jnp.concatenate(
        silu_parts(hidden_grad, expert_g, expert_u), axis=-1
    ).astype(halves)
    expert_out = dot(expert_hidden, expert_dn).astype(halves)
    slot_in_grad = dot_nt(expert_pre_grad, expert_up).astype(halves)
    eu_term = dot_tn(slot_in, expert_pre_grad).astype(halves)
    ed_term = dot_tn(expert_hidden, slot_grad).astype(halves)

    shared_pre = dot(after(all_normed, eu_term, ed_term), shared_up)
    shared_g, shared_u = shared_pre[:, :hidden_units], shared_pre[:, hidden_units:]
    shared_hidden = (jax.nn.silu(shared_g) * shared_u).astype(halves)
    gate_shared = jax.nn.sigmoid(
        jnp.sum(all_normed.astype(floats) * gate_vector, axis=-1, keepdims=True)
    )
    shared_grad = (gate_shared * all_grads.astype(floats)).astype(halves)
    hidden_grad = dot(shared_grad, shared_dn)
    shared_pre_grad = jnp.concatenate(
        silu_parts(hidden_grad, shared_g, shared_u), axis=-1
    ).astype(halves)
    shared_part = dot_nt(shared_hidden, shared_dn)
    logit_part = jnp.sum(all_grads.astype(floats) * shared_part, axis=-1)
    su_term = dot_tn(all_normed, shared_pre_grad).astype(halves)
    sd_term = dot_tn(shared_grad, shared_hidden).astype(halves)

    ffn_part = dot_nt(shared_pre_grad, shared_up) + from_slots(slot_in_grad)
    out_part = gate_shared * shared_part + gate.reshape(length, 1) * from_slots(expert_out)

    logit_sums = lax.all_to_all(
        logit_part.reshape(count, 1, tok_count), group, split_axis=0, concat_axis=0, tiled=True
    )
    own_gate = jax.nn.sigmoid(
        jnp.sum(normed_ffn.astype(floats) * gate_vector, axis=-1, keepdims=True)
    )
    logit_grad = jnp.sum(logit_sums, axis=0).reshape(tok_count, 1) * own_gate * (1.0 - own_gate)
    ffn_grad = group_reduce(ffn_part)[0] + logit_grad * gate_vector
    unit_grad = ffn_grad * gain_ffn
    gain_ffn_part = jnp.sum(ffn_grad * unit_ffn, axis=0)
    gate_vector_part = jnp.sum(logit_grad * normed_ffn.astype(floats), axis=0)
    mid_grad = grad_out + stat_ffn * (
        unit_grad - unit_ffn * jnp.mean(unit_grad * unit_ffn, axis=-1, keepdims=True)
    )
    mid_low = after(mid_grad.astype(halves), su_term, sd_term)

    su_sum, sd_sum, eu_sum = sum_weight(su_term), sum_weight(sd_term), sum_weight(eu_term)

    if by_heads:
        attn_in_grad, gain_attn_part, bias_part, qkv_out, out_weight_out, layer_sum, marks = heads_backward(
            all_tokens, gain_attn, weights, saved, mid_low, (eu_sum, su_sum, sd_sum, out_part)
        )
    else:
        attn_in_grad, gain_attn_part, bias_part, qkv_out, out_weight_out = rows_backward(
            weights, saved, mid_low
        )
        marks = (mid_low, attn_in_grad)
        layer_sum = group_reduce(out_part)[0]
    layer_sum = resid_mid + layer_sum
    mark_end = marks[1]

    ed_sum = sum_weight(after(ed_term, mark_end))
    su_sum, sd_sum, eu_sum = (after(total, mark_end) for total in (su_sum, sd_sum, eu_sum))
    shared_up_out = jnp.concatenate(
        [
            array.reshape(width // 8, 2, hidden_units).transpose(1, 0, 2)
            for array in cores_in_order(su_sum)
        ],
        axis=-1,
    ).astype(floats)
    shared_down_out = jnp.concatenate(cores_in_order(sd_sum), axis=-1).T.astype(floats)
    expert_up_out = jnp.stack(cores_in_order(eu_sum)).astype(floats)
    expert_down_out = jnp.stack(cores_in_order(ed_sum)).astype(floats)

    stat_attn = lax.rsqrt(jnp.mean(resid_in * resid_in, axis=-1, keepdims=True) + eps_norm)
    unit_attn = resid_in * stat_attn
    unit_grad = attn_in_grad * gain_attn
    input_grad = mid_grad + stat_attn * (
        unit_grad - unit_attn * jnp.mean(unit_grad * unit_attn, axis=-1, keepdims=True)
    )

    parts = [gain_attn_part, gain_ffn_part, gate_vector_part, bias_part]
    packed = jnp.concatenate([part.reshape(devices, -1) for part in parts], axis=1)
    total = packed.shape[1]
    packed = jnp.pad(after(packed, mark_end), ((0, 0), (0, -total % 128)))
    packed = lax.all_to_all(
        packed.reshape(devices, -1, 128), every, split_axis=0, concat_axis=0, tiled=True
    )
    sums = jnp.sum(packed, axis=0).reshape(-1)
    at = 0
    small_out = []
    for size in lengths:
        small_out.append(sums[at : at + size])
        at += size
    gain_attn_out, gain_ffn_out, gate_vector_out, bias_out = small_out
    return (
        layer_sum.astype(halves)[None],
        input_grad[None],
        qkv_out,
        bias_out,
        out_weight_out,
        gain_attn_out,
        gain_ffn_out,
        shared_up_out,
        shared_down_out,
        gate_vector_out,
        expert_up_out,
        expert_down_out,
    )


def solution(mesh):
    placed = (
        P("dp", ("expert", "context"), None),
        P("dp", ("expert", "context"), None),
        P("dp", None),
        P("dp", ("expert", "context"), None),
        P("dp", ("expert", "context"), None),
        P("dp", ("expert", "context"), None),
        P(("expert", "context", "dp"), None),
        P(("expert", "context", "dp")),
        P(("expert", "context", "dp"), None),
        P(("expert", "context", "dp")),
        P(("expert", "context", "dp")),
        P(None, ("context", "dp"), "expert"),
        P("expert", ("context", "dp")),
        P(("expert", "context", "dp")),
        P("expert", ("context", "dp"), None),
        P("expert", ("context", "dp"), None),
    )
    return jax.shard_map(
        shards,
        mesh=mesh,
        in_specs=placed,
        out_specs=(
            P("dp", ("expert", "context"), None),
            P("dp", ("expert", "context"), None),
            P(("expert", "context", "dp"), None),
            P(("expert", "context", "dp")),
            P(("expert", "context", "dp"), None),
            P(("expert", "context", "dp")),
            P(("expert", "context", "dp")),
            P(None, ("context", "dp"), "expert"),
            P("expert", ("context", "dp")),
            P(("expert", "context", "dp")),
            P("expert", ("context", "dp"), None),
            P("expert", ("context", "dp"), None),
        ),
        check_vma=False,
    )
```

```python
import math

import jax
import jax.numpy as jnp
from jax import lax
from jax.experimental import pallas as pl
from jax.experimental.pallas import tpu as pltpu
from jax.sharding import PartitionSpec as P

HEADS = 16
HEAD_DIM = 128


eps_norm = 1e-06
neg_fill = -1e30
rope_base = 1000000.0
group_heads = 4
floats = jnp.float32
halves = jnp.bfloat16
every = ("expert", "context", "dp")
group = ("expert", "context")
cost_scale = 0.0


def rope_tables(positions, half):
    inverse = jnp.exp(
        jnp.arange(half).astype(jnp.float32) * (-2.0 * math.log(rope_base) / (2 * half))
    )
    angle = positions.astype(jnp.float32)[:, None] * inverse[None, :]
    return (jnp.cos(angle), jnp.sin(angle))


def rotate(values, cosine, sine):
    half = values.shape[-1] // 2
    front = values[..., :half]
    behind = values[..., half:]
    cosine = cosine[:, None, :]
    sine = sine[:, None, :]
    return jnp.concatenate(
        [front * cosine - behind * sine, behind * cosine + front * sine], axis=-1
    )


def rotate_back(grads, cosine, sine):
    half = grads.shape[-1] // 2
    front = grads[..., :half]
    behind = grads[..., half:]
    cosine = cosine[:, None, :]
    sine = sine[:, None, :]
    return jnp.concatenate(
        [front * cosine + behind * sine, behind * cosine - front * sine], axis=-1
    )


def silu_parts(grad_hidden, gate_pre, up_pre):
    sigma = jax.nn.sigmoid(gate_pre)
    gate_grad = grad_hidden * up_pre * sigma * (1.0 + gate_pre * (1.0 - sigma))
    up_grad = grad_hidden * gate_pre * sigma
    return (gate_grad, up_grad)


def dot(left, right):
    return jnp.dot(left, right, preferred_element_type=floats)


def dot_tn(left, right):
    return lax.dot_general(left, right, (((0,), (0,)), ((), ())), preferred_element_type=floats)


def dot_nt(left, right):
    return lax.dot_general(left, right, (((1,), (1,)), ((), ())), preferred_element_type=floats)


def dp_step(value, step):
    count = lax.axis_size("dp")
    return lax.ppermute(value, "dp", [(i, i ^ step) for i in range(count)])


def other_core(value):
    return lax.ppermute(value, "context", [(0, 1), (1, 0)])


def after(value, *others):
    return lax.optimization_barrier((value,) + others)[0]


def near_blocks(block):
    return dp_step(block, 1), dp_step(block, 2)


def place_blocks(pieces, places, out_shape, views, window):
    at, size = window

    count = len(pieces)

    def kernel(place_ref, *refs):
        blocks, out, held = refs[:count], refs[count], refs[count + 1 : 2 * count + 1]
        in_sems, out_sems = refs[2 * count + 1 :]
        loads = [
            pltpu.make_async_copy(blocks[i].at[..., pl.ds(at, size)], held[i], in_sems.at[i])
            for i in range(count)
        ]
        stores = [
            pltpu.make_async_copy(held[i], views[i](out, place_ref[i]), out_sems.at[i])
            for i in range(count)
        ]
        for load in loads:
            load.start()
        for load, store in zip(loads, stores):
            load.wait()
            store.start()
        for store in stores:
            store.wait()

    return pl.pallas_call(
        kernel,
        out_shape=jax.ShapeDtypeStruct(out_shape, pieces[0].dtype),
        in_specs=[pl.BlockSpec(memory_space=pltpu.SMEM)]
        + [pl.BlockSpec(memory_space=pl.ANY)] * len(pieces),
        out_specs=pl.BlockSpec(memory_space=pl.ANY),
        scratch_shapes=[pltpu.VMEM(piece.shape[:-1] + (size,), piece.dtype) for piece in pieces]
        + [
            pltpu.SemaphoreType.DMA((count,)),
            pltpu.SemaphoreType.DMA((count,)),
        ],
        compiler_params=pltpu.CompilerParams(vmem_limit_bytes=32 * 1024 * 1024),
        cost_estimate=pl.CostEstimate(
            flops=0, bytes_accessed=1024, transcendentals=0
        ),
    )(jnp.stack(places).astype(jnp.int32), *pieces)


def sum_weight(part):
    rows, wide = part.shape
    return lax.psum_scatter(
        part.reshape(2, rows // 2, wide), "dp", scatter_dimension=1, tiled=True
    )


def both_cores(kept, given):
    core = lax.axis_index("context")
    taken = other_core(given)
    return jnp.stack([jnp.where(core == 0, kept, taken), jnp.where(core == 0, taken, kept)])


def gather_rows(both):
    out = lax.all_gather(both, "dp", axis=1, tiled=True)
    return out.reshape(-1, both.shape[2])


def cores_in_order(blocks):
    core = lax.axis_index("context")
    mine = jnp.where(core == 0, blocks[0], blocks[1])
    other = other_core(jnp.where(core == 0, blocks[1], blocks[0]))
    return jnp.where(core == 0, mine, other), jnp.where(core == 0, other, mine)


def along_expert(blocks):
    return lax.all_to_all(blocks, "expert", split_axis=0, concat_axis=0, tiled=True)


def gather_line(block):
    return along_expert(jnp.broadcast_to(block[None], (lax.axis_size("expert"),) + block.shape))


def gather_cores(mine):
    core = lax.axis_index("context")
    other = other_core(mine)
    both = jnp.stack([jnp.where(core == 0, mine, other), jnp.where(core == 0, other, mine)], axis=1)
    return both.reshape((-1,) + mine.shape[2:])


def group_sum(mine, other):
    rows = (mine.astype(floats) + other_core(other).astype(floats)).astype(halves)
    return jnp.sum(along_expert(rows).astype(floats), axis=0)


up_line = [(0, 1), (1, 2), (2, 3)]
down_line = [(1, 0), (2, 1), (3, 2)]
cross_line = [(0, 2), (1, 3), (2, 0), (3, 1)]


def line_gather(block, *pins):
    here = lax.axis_index("expert")
    second = lax.ppermute(block, "expert", cross_line)
    lower = lax.ppermute(block, "expert", up_line)
    upper = lax.ppermute(block, "expert", down_line)
    third = lax.ppermute(second, "expert", [(2, 3), (1, 0)])
    third = after(third, *pins) if pins else third
    mine = jnp.stack(
        [block, jnp.where(here == 3, third, upper), second, jnp.where(here == 0, third, lower)]
    )
    return mine


def line_sum(mine, other, *pins):
    here = lax.axis_index("expert")
    rows = [
        (mine[k].astype(floats) + other[k].astype(floats)).astype(halves) for k in range(4)
    ]
    corner = lax.ppermute(jnp.where(here == 3, rows[1], rows[3]), "expert", [(3, 2), (0, 1)])
    lower = lax.ppermute(rows[1], "expert", up_line)
    upper = lax.ppermute(rows[3], "expert", down_line)
    passed = (rows[2].astype(floats) + corner.astype(floats)).astype(halves)
    second = lax.ppermute(passed, "expert", cross_line)
    second = after(second, *pins) if pins else second
    return (
        rows[0].astype(floats) + lower.astype(floats) + upper.astype(floats) + second.astype(floats)
    )


def further_on(array, back=False):
    here = lax.axis_index("expert")
    count = array.shape[0]
    array = jnp.where(lax.axis_index("context") == 0, array, array[:, ::-1])
    start = lax.rem(count - here, count) if back else here
    return lax.dynamic_slice_in_dim(jnp.concatenate([array, array]), start, count, 0)


def spread(values):
    count = lax.axis_size(every)
    padded = jnp.broadcast_to(values.reshape(1, -1, 128), (count, values.shape[0] // 128, 128))
    got = lax.all_to_all(padded, every, split_axis=0, concat_axis=0, tiled=True)
    return got.reshape(count, -1)


def kernel_call(kernel, out_shapes, in_specs, out_specs, flops, grid=None, scratch=(), aliases=None):
    extra = {} if grid is None else {"grid": grid}
    return pl.pallas_call(
        kernel,
        out_shape=out_shapes,
        in_specs=in_specs,
        out_specs=out_specs,
        scratch_shapes=list(scratch),
        input_output_aliases=aliases or {},
        compiler_params=pltpu.CompilerParams(vmem_limit_bytes=56 * 1024 * 1024),
        cost_estimate=pl.CostEstimate(
            flops=int(flops * cost_scale), bytes_accessed=1024, transcendentals=0
        ),
        **extra,
    )


def kdot(left, right, dims):
    return lax.dot_general(left, right, (dims, ((), ())), preferred_element_type=floats)


nn = ((1,), (0,))
nt = ((1,), (1,))
tn = ((0,), (0,))


def ordered(core, first, second):
    return jnp.where(core == 0, first, second), jnp.where(core == 0, second, first)


def pack_shared(core, gate_up, down):
    rows, both = gate_up.shape[1:]
    units = both // 2
    full = units + -units % 128

    def kernel(core_ref, up_ref, down_ref, out):
        keep = lax.broadcasted_iota(jnp.int32, (rows, full), 1) < units
        fill = jnp.zeros((rows, full - units), floats)
        for at in range(3):
            if at < 2:
                part = up_ref[at].astype(floats)
                low = part[:, :full]
                high = pltpu.roll(part, units, 1)[:, :full]
            else:
                low = jnp.concatenate([down_ref[:units, :].astype(floats).T, fill], axis=1)
                high = jnp.concatenate([down_ref[units:, :].astype(floats).T, fill], axis=1)
            low, high = jnp.where(keep, low, 0.0), jnp.where(keep, high, 0.0)
            mine, other = ordered(core_ref[0], low, high)
            columns = slice(at * full, (at + 1) * full)
            out[0, :, columns] = mine.astype(halves)
            out[1, :, columns] = other.astype(halves)

    vmem = pl.BlockSpec(memory_space=pltpu.VMEM)
    return kernel_call(
        kernel,
        jax.ShapeDtypeStruct((2, rows, 3 * full), halves),
        [pl.BlockSpec(memory_space=pltpu.SMEM), vmem, vmem],
        vmem,
        0,
    )(core, gate_up, down)


def unpack_shared(core, sums, got, units):
    rows, wide = got.shape
    full = wide // 3

    def kernel(core_ref, sums_ref, got_ref, up_out, down_out):
        low, high = ordered(core_ref[0], sums_ref[core_ref[0]], got_ref[...])
        fill = jnp.zeros((rows, 2 * units - full), floats)
        for at in range(2):
            columns = slice(at * full, (at + 1) * full)
            first = jnp.concatenate([low[:, columns].astype(floats), fill], axis=1)
            second = jnp.concatenate([high[:, columns].astype(floats), fill], axis=1)
            up_out[at] = first + pltpu.roll(second, units, 1)
        down_out[:units, :] = low[:, 2 * full :].astype(floats).T[:units]
        down_out[units:, :] = high[:, 2 * full :].astype(floats).T[:units]

    vmem = pl.BlockSpec(memory_space=pltpu.VMEM)
    shape = jax.ShapeDtypeStruct
    return kernel_call(
        kernel,
        (shape((2, rows, 2 * units), floats), shape((2 * units, rows), floats)),
        [pl.BlockSpec(memory_space=pltpu.SMEM), vmem, vmem],
        (vmem, vmem),
        0,
    )(core, sums, got)


def attention_forward(core, places, tokens, gain, blocks, bias, cosine, sine, seg_col, seg_row):
    length, width = tokens.shape
    count, rows_each, wide = blocks[0].shape
    piece = (wide - 128) // 4
    half = count // 2
    spans = [(0, count)] * 3 + [(0, half), (half, count)]
    heads = piece // HEAD_DIM
    scale = 1.0 / math.sqrt(HEAD_DIM)
    tile = 256

    def kernel(
        core_ref, place_ref, tok, gain_ref, bias_ref, cos_ref, sin_ref, segc, segr, *refs
    ):
        pieces, refs = refs[:5], refs[5:]
        w, wout, normed, query, key, value, lse, attended, mine, other, sems = refs
        copies = []
        for i, (first, last) in enumerate(spans):
            for g in range(first, last):
                row = pl.multiple_of((g * 4 + place_ref[i]) * rows_each, rows_each)
                copies.append(
                    pltpu.make_async_copy(
                        pieces[i].at[g - first, :, pl.ds(0, 3 * piece)],
                        w.at[pl.ds(row, rows_each)],
                        sems.at[len(copies)],
                    )
                )
                row = pl.multiple_of(place_ref[i] * rows_each, rows_each)
                copies.append(
                    pltpu.make_async_copy(
                        pieces[i].at[g - first, :, pl.ds(3 * piece + 128, piece)],
                        wout.at[pl.ds(row, rows_each), pl.ds(g * piece, piece)],
                        sems.at[len(copies)],
                    )
                )
        for copy in copies:
            copy.start()
        for copy in copies:
            copy.wait()
        for t in range(length // tile):
            rows = pl.ds(t * tile, tile)
            x = tok[rows, :].astype(floats)
            stat = lax.rsqrt(jnp.mean(x * x, axis=-1, keepdims=True) + eps_norm)
            low = (x * stat * gain_ref[...]).astype(halves)
            normed[rows, :] = low
            proj = kdot(low, w[...], nn) + bias_ref[...]
            c, s = cos_ref[rows, :], sin_ref[rows, :]
            for h in range(heads):
                at = slice(h * HEAD_DIM, (h + 1) * HEAD_DIM)
                q = proj[:, at]
                query[rows, at] = ((q * c + pltpu.roll(q, 64, 1) * s) * scale).astype(halves)
                k = proj[:, piece + h * HEAD_DIM : piece + (h + 1) * HEAD_DIM]
                key[rows, at] = (k * c + pltpu.roll(k, 64, 1) * s).astype(halves)
            value[rows, :] = proj[:, 2 * piece :].astype(halves)
        for t in range(length // tile):
            rows = pl.ds(t * tile, tile)
            seen = (t + 1) * tile
            place = lax.broadcasted_iota(jnp.int32, (tile, seen), 0) + t * tile
            visible = (lax.broadcasted_iota(jnp.int32, (tile, seen), 1) <= place) & (
                segc[rows, :] == segr[:, :seen]
            )
            for h in range(heads):
                at = slice(h * HEAD_DIM, (h + 1) * HEAD_DIM)
                scores = kdot(query[rows, at], key[:seen, at], nt)
                scores = jnp.where(visible, scores, neg_fill)
                top = jnp.max(scores, axis=-1, keepdims=True)
                grown = jnp.exp(scores - top)
                total = jnp.sum(grown, axis=-1, keepdims=True)
                probs = (grown / total).astype(halves)
                attended[rows, at] = kdot(probs, value[:seen, at], nn).astype(halves)
                lse[rows, h : h + 1] = top + jnp.log(total)
            mixed = kdot(attended[rows, :], wout[...], nn).astype(halves)
            k = lax.rem(t + 4 - core_ref[1], 4)
            mine[k], other[k] = ordered(core_ref[0], mixed[: tile // 2], mixed[tile // 2 :])

    vmem = pl.BlockSpec(memory_space=pltpu.VMEM)
    shape = jax.ShapeDtypeStruct
    return kernel_call(
        kernel,
        (
            shape((width, 3 * piece), halves),
            shape((piece, width), halves),
            shape((length, width), halves),
            shape((length, piece), halves),
            shape((length, piece), halves),
            shape((length, piece), halves),
            shape((length, heads), floats),
            shape((length, piece), halves),
            shape((length // tile, tile // 2, width), halves),
            shape((length // tile, tile // 2, width), halves),
        ),
        [pl.BlockSpec(memory_space=pltpu.SMEM)] * 2
        + [vmem] * 7
        + [pl.BlockSpec(memory_space=pl.ANY)] * 5,
        (vmem,) * 10,
        2 * length * width * 4 * piece + 2 * length * length * 2 * piece,
        scratch=[pltpu.SemaphoreType.DMA((8 * count,))],
    )(core, places, tokens, gain, bias, cosine, sine, seg_col, seg_row, *blocks)


def attention_backward(
    core, mid_mine, mid_other, tokens, weight, cosine, sine, seg_col, seg_row, out_rows,
    query, key, value, lse, attended,
):
    length, width = tokens.shape
    piece = out_rows.shape[0]
    heads = piece // HEAD_DIM
    scale = 1.0 / math.sqrt(HEAD_DIM)
    tile = 256

    def kernel(
        core_ref, mid_m, mid_o, tok, w, cos_ref, sin_ref, segc, segr, wout, q_ref, k_ref, v_ref, lse_ref,
        att_ref, proj_grad, mine, other, gain_part, bias_part, out_part, key_grad, value_grad, out_grad,
    ):
        out_grad[...] = jnp.zeros_like(out_grad)
        key_grad[...] = jnp.zeros_like(key_grad)
        value_grad[...] = jnp.zeros_like(value_grad)
        for t in range(length // tile):
            rows = pl.ds(t * tile, tile)
            seen = (t + 1) * tile
            place = lax.broadcasted_iota(jnp.int32, (tile, seen), 0) + t * tile
            visible = (lax.broadcasted_iota(jnp.int32, (tile, seen), 1) <= place) & (
                segc[rows, :] == segr[:, :seen]
            )
            k = lax.rem(t + 4 - core_ref[1], 4)
            mid = jnp.concatenate(ordered(core_ref[0], mid_m[k], mid_o[k]))
            grad = kdot(mid, wout[...], nt).astype(halves)
            out_grad[...] += kdot(att_ref[rows, :], mid, tn)
            c, s = cos_ref[rows, :], sin_ref[rows, :]
            for h in range(heads):
                at = slice(h * HEAD_DIM, (h + 1) * HEAD_DIM)
                query = q_ref[rows, at]
                scores = kdot(query, k_ref[:seen, at], nt)
                probs = jnp.where(visible, jnp.exp(scores - lse_ref[rows, h : h + 1]), 0.0)
                prob_grad = kdot(grad[:, at], v_ref[:seen, at], nt)
                delta = jnp.sum(probs * prob_grad, axis=-1, keepdims=True)
                score_grad = (probs * (prob_grad - delta)).astype(halves)
                q_grad = kdot(score_grad, k_ref[:seen, at], nn) * scale
                proj_grad[rows, at] = (q_grad * c - pltpu.roll(q_grad, 64, 1) * s).astype(halves)
                key_grad[:seen, at] += kdot(score_grad, query, tn)
                value_grad[:seen, at] += kdot(probs.astype(halves), grad[:, at], tn)
        gains = jnp.zeros((1, width), floats)
        biases = jnp.zeros((1, 3 * piece), floats)
        for t in range(length // tile):
            rows = pl.ds(t * tile, tile)
            c, s = cos_ref[rows, :], sin_ref[rows, :]
            for h in range(heads):
                at = slice(h * HEAD_DIM, (h + 1) * HEAD_DIM)
                k_grad = key_grad[rows, at]
                proj_grad[rows, piece + h * HEAD_DIM : piece + (h + 1) * HEAD_DIM] = (
                    k_grad * c - pltpu.roll(k_grad, 64, 1) * s
                ).astype(halves)
            proj_grad[rows, 2 * piece :] = value_grad[rows, :].astype(halves)
            grads = proj_grad[rows, :]
            biases = biases + jnp.sum(grads.astype(floats), axis=0, keepdims=True)
            part = kdot(grads, w[...], nt)
            x = tok[rows, :].astype(floats)
            stat = lax.rsqrt(jnp.mean(x * x, axis=-1, keepdims=True) + eps_norm)
            gains = gains + jnp.sum(part * (x * stat), axis=0, keepdims=True)
            k = lax.rem(t + 4 - core_ref[1], 4)
            part = part.astype(halves)
            mine[k], other[k] = ordered(core_ref[0], part[: tile // 2], part[tile // 2 :])
        out_part[...] = out_grad[...].astype(halves)
        gain_part[...] = gains
        bias_part[...] = biases

    vmem = pl.BlockSpec(memory_space=pltpu.VMEM)
    shape = jax.ShapeDtypeStruct
    return kernel_call(
        kernel,
        (
            shape((length, 3 * piece), halves),
            shape((length // tile, tile // 2, width), halves),
            shape((length // tile, tile // 2, width), halves),
            shape((1, width), floats),
            shape((1, 3 * piece), floats),
            shape((piece, width), halves),
        ),
        [pl.BlockSpec(memory_space=pltpu.SMEM)] + [vmem] * 14,
        (vmem,) * 6,
        2 * length * width * 5 * piece + 2 * length * length * 5 * piece,
        scratch=[
            pltpu.VMEM((length, piece), floats),
            pltpu.VMEM((length, piece), floats),
            pltpu.VMEM((piece, width), floats),
        ],
    )(
        core, mid_mine, mid_other, tokens, weight, cosine, sine, seg_col, seg_row, out_rows,
        query, key, value, lse, attended,
    )


def expert_pass(slot_row, gate_row, rows_in, grads_in, up, downs, places, capacity):
    pairs, half, width = rows_in[0].shape
    rows_each = downs[0].shape[0]
    ff = rows_each * len(downs)
    pair = 2 * half
    count = pairs * capacity
    wide = 2 * ff

    def kernel(
        place_ref, slot_ref, gate_ref, x_mine, x_other, g_mine, g_other, up_hbm, *refs
    ):
        downs_hbm, refs = refs[: len(downs)], refs[len(downs) :]
        slot_in, slot_grad, hidden, pre_grad, out, in_grad, w_up, w_down, pre, up_sems, down_sems = refs
        chunk = 256
        chunks = wide // chunk
        loads = [
            pltpu.make_async_copy(
                up_hbm.at[:, pl.ds(j * chunk, chunk)], w_up.at[:, pl.ds(j * chunk, chunk)], up_sems.at[j]
            )
            for j in range(chunks)
        ]
        down_loads = [
            pltpu.make_async_copy(
                block,
                w_down.at[pl.ds(pl.multiple_of(place_ref[i] * rows_each, 16), rows_each)],
                down_sems.at[i],
            )
            for i, block in enumerate(downs_hbm)
        ]
        for load in loads + down_loads:
            load.start()
        for p in range(pairs):
            slots = pl.ds(p * capacity, capacity)
            picks = lax.broadcasted_iota(jnp.int32, (capacity, pair), 0) == slot_ref[p]
            pick = jnp.where(picks, 1.0, 0.0).astype(halves)
            gates = jnp.sum(jnp.where(picks, gate_ref[p], 0.0), axis=-1, keepdims=True)
            x = jnp.concatenate([x_mine[p], x_other[p]])
            slot_in[slots, :] = kdot(pick, x, nn).astype(halves)
            g = jnp.concatenate([g_mine[p], g_other[p]])
            slot_grad[slots, :] = (kdot(pick, g, nn) * gates).astype(halves)
        for j in range(chunks):
            loads[j].wait()
            at = pl.ds(j * chunk, chunk)
            pre[:, at] = kdot(slot_in[...], w_up[:, at], nn)
        for load in down_loads:
            load.wait()
        start = 0
        while start < ff:
            size = min(256, ff - start)
            at = slice(start, start + size)
            up_at = slice(ff + start, ff + start + size)
            grad = kdot(slot_grad[...], w_down[at, :], nt)
            gate_pre, up_pre = pre[:, at], pre[:, up_at]
            sigma = jax.nn.sigmoid(gate_pre)
            act = gate_pre * sigma
            hidden[:, at] = (act * up_pre).astype(halves)
            pre_grad[:, at] = (grad * up_pre * sigma * (1.0 + gate_pre * (1.0 - sigma))).astype(halves)
            pre_grad[:, up_at] = (grad * act).astype(halves)
            start += size
        for j in range(width // 512):
            at = pl.ds(j * 512, 512)
            out[:, at] = kdot(hidden[...], w_down[:, at], nn).astype(halves)
            in_grad[:, at] = kdot(pre_grad[...], w_up[at, :], nt).astype(halves)

    vmem = pl.BlockSpec(memory_space=pltpu.VMEM)
    hbm = pl.BlockSpec(memory_space=pl.ANY)
    shape = jax.ShapeDtypeStruct
    return kernel_call(
        kernel,
        (
            shape((count, width), halves),
            shape((count, width), halves),
            shape((count, ff), halves),
            shape((count, wide), halves),
            shape((count, width), halves),
            shape((count, width), halves),
        ),
        [pl.BlockSpec(memory_space=pltpu.SMEM)] + [vmem] * 6 + [hbm] * (1 + len(downs)),
        (vmem,) * 6,
        2 * count * width * ff * 6,
        scratch=[
            pltpu.VMEM(up.shape, halves),
            pltpu.VMEM((ff, width), halves),
            pltpu.VMEM((count, wide), floats),
            pltpu.SemaphoreType.DMA((wide // 256,)),
            pltpu.SemaphoreType.DMA((len(downs),)),
        ],
    )(places, slot_row, gate_row, *rows_in, *grads_in, up, *downs)


def shared_pass(slot_col, gate_col, rows_in, grads_in, weights, vector, expert_out, expert_grad):
    pairs, half, width = rows_in[0].shape
    tile = 2 * half
    length = pairs * tile
    units = weights.shape[1] // 3
    capacity = expert_out.shape[0] * tile // length

    def kernel(
        slot_ref, gate_ref, x_mine, x_other, g_mine, g_other, up_ref, down_ref, vec_ref, eout_ref, egrad_ref,
        ffn_mine, ffn_other, out_mine, out_other, pre_grad, hidden, shared_grad, logit,
    ):
        x = jnp.concatenate([x_mine[0], x_other[0]])
        pre = kdot(x, up_ref[...], nn)
        gate_shared = jax.nn.sigmoid(
            jnp.sum(x.astype(floats) * vec_ref[...], axis=-1, keepdims=True)
        )
        grads = jnp.concatenate([g_mine[0], g_other[0]]).astype(floats)
        low_grad = (gate_shared * grads).astype(halves)
        shared_grad[...] = low_grad
        grad = kdot(low_grad, down_ref[...], nn)
        gate_pre, up_pre = pre[:, :units], pre[:, units:]
        sigma = jax.nn.sigmoid(gate_pre)
        act = gate_pre * sigma
        hid = (act * up_pre).astype(halves)
        hidden[...] = hid
        pre_grad[:, :units] = (grad * up_pre * sigma * (1.0 + gate_pre * (1.0 - sigma))).astype(halves)
        pre_grad[:, units:] = (grad * act).astype(halves)
        picks = lax.broadcasted_iota(jnp.int32, (tile, capacity), 1) == slot_ref[...]
        pick = jnp.where(picks, 1.0, 0.0).astype(halves)
        ffn = kdot(pre_grad[...], up_ref[...], nt) + kdot(pick, egrad_ref[...], nn)
        ffn_mine[0], ffn_other[0] = ffn[:half].astype(halves), ffn[half:].astype(halves)
        shared_out = kdot(hid, down_ref[...], nt)
        logit[...] = jnp.sum(grads * shared_out, axis=-1, keepdims=True)
        out = gate_shared * shared_out + gate_ref[...] * kdot(pick, eout_ref[...], nn)
        out_mine[0], out_other[0] = out[:half].astype(halves), out[half:].astype(halves)

    shape = jax.ShapeDtypeStruct
    rows = lambda n: pl.BlockSpec((tile, n), lambda i: (i, 0))
    whole = lambda a: pl.BlockSpec(a.shape, lambda i: (0,) * a.ndim)
    slots = pl.BlockSpec((capacity, width), lambda i: (i, 0))
    halfs = pl.BlockSpec((1, half, width), lambda i: (i, 0, 0))
    half_shape = shape((pairs, half, width), halves)
    return kernel_call(
        kernel,
        (half_shape,) * 4
        + (
            shape((length, 2 * units), halves),
            shape((length, units), halves),
            shape((length, width), halves),
            shape((length, 1), floats),
        ),
        [
            rows(1), rows(1), halfs, halfs, halfs, halfs,
            pl.BlockSpec((width, 2 * units), lambda i: (0, 0)),
            pl.BlockSpec((width, units), lambda i: (0, 2)),
            whole(vector), slots, slots,
        ],
        (halfs,) * 4 + (rows(2 * units), rows(units), rows(width), rows(1)),
        2 * length * width * units * 6,
        grid=(pairs,),
    )(slot_col, gate_col, *rows_in, *grads_in, weights, weights, vector, expert_out, expert_grad)


def weight_grad(lefts, right, into=None, at=0, wide=None):
    rows = lefts[0].shape[-1]
    depth, each = right.shape[0], lefts[0].shape[-2]
    tile = 256
    first = at // tile
    wide = right.shape[1] if wide is None else wide

    def kernel(*refs):
        left_refs, right_ref = refs[: len(lefts)], refs[len(lefts)]
        out, turned = refs[-2:]

        @pl.when(pl.program_id(0) == 0)
        def _():
            if len(lefts) == 1:
                turned[...] = left_refs[0][...].T
            else:
                for block in range(depth // each):
                    rows_low = left_refs[block % 2][block // 2]
                    turned[:, block * each : (block + 1) * each] = rows_low.T

        out[...] = kdot(turned[...], right_ref[...], nn).astype(halves)

    more = [] if into is None else [into]
    return kernel_call(
        kernel,
        jax.ShapeDtypeStruct((rows, wide), halves),
        [pl.BlockSpec(left.shape, lambda j, n=left.ndim: (0,) * n) for left in lefts]
        + [pl.BlockSpec((depth, tile), lambda j: (0, j))]
        + [pl.BlockSpec(memory_space=pl.ANY)] * len(more),
        pl.BlockSpec((rows, tile), lambda j: (0, first + j)),
        2 * depth * rows * right.shape[1],
        grid=(right.shape[1] // tile,),
        scratch=[pltpu.VMEM((rows, depth), halves)],
        aliases={len(lefts) + 1: 0} if more else {},
    )(*lefts, right, *more)


def head_cut(qkv_weight, out_weight, vectors):
    count = lax.axis_size(group)
    rows, wide = qkv_weight.shape
    piece = wide // (3 * count)
    cut = qkv_weight.reshape(rows, 3, count, piece).transpose(2, 0, 1, 3).reshape(count, rows, 3 * piece)
    columns = jnp.concatenate([vector.reshape(-1, rows) for vector in vectors]).T
    columns = jnp.pad(columns, ((0, 0), (0, 128 - columns.shape[1])))
    columns = jnp.broadcast_to(columns[None], (count,) + columns.shape)
    cut = jnp.concatenate([cut, columns], axis=-1)
    cut = lax.all_to_all(cut, group, split_axis=0, concat_axis=0, tiled=True)
    out = out_weight.reshape(rows, count, piece).transpose(1, 0, 2)
    return jnp.concatenate([cut, out], axis=-1)


def head_vectors(blocks, places):
    count, rows, wide = blocks[0].shape
    piece = (wide - 128) // 4
    half = count // 2
    whole = lambda out, at: out.at[:, at]
    low = lambda out, at: out.at[pl.ds(0, half), at]
    high = lambda out, at: out.at[pl.ds(half, half), at]
    packed = place_blocks(
        blocks, places, (count, 4, rows, 128), [whole] * 3 + [low, high], (3 * piece, 128)
    )
    columns = packed[..., :6].astype(floats)
    vectors = [columns[..., at].reshape(-1) for at in range(3)]
    vectors.append(columns[..., 3:].transpose(0, 1, 3, 2).reshape(-1))
    return vectors


def rows_weights(qkv_weight, out_weight):
    return (
        lax.all_gather(qkv_weight, every, axis=0, tiled=True),
        lax.all_gather(out_weight, every, axis=0, tiled=True),
    )


def rows_forward(own_tokens, gain, bias, weights, seq_ids):
    weight, out_weight = weights
    tok_count, width = own_tokens.shape
    seq_len = seq_ids.shape[0]
    head_groups = HEADS // group_heads
    block_place = lax.axis_index(group)
    positions = block_place * tok_count + jnp.arange(tok_count, dtype=jnp.int32)
    cosine, sine = rope_tables(positions, HEAD_DIM // 2)
    scale = 1.0 / math.sqrt(HEAD_DIM)
    tokens = own_tokens.astype(floats)
    stat = lax.rsqrt(jnp.mean(tokens * tokens, axis=-1, keepdims=True) + eps_norm)
    unit = tokens * stat
    normed = (unit * gain).astype(halves)
    projected = dot(normed, weight) + bias
    raw = projected.reshape(tok_count, 3, HEADS, HEAD_DIM)
    query = (rotate(raw[:, 0], cosine, sine) * scale).astype(halves)
    key = rotate(raw[:, 1], cosine, sine).astype(halves)
    value = raw[:, 2].astype(halves)

    def by_group(array):
        return array.reshape(tok_count, head_groups, group_heads, HEAD_DIM).transpose(1, 0, 2, 3)

    query_groups = by_group(query)
    key_all = lax.all_gather(by_group(key), group, axis=1, tiled=True)
    value_all = lax.all_gather(by_group(value), group, axis=1, tiled=True)
    query_ids = lax.dynamic_slice_in_dim(seq_ids, block_place * tok_count, tok_count)
    key_places = jnp.arange(seq_len, dtype=jnp.int32)
    visible = (key_places[None, :] <= positions[:, None]) & (seq_ids[None, :] == query_ids[:, None])

    def attend_group(pieces):
        q_part, k_part, v_part = pieces
        scores = jnp.einsum("qhd,khd->hqk", q_part, k_part, preferred_element_type=floats)
        scores = jnp.where(visible[None], scores, neg_fill)
        top_score = jnp.max(scores, axis=-1, keepdims=True)
        grown = jnp.exp(scores - top_score)
        total = jnp.sum(grown, axis=-1, keepdims=True)
        probs_low = (grown / total).astype(halves)
        mixed = jnp.einsum("hqk,khd->qhd", probs_low, v_part, preferred_element_type=floats)
        return (mixed, top_score + jnp.log(total))

    mixed_groups, log_totals = lax.map(attend_group, (query_groups, key_all, value_all))
    attended = mixed_groups.transpose(1, 0, 2, 3).reshape(tok_count, width).astype(halves)
    saved = (normed, unit, query_groups, key_all, value_all, log_totals, attended, cosine, sine, visible)
    return dot(attended, out_weight), saved


def rows_backward(weights, saved, mid_low):
    weight, out_weight = weights
    normed, unit, query_groups, key_all, value_all, log_totals, attended, cosine, sine, visible = saved
    tok_count, width = mid_low.shape
    head_groups = HEADS // group_heads
    scale = 1.0 / math.sqrt(HEAD_DIM)
    attended_grad = dot_nt(mid_low, out_weight).astype(halves)
    grad_groups = attended_grad.reshape(tok_count, head_groups, group_heads, HEAD_DIM).transpose(
        1, 0, 2, 3
    )

    def attend_back(pieces):
        q_part, k_part, v_part, g_part, log_part = pieces
        scores = jnp.einsum("qhd,khd->hqk", q_part, k_part, preferred_element_type=floats)
        scores = jnp.where(visible[None], scores, neg_fill)
        probs = jnp.exp(scores - log_part)
        prob_grad = jnp.einsum("qhd,khd->hqk", g_part, v_part, preferred_element_type=floats)
        delta = jnp.sum(probs * prob_grad, axis=-1, keepdims=True)
        score_grad = (probs * (prob_grad - delta)).astype(halves)
        q_grad = jnp.einsum("hqk,khd->qhd", score_grad, k_part, preferred_element_type=floats)
        k_grad = jnp.einsum("hqk,qhd->khd", score_grad, q_part, preferred_element_type=floats)
        v_grad = jnp.einsum(
            "hqk,qhd->khd", probs.astype(halves), g_part, preferred_element_type=floats
        )
        return (q_grad, k_grad, v_grad)

    query_grads, key_grads, value_grads = lax.map(
        attend_back, (query_groups, key_all, value_all, grad_groups, log_totals)
    )
    key_grad = lax.psum_scatter(key_grads, group, scatter_dimension=1, tiled=True)
    value_grad = lax.psum_scatter(value_grads, group, scatter_dimension=1, tiled=True)

    def by_head(array):
        return array.transpose(1, 0, 2, 3).reshape(tok_count, HEADS, HEAD_DIM)

    proj_grad = jnp.concatenate(
        [
            rotate_back(by_head(query_grads) * scale, cosine, sine).reshape(tok_count, width),
            rotate_back(by_head(key_grad), cosine, sine).reshape(tok_count, width),
            by_head(value_grad).reshape(tok_count, width),
        ],
        axis=-1,
    ).astype(halves)
    bias_part = jnp.sum(proj_grad.astype(floats), axis=0)
    attn_in_grad = dot_nt(proj_grad, weight)
    gain_part = jnp.sum(attn_in_grad * unit, axis=0)
    qkv_out = lax.psum_scatter(dot_tn(normed, proj_grad), every, scatter_dimension=0, tiled=True)
    out_out = lax.psum_scatter(dot_tn(attended, mid_low), every, scatter_dimension=0, tiled=True)
    return attn_in_grad, gain_part, bias_part, qkv_out, out_out


def routing_of(expert_ids, slot_order, gate_weights, count, mark):
    tok_count, topk = expert_ids.shape[1:]
    routing = [expert_ids[0].reshape(-1), slot_order[0, 0], gate_weights[0].reshape(-1)]
    routing = jnp.concatenate([v.astype(floats) for v in routing]).reshape(1, -1, 128)
    routing = jnp.broadcast_to(routing, (count,) + routing.shape[1:])
    routing = lax.all_to_all(after(routing, mark), group, split_axis=0, concat_axis=0, tiled=True)
    routing = routing.reshape(count, 3, tok_count, topk)
    return routing[:, 0], routing[:, 1], routing[:, 2]


def slots_of(routes, index, capacity):
    pair_expert, pair_order, pair_gate = routes
    chosen = pair_expert == index.astype(floats)
    has_pair = jnp.any(chosen, axis=-1)
    order = jnp.sum(jnp.where(chosen, pair_order, 0.0), axis=-1)
    gate = jnp.sum(jnp.where(chosen, pair_gate, 0.0), axis=-1)
    earlier = has_pair[:, None, :] & (order[:, None, :] < order[:, :, None])
    rank = jnp.sum(earlier.astype(jnp.int32), axis=-1)
    kept = has_pair & (rank < capacity)
    return rank, kept, jnp.where(kept, gate, 0.0)


def small_sums(parts, lengths, mark):
    devices = lax.axis_size(every)
    packed = jnp.concatenate([part.reshape(devices, -1) for part in parts], axis=1)
    packed = jnp.pad(after(packed, mark), ((0, 0), (0, -packed.shape[1] % 128)))
    packed = lax.all_to_all(
        packed.reshape(devices, -1, 128), every, split_axis=0, concat_axis=0, tiled=True
    )
    sums = jnp.sum(packed, axis=0).reshape(-1)
    out, at = [], 0
    for size in lengths:
        out.append(sums[at : at + size])
        at += size
    return out


def norm_backward(grad_out, grads, gain, unit, stat):
    unit_grad = grads * gain
    return grad_out + stat * (unit_grad - unit * jnp.mean(unit_grad * unit, axis=-1, keepdims=True))


def halves_of(array, axis, which):
    size = array.shape[axis] // 2
    return lax.dynamic_slice_in_dim(array, which * size, size, axis)


def entry(array, which):
    return lax.dynamic_index_in_dim(array, which, 0, keepdims=False)


def shards_by_heads(
    tokens,
    cotangent,
    segments,
    expert_ids,
    slot_order,
    gate_weights,
    qkv_weight,
    qkv_bias,
    out_weight,
    norm_attn,
    norm_ffn,
    shared_gate_up,
    shared_down,
    shared_gate,
    expert_gate_up,
    expert_down,
):
    count = lax.axis_size(group)
    core = lax.axis_index("context")
    place = lax.axis_index("dp")
    index = lax.axis_index(group)
    tok_count, width = tokens.shape[1:]
    pairs = tok_count * expert_ids.shape[2]
    experts = expert_gate_up.shape[0] * lax.axis_size("expert")
    capacity = (9 * pairs + 8 * experts - 1) // (8 * experts)
    length = count * tok_count
    core_at = jnp.stack([core, lax.axis_index("expert")]).astype(jnp.int32)
    vectors = [norm_attn, norm_ffn, shared_gate, qkv_bias]
    lengths = [vector.shape[0] for vector in vectors]
    own_tokens = tokens[0]
    resid_in = own_tokens.astype(floats)

    cut = head_cut(qkv_weight, out_weight, vectors)
    all_tokens = lax.all_gather(after(own_tokens, cut), group, axis=0, tiled=True)
    cut_x, cut_y = near_blocks(cut)
    eu_both = both_cores(entry(expert_gate_up, core), entry(expert_gate_up, 1 - core))
    half = count // 2
    cut_far = (
        dp_step(after(cut_x[:half], eu_both), 2),
        dp_step(after(cut_y[half:], eu_both), 1),
    )
    blocks = [cut, cut_x, cut_y, *cut_far]
    places = [place, place ^ 1, place ^ 2, place ^ 3, place ^ 3]
    gain_attn, gain_ffn, gate_vector, bias = head_vectors(blocks, places)
    expert_up = gather_rows(eu_both)
    grads_mine = line_gather(after(cotangent[0], cut))
    routes = routing_of(expert_ids, slot_order, gate_weights, count, cut)
    rank, kept, gate = slots_of(routes, index, capacity)
    slot = further_on(jnp.where(kept, rank, -1).reshape(-1, 2, tok_count))
    slot = slot + jnp.where(slot < 0, 0, jnp.arange(2, dtype=jnp.int32)[:, None] * capacity)
    gate = further_on(gate.reshape(-1, 2, tok_count))
    all_tokens = after(all_tokens, slot, gate)

    piece = width // count
    positions = jnp.arange(length, dtype=jnp.int32)
    cosine, sine = rope_tables(positions, HEAD_DIM // 2)
    cosine = jnp.concatenate([cosine, cosine], axis=-1)
    sine = jnp.concatenate([-sine, sine], axis=-1)
    seg_row = segments.astype(jnp.int32)
    seg_col = seg_row.reshape(length, 1)
    own_bias = lax.dynamic_index_in_dim(bias.reshape(3, count, piece), index, 1, keepdims=False)
    weight, out_rows, normed, query, key, value, lse, attended, mine, other = attention_forward(
        core_at,
        jnp.stack(places).astype(jnp.int32),
        all_tokens,
        gain_attn.reshape(1, width),
        blocks,
        own_bias.reshape(1, 3 * piece),
        cosine,
        sine,
        seg_col,
        seg_row,
    )

    ed_first = after(entry(expert_down, core), *cut_far)
    ed_second = after(other_core(entry(expert_down, 1 - core)), *cut_far)
    ed_first_x, ed_first_y = near_blocks(ed_first)
    ed_second_x, ed_second_y = near_blocks(ed_second)
    other = other_core(after(other, grads_mine))
    mixed = line_sum(mine, other, ed_first_x, ed_first_y, ed_second_x, ed_second_y)
    ed_first_far, ed_second_far = dp_step(ed_first_x, 2), dp_step(ed_second_y, 1)
    units = shared_down.shape[0] // 2
    sh_pack = pack_shared(core_at, shared_gate_up, shared_down)
    sh_both = both_cores(sh_pack[0], sh_pack[1])
    shared_weights = gather_rows(after(sh_both, attended))

    resid_mid = resid_in + mixed
    stat_ffn = lax.rsqrt(jnp.mean(resid_mid * resid_mid, axis=-1, keepdims=True) + eps_norm)
    unit_ffn = resid_mid * stat_ffn
    normed_ffn = (unit_ffn * gain_ffn).astype(halves)
    grad_out = cotangent[0].astype(floats)
    all_grads = (grads_mine, other_core(after(grads_mine, mine)))
    normed_mine = line_gather(normed_ffn, ed_first_far, ed_second_far, all_grads[1])
    all_normed = (normed_mine, other_core(normed_mine))

    slot_in, slot_grad, hidden, pre_grad, expert_out, expert_grad = expert_pass(
        slot.reshape(count // 2, 1, 2 * tok_count),
        gate.reshape(count // 2, 1, 2 * tok_count),
        all_normed,
        all_grads,
        expert_up,
        [ed_first, ed_first_x, ed_first_y, ed_first_far]
        + [ed_second, ed_second_x, ed_second_y, ed_second_far],
        jnp.stack(
            [4 * which + (place ^ step) for which in (core, 1 - core) for step in range(4)]
        ).astype(jnp.int32),
        2 * capacity,
    )
    eu_term = weight_grad([slot_in], pre_grad)
    ed_term = weight_grad([hidden], slot_grad)
    ffn_mine, ffn_other, out_mine, out_other, sh_pre_grad, sh_hidden, sh_grad, logit_part = shared_pass(
        slot.reshape(length, 1),
        gate.reshape(length, 1),
        (after(all_normed[0], eu_term, ed_term), all_normed[1]),
        all_grads,
        shared_weights,
        gate_vector.reshape(1, width),
        expert_out,
        expert_grad,
    )
    wide = shared_weights.shape[1]
    sh_term = weight_grad(all_normed, sh_pre_grad, None, 0, wide)
    sh_term = weight_grad([sh_grad], sh_hidden, sh_term, sh_pre_grad.shape[1], wide)
    eu_sum, sh_sum = sum_weight(eu_term), sum_weight(sh_term)

    ffn_other = other_core(ffn_other)
    ffn_grad = line_sum(ffn_mine, ffn_other)
    logit_part = further_on(logit_part.reshape(-1, 2, tok_count), True)
    logit_sums = lax.all_to_all(
        after(logit_part.reshape(count, 1, tok_count), ffn_other),
        group,
        split_axis=0,
        concat_axis=0,
        tiled=True,
    )
    own_gate = jax.nn.sigmoid(
        jnp.sum(normed_ffn.astype(floats) * gate_vector, axis=-1, keepdims=True)
    )
    logit_grad = jnp.sum(logit_sums, axis=0).reshape(tok_count, 1) * own_gate * (1.0 - own_gate)
    ffn_grad = ffn_grad + logit_grad * gate_vector
    gain_ffn_part = jnp.sum(ffn_grad * unit_ffn, axis=0)
    gate_vector_part = jnp.sum(logit_grad * normed_ffn.astype(floats), axis=0)
    mid_grad = norm_backward(grad_out, ffn_grad, gain_ffn, unit_ffn, stat_ffn)
    mid_low = after(mid_grad.astype(halves), sh_term)

    out_got = other_core(out_other)
    mid_mine = line_gather(mid_low, eu_sum, out_got)
    mid_other = other_core(mid_mine)
    proj_grad, mine, other, gain_attn_part, bias_part, out_part = attention_backward(
        core_at, mid_mine, mid_other, all_tokens, weight, cosine, sine, seg_col, seg_row, out_rows,
        query, key, value, lse, attended,
    )
    layer_sum = line_sum(out_mine, after(out_got, mid_mine))
    other = other_core(after(other, layer_sum))
    attn_in_grad = line_sum(mine, other)
    rows = other
    weight_part = weight_grad([normed], proj_grad).reshape(count, -1, 3 * piece)
    out_part = out_part.reshape(-1, count, piece).transpose(1, 0, 2)
    total = lax.psum_scatter(
        jnp.concatenate([weight_part, out_part], axis=-1), "dp", scatter_dimension=1, tiled=True
    )
    ed_sum = sum_weight(after(ed_term, sh_term))
    qkv_total = lax.all_to_all(
        after(total[..., : 3 * piece], attn_in_grad), group, split_axis=0, concat_axis=0, tiled=True
    )
    each = qkv_weight.shape[0]
    qkv_out = (
        qkv_total.reshape(count, each, 3, piece)
        .transpose(1, 2, 0, 3)
        .reshape(each, 3 * width)
        .astype(floats)
    )
    out_weight_out = total[..., 3 * piece :].transpose(1, 0, 2).reshape(each, width).astype(floats)
    bias_part = lax.dynamic_update_slice(
        jnp.zeros((3, count, piece), floats), bias_part.reshape(3, 1, piece), (0, index, 0)
    ).reshape(-1)
    layer_sum = resid_mid + layer_sum
    stat_attn = lax.rsqrt(jnp.mean(resid_in * resid_in, axis=-1, keepdims=True) + eps_norm)
    unit_attn = resid_in * stat_attn
    input_grad = norm_backward(mid_grad, attn_in_grad, gain_attn, unit_attn, stat_attn)

    eu_sum, sh_sum, ed_sum = (after(total, rows) for total in (eu_sum, sh_sum, ed_sum))
    got = other_core(entry(sh_sum, 1 - core))
    shared_up_out, shared_down_out = unpack_shared(core_at, sh_sum, got, units)
    gain_attn_out, gain_ffn_out, gate_vector_out, bias_out = small_sums(
        [gain_attn_part, gain_ffn_part, gate_vector_part, bias_part], lengths, attn_in_grad
    )
    return (
        layer_sum.astype(halves)[None],
        input_grad[None],
        qkv_out,
        bias_out,
        out_weight_out,
        gain_attn_out,
        gain_ffn_out,
        shared_up_out,
        shared_down_out,
        gate_vector_out,
        jnp.stack(cores_in_order(eu_sum)).astype(floats),
        jnp.stack(cores_in_order(ed_sum)).astype(floats),
    )


def shards_by_rows(
    tokens,
    cotangent,
    segments,
    expert_ids,
    slot_order,
    gate_weights,
    qkv_weight,
    qkv_bias,
    out_weight,
    norm_attn,
    norm_ffn,
    shared_gate_up,
    shared_down,
    shared_gate,
    expert_gate_up,
    expert_down,
):
    count = lax.axis_size(group)
    core = lax.axis_index("context")
    index = lax.axis_index(group)
    tok_count, width = tokens.shape[1:]
    pairs = tok_count * expert_ids.shape[2]
    experts = expert_gate_up.shape[0] * lax.axis_size("expert")
    capacity = (9 * pairs + 8 * experts - 1) // (8 * experts)
    length = count * tok_count
    vectors = [norm_attn, norm_ffn, shared_gate, qkv_bias]
    lengths = [vector.shape[0] for vector in vectors]
    payload = jnp.concatenate([vector.astype(floats) for vector in vectors])
    small = spread(jnp.pad(payload, (0, -payload.shape[0] % 128)))
    gathered = []
    for at, size in enumerate(lengths):
        first = sum(lengths[:at])
        gathered.append(small[:, first : first + size].reshape(-1))
    gain_attn, gain_ffn, gate_vector, bias = gathered
    routes = routing_of(expert_ids, slot_order, gate_weights, count, small)

    resid_in = tokens[0].astype(floats)
    weights = rows_weights(qkv_weight, out_weight)
    mixed, saved = rows_forward(tokens[0], gain_attn, bias, weights, segments[0])

    def gate_up_half(which):
        part = halves_of(shared_gate_up, 2, which)
        return jnp.concatenate([part[0], part[1]], axis=-1)

    def down_half(which):
        return halves_of(shared_down, 0, which).T

    expert_up = gather_rows(both_cores(entry(expert_gate_up, core), entry(expert_gate_up, 1 - core)))
    expert_dn = gather_rows(both_cores(entry(expert_down, core), entry(expert_down, 1 - core)))
    shared_up = gather_rows(both_cores(gate_up_half(core), gate_up_half(1 - core)))
    shared_dn = gather_rows(both_cores(down_half(core), down_half(1 - core)))
    ff_width = expert_dn.shape[0]
    units = shared_dn.shape[1]

    resid_mid = resid_in + mixed
    stat_ffn = lax.rsqrt(jnp.mean(resid_mid * resid_mid, axis=-1, keepdims=True) + eps_norm)
    unit_ffn = resid_mid * stat_ffn
    normed_ffn = (unit_ffn * gain_ffn).astype(halves)
    grad_out = cotangent[0].astype(floats)
    all_grads = gather_cores(gather_line(cotangent[0]))
    all_normed = gather_cores(gather_line(normed_ffn))

    rank, kept, gate = slots_of(routes, index, capacity)
    slots = jnp.arange(capacity, dtype=jnp.int32)
    select = (rank[:, None, :] == slots[None, :, None]) & kept[:, None, :]
    slot_gate = jnp.sum(jnp.where(select, gate[:, None, :], 0.0), axis=-1).reshape(-1, 1)
    select = select.astype(halves)

    def to_slots(rows):
        rows = rows.reshape(count, tok_count, width)
        got = jnp.einsum("brt,btd->brd", select, rows, preferred_element_type=floats)
        return got.reshape(count * capacity, width)

    def from_slots(rows):
        rows = rows.reshape(count, capacity, width)
        got = jnp.einsum("brt,brd->btd", select, rows, preferred_element_type=floats)
        return got.reshape(length, width)

    slot_in = to_slots(all_normed).astype(halves)
    slot_grad = (to_slots(all_grads) * slot_gate).astype(halves)
    expert_pre = dot(slot_in, expert_up)
    expert_g, expert_u = expert_pre[:, :ff_width], expert_pre[:, ff_width:]
    expert_hidden = (jax.nn.silu(expert_g) * expert_u).astype(halves)
    hidden_grad = dot_nt(slot_grad, expert_dn)
    expert_pre_grad = jnp.concatenate(
        silu_parts(hidden_grad, expert_g, expert_u), axis=-1
    ).astype(halves)
    expert_out = dot(expert_hidden, expert_dn).astype(halves)
    slot_in_grad = dot_nt(expert_pre_grad, expert_up).astype(halves)
    eu_sum = sum_weight(dot_tn(slot_in, expert_pre_grad).astype(halves))
    ed_sum = sum_weight(dot_tn(expert_hidden, slot_grad).astype(halves))

    shared_pre = dot(all_normed, shared_up)
    shared_g, shared_u = shared_pre[:, :units], shared_pre[:, units:]
    shared_hidden = (jax.nn.silu(shared_g) * shared_u).astype(halves)
    gate_shared = jax.nn.sigmoid(
        jnp.sum(all_normed.astype(floats) * gate_vector, axis=-1, keepdims=True)
    )
    shared_grad = (gate_shared * all_grads.astype(floats)).astype(halves)
    hidden_grad = dot(shared_grad, shared_dn)
    shared_pre_grad = jnp.concatenate(
        silu_parts(hidden_grad, shared_g, shared_u), axis=-1
    ).astype(halves)
    shared_part = dot_nt(shared_hidden, shared_dn)
    logit_part = jnp.sum(all_grads.astype(floats) * shared_part, axis=-1)
    su_sum = sum_weight(dot_tn(all_normed, shared_pre_grad).astype(halves))
    sd_sum = sum_weight(dot_tn(shared_grad, shared_hidden).astype(halves))
    ffn_part = dot_nt(shared_pre_grad, shared_up) + from_slots(slot_in_grad)
    out_part = gate_shared * shared_part + gate.reshape(length, 1) * from_slots(expert_out)

    logit_sums = lax.all_to_all(
        logit_part.reshape(count, 1, tok_count), group, split_axis=0, concat_axis=0, tiled=True
    )
    own_gate = jax.nn.sigmoid(
        jnp.sum(normed_ffn.astype(floats) * gate_vector, axis=-1, keepdims=True)
    )
    logit_grad = jnp.sum(logit_sums, axis=0).reshape(tok_count, 1) * own_gate * (1.0 - own_gate)

    def own_sum(part):
        part = part.reshape(-1, 2, tok_count, width)
        mine = lax.dynamic_index_in_dim(part, core, 1, keepdims=False)
        other = lax.dynamic_index_in_dim(part, 1 - core, 1, keepdims=False)
        return group_sum(mine, other.astype(halves))

    layer_sum = resid_mid + own_sum(out_part)
    ffn_grad = own_sum(ffn_part) + logit_grad * gate_vector
    gain_ffn_part = jnp.sum(ffn_grad * unit_ffn, axis=0)
    gate_vector_part = jnp.sum(logit_grad * normed_ffn.astype(floats), axis=0)
    mid_grad = norm_backward(grad_out, ffn_grad, gain_ffn, unit_ffn, stat_ffn)
    mid_low = mid_grad.astype(halves)

    attn_in_grad, gain_attn_part, bias_part, qkv_out, out_weight_out = rows_backward(
        weights, saved, mid_low
    )
    stat_attn = lax.rsqrt(jnp.mean(resid_in * resid_in, axis=-1, keepdims=True) + eps_norm)
    unit_attn = resid_in * stat_attn
    input_grad = norm_backward(mid_grad, attn_in_grad, gain_attn, unit_attn, stat_attn)
    shared_up_out = jnp.concatenate(
        [
            array.reshape(-1, 2, units).transpose(1, 0, 2) for array in cores_in_order(su_sum)
        ],
        axis=-1,
    )
    gain_attn_out, gain_ffn_out, gate_vector_out, bias_out = small_sums(
        [gain_attn_part, gain_ffn_part, gate_vector_part, bias_part], lengths, attn_in_grad
    )
    return (
        layer_sum.astype(halves)[None],
        input_grad[None],
        qkv_out,
        bias_out,
        out_weight_out,
        gain_attn_out,
        gain_ffn_out,
        shared_up_out.astype(floats),
        jnp.concatenate(cores_in_order(sd_sum), axis=-1).T.astype(floats),
        gate_vector_out,
        jnp.stack(cores_in_order(eu_sum)).astype(floats),
        jnp.stack(cores_in_order(ed_sum)).astype(floats),
    )


def shards(*arrays):
    if HEADS % lax.axis_size(group) == 0 and lax.axis_size("dp") == 4 and lax.axis_size("expert") == 4:
        return shards_by_heads(*arrays)
    return shards_by_rows(*arrays)


def solution(mesh):
    placed = (
        P("dp", ("expert", "context"), None),
        P("dp", ("expert", "context"), None),
        P("dp", None),
        P("dp", ("expert", "context"), None),
        P("dp", ("expert", "context"), None),
        P("dp", ("expert", "context"), None),
        P(("expert", "context", "dp"), None),
        P(("expert", "context", "dp")),
        P(("expert", "context", "dp"), None),
        P(("expert", "context", "dp")),
        P(("expert", "context", "dp")),
        P(None, ("context", "dp"), "expert"),
        P("expert", ("context", "dp")),
        P(("expert", "context", "dp")),
        P("expert", ("context", "dp"), None),
        P("expert", ("context", "dp"), None),
    )
    return jax.shard_map(
        shards,
        mesh=mesh,
        in_specs=placed,
        out_specs=(
            P("dp", ("expert", "context"), None),
            P("dp", ("expert", "context"), None),
            P(("expert", "context", "dp"), None),
            P(("expert", "context", "dp")),
            P(("expert", "context", "dp"), None),
            P(("expert", "context", "dp")),
            P(("expert", "context", "dp")),
            P(None, ("context", "dp"), "expert"),
            P("expert", ("context", "dp")),
            P(("expert", "context", "dp")),
            P("expert", ("context", "dp"), None),
            P("expert", ("context", "dp"), None),
        ),
        check_vma=False,
    )
```

```python
import math

import jax
import jax.numpy as jnp
import numpy as np
from jax import lax
from jax.experimental import pallas as pl
from jax.experimental.pallas import tpu as pltpu
from jax.sharding import PartitionSpec as P

HEADS = 16
HEAD_DIM = 128


eps_norm = 1e-06
neg_fill = -1e30
rope_base = 1000000.0
group_heads = 4
floats = jnp.float32
halves = jnp.bfloat16
every = ("expert", "context", "dp")
group = ("expert", "context")
cost_scale = 0.0


def rope_tables(positions, half):
    inverse = jnp.exp(
        jnp.arange(half).astype(jnp.float32) * (-2.0 * math.log(rope_base) / (2 * half))
    )
    angle = positions.astype(jnp.float32)[:, None] * inverse[None, :]
    return (jnp.cos(angle), jnp.sin(angle))


def rotate(values, cosine, sine):
    half = values.shape[-1] // 2
    front = values[..., :half]
    behind = values[..., half:]
    cosine = cosine[:, None, :]
    sine = sine[:, None, :]
    return jnp.concatenate(
        [front * cosine - behind * sine, behind * cosine + front * sine], axis=-1
    )


def rotate_back(grads, cosine, sine):
    half = grads.shape[-1] // 2
    front = grads[..., :half]
    behind = grads[..., half:]
    cosine = cosine[:, None, :]
    sine = sine[:, None, :]
    return jnp.concatenate(
        [front * cosine + behind * sine, behind * cosine - front * sine], axis=-1
    )


def silu_parts(grad_hidden, gate_pre, up_pre):
    sigma = jax.nn.sigmoid(gate_pre)
    gate_grad = grad_hidden * up_pre * sigma * (1.0 + gate_pre * (1.0 - sigma))
    up_grad = grad_hidden * gate_pre * sigma
    return (gate_grad, up_grad)


def dot(left, right):
    return jnp.dot(left, right, preferred_element_type=floats)


def dot_tn(left, right):
    return lax.dot_general(left, right, (((0,), (0,)), ((), ())), preferred_element_type=floats)


def dot_nt(left, right):
    return lax.dot_general(left, right, (((1,), (1,)), ((), ())), preferred_element_type=floats)


def dp_step(value, step):
    count = lax.axis_size("dp")
    return lax.ppermute(value, "dp", [(i, i ^ step) for i in range(count)])


def other_core(value):
    return lax.ppermute(value, "context", [(0, 1), (1, 0)])


def after(value, *others):
    return lax.optimization_barrier((value,) + others)[0]


def near_blocks(block):
    return dp_step(block, 1), dp_step(block, 2)


def place_blocks(pieces, places, out_shape, views, window):
    at, size = window

    count = len(pieces)

    def kernel(place_ref, *refs):
        blocks, out, held = refs[:count], refs[count], refs[count + 1 : 2 * count + 1]
        in_sems, out_sems = refs[2 * count + 1 :]
        loads = [
            pltpu.make_async_copy(blocks[i].at[..., pl.ds(at, size)], held[i], in_sems.at[i])
            for i in range(count)
        ]
        stores = [
            pltpu.make_async_copy(held[i], views[i](out, place_ref[i]), out_sems.at[i])
            for i in range(count)
        ]
        for load in loads:
            load.start()
        for load, store in zip(loads, stores):
            load.wait()
            store.start()
        for store in stores:
            store.wait()

    return pl.pallas_call(
        kernel,
        out_shape=jax.ShapeDtypeStruct(out_shape, pieces[0].dtype),
        in_specs=[pl.BlockSpec(memory_space=pltpu.SMEM)]
        + [pl.BlockSpec(memory_space=pl.ANY)] * len(pieces),
        out_specs=pl.BlockSpec(memory_space=pl.ANY),
        scratch_shapes=[pltpu.VMEM(piece.shape[:-1] + (size,), piece.dtype) for piece in pieces]
        + [
            pltpu.SemaphoreType.DMA((count,)),
            pltpu.SemaphoreType.DMA((count,)),
        ],
        compiler_params=pltpu.CompilerParams(vmem_limit_bytes=32 * 1024 * 1024),
        cost_estimate=pl.CostEstimate(
            flops=0, bytes_accessed=1024, transcendentals=0
        ),
    )(jnp.stack(places).astype(jnp.int32), *pieces)


def sum_weight(part):
    rows, wide = part.shape
    return lax.psum_scatter(
        part.reshape(2, rows // 2, wide), "dp", scatter_dimension=1, tiled=True
    )


def both_cores(kept, given):
    core = lax.axis_index("context")
    taken = other_core(given)
    return jnp.stack([jnp.where(core == 0, kept, taken), jnp.where(core == 0, taken, kept)])


def gather_rows(both):
    out = lax.all_gather(both, "dp", axis=1, tiled=True)
    return out.reshape(-1, both.shape[2])


def cores_in_order(blocks):
    core = lax.axis_index("context")
    mine = jnp.where(core == 0, blocks[0], blocks[1])
    other = other_core(jnp.where(core == 0, blocks[1], blocks[0]))
    return jnp.where(core == 0, mine, other), jnp.where(core == 0, other, mine)


def along_expert(blocks):
    return lax.all_to_all(blocks, "expert", split_axis=0, concat_axis=0, tiled=True)


def gather_line(block):
    return along_expert(jnp.broadcast_to(block[None], (lax.axis_size("expert"),) + block.shape))


def gather_cores(mine):
    core = lax.axis_index("context")
    other = other_core(mine)
    both = jnp.stack([jnp.where(core == 0, mine, other), jnp.where(core == 0, other, mine)], axis=1)
    return both.reshape((-1,) + mine.shape[2:])


def group_sum(mine, other):
    rows = (mine.astype(floats) + other_core(other).astype(floats)).astype(halves)
    return jnp.sum(along_expert(rows).astype(floats), axis=0)


def along_line(value, step):
    count = lax.axis_size("expert")
    return lax.ppermute(value, "expert", [(i, (i + step) % count) for i in range(count)])


def line_blocks(block):
    count = lax.axis_size("expert")
    return [block] + [along_line(block, count - k) for k in range(1, count)]


def line_gather(block, *pins):
    got = line_blocks(block)
    got[-1] = after(got[-1], *pins)
    return jnp.stack(got)


def line_sum(mine, other, *pins):
    rows = [
        (mine[k].astype(floats) + other[k].astype(floats)).astype(halves)
        for k in range(mine.shape[0])
    ]
    got = [along_line(row, k) for k, row in enumerate(rows) if k > 0]
    if pins:
        got[-1] = after(got[-1], *pins)
    total = rows[0].astype(floats)
    for row in got:
        total = total + row.astype(floats)
    return total


def further_on(array, back=False):
    here = lax.axis_index("expert")
    count = array.shape[0]
    array = jnp.where(lax.axis_index("context") == 0, array, array[:, ::-1])
    start = lax.rem(count - here, count) if back else here
    return lax.dynamic_slice_in_dim(jnp.concatenate([array, array]), start, count, 0)


def spread(values):
    count = lax.axis_size(every)
    padded = jnp.broadcast_to(values.reshape(1, -1, 128), (count, values.shape[0] // 128, 128))
    got = lax.all_to_all(padded, every, split_axis=0, concat_axis=0, tiled=True)
    return got.reshape(count, -1)


def kernel_call(kernel, out_shapes, in_specs, out_specs, flops, grid=None, scratch=(), aliases=None):
    extra = {} if grid is None else {"grid": grid}
    return pl.pallas_call(
        kernel,
        out_shape=out_shapes,
        in_specs=in_specs,
        out_specs=out_specs,
        scratch_shapes=list(scratch),
        input_output_aliases=aliases or {},
        compiler_params=pltpu.CompilerParams(vmem_limit_bytes=58 * 1024 * 1024),
        cost_estimate=pl.CostEstimate(
            flops=int(flops * cost_scale), bytes_accessed=1024, transcendentals=0
        ),
        **extra,
    )


def kdot(left, right, dims):
    return lax.dot_general(left, right, (dims, ((), ())), preferred_element_type=floats)


nn = ((1,), (0,))
nt = ((1,), (1,))
tn = ((0,), (0,))


def ordered(core, first, second):
    return jnp.where(core == 0, first, second), jnp.where(core == 0, second, first)


def unpack_shared(core, sums, got, units):
    rows, wide = got.shape
    full = wide // 3
    cut = 2 * full - units

    def kernel(core_ref, sums_ref, got_ref, up_out, down_out):
        low, high = ordered(core_ref[0], sums_ref[core_ref[0]], got_ref[...])
        for at in range(2):
            up_out[at, :, :full] = low[:, at * full : (at + 1) * full].astype(floats)
            up_out[at, :, full:] = high[:, at * full + cut : (at + 1) * full].astype(floats)
        down_out[:full, :] = low[:, 2 * full :].astype(floats).T
        down_out[full:, :] = high[:, 2 * full :].astype(floats).T[cut:]

    vmem = pl.BlockSpec(memory_space=pltpu.VMEM)
    shape = jax.ShapeDtypeStruct
    return kernel_call(
        kernel,
        (shape((2, rows, units), floats), shape((units, rows), floats)),
        [pl.BlockSpec(memory_space=pltpu.SMEM), vmem, vmem],
        (vmem, vmem),
        0,
    )(core, sums, got)


def slot_table(place, routing, capacity):
    blocks, lines, tokens = routing.shape
    choices = lines // 6
    pairs = blocks // 2

    def kernel(place_ref, routing_ref, slot_row, gate_row, slot_col, gate_col, slots, gates):
        expert = place_ref[2].astype(floats)
        has = jnp.zeros((blocks, tokens), floats)
        order = jnp.zeros((blocks, tokens), floats)
        gate = jnp.zeros((blocks, tokens), floats)
        for k in range(choices):
            parts = [routing_ref[:, at * choices + k, :] for at in range(6)]
            chosen = parts[0] == expert
            has = jnp.where(chosen, 1.0, has)
            order = jnp.where(chosen, parts[1] * 16.0 + parts[2], order)
            gate = jnp.where(chosen, (parts[3] + parts[4]) + parts[5], gate)
        none = has == 0.0
        order = jnp.where(none, 1e9, order)
        turned = order.T
        for b in range(blocks):
            earlier = turned[:, b : b + 1] < order[b : b + 1, :]
            rank = jnp.sum(jnp.where(earlier, 1.0, 0.0), axis=0, keepdims=True)
            kept = (rank < capacity) & (has[b : b + 1, :] > 0.0)
            slots[b : b + 1, :] = jnp.where(kept, rank, -1.0)
            gates[b : b + 1, :] = jnp.where(kept, gate[b : b + 1, :], 0.0)
        for p in range(pairs):
            span = lax.rem(place_ref[1] + p, pairs)
            for at in range(2):
                row = 2 * span + lax.rem(place_ref[0] + at, 2)
                slot = slots[pl.ds(row, 1), :]
                slot = jnp.where(slot < 0.0, slot, slot + at * capacity)
                columns = slice(at * tokens, (at + 1) * tokens)
                slot_row[p, :, columns] = slot.astype(jnp.int32)
                gate_row[p, :, columns] = gates[pl.ds(row, 1), :]
                lines = slice((2 * p + at) * tokens, (2 * p + at + 1) * tokens)
                wide = jnp.broadcast_to(slot, (8, tokens)).T
                slot_col[lines, :] = wide[:, :1].astype(jnp.int32)
                wide = jnp.broadcast_to(gates[pl.ds(row, 1), :], (8, tokens)).T
                gate_col[lines, :] = wide[:, :1]

    vmem = pl.BlockSpec(memory_space=pltpu.VMEM)
    shape = jax.ShapeDtypeStruct
    return kernel_call(
        kernel,
        (
            shape((pairs, 1, 2 * tokens), jnp.int32),
            shape((pairs, 1, 2 * tokens), floats),
            shape((blocks * tokens, 1), jnp.int32),
            shape((blocks * tokens, 1), floats),
        ),
        [pl.BlockSpec(memory_space=pltpu.SMEM), vmem],
        (vmem,) * 4,
        0,
        scratch=[pltpu.VMEM((blocks, tokens), floats), pltpu.VMEM((blocks, tokens), floats)],
    )(place, routing)


def attention_project(places, tokens, gain, blocks, bias, cosine, sine):
    length, width = tokens.shape
    count, rows_each, wide = blocks[0].shape
    piece = (wide - 128) // 4
    half = count // 2
    spans = [(0, count)] * 3 + [(0, half), (half, count)]
    heads = piece // HEAD_DIM
    scale = 1.0 / math.sqrt(HEAD_DIM)
    tile = 256

    def kernel(
        place_ref, tok, gain_ref, bias_ref, cos_ref, sin_ref, *refs
    ):
        pieces, refs = refs[:5], refs[5:]
        w, wout, normed, query, key, value, sems = refs
        copies = []
        for i, (first, last) in enumerate(spans):
            for g in range(first, last):
                row = pl.multiple_of((g * 4 + place_ref[i]) * rows_each, rows_each)
                copies.append(
                    pltpu.make_async_copy(
                        pieces[i].at[g - first, :, pl.ds(0, 3 * piece)],
                        w.at[pl.ds(row, rows_each)],
                        sems.at[len(copies)],
                    )
                )
                row = pl.multiple_of(place_ref[i] * rows_each, rows_each)
                copies.append(
                    pltpu.make_async_copy(
                        pieces[i].at[g - first, :, pl.ds(3 * piece + 128, piece)],
                        wout.at[pl.ds(row, rows_each), pl.ds(g * piece, piece)],
                        sems.at[len(copies)],
                    )
                )
        for copy in copies:
            copy.start()
        for copy in copies:
            copy.wait()
        for t in range(length // tile):
            rows = pl.ds(t * tile, tile)
            x = tok[rows, :].astype(floats)
            stat = lax.rsqrt(jnp.mean(x * x, axis=-1, keepdims=True) + eps_norm)
            low = (x * stat * gain_ref[...]).astype(halves)
            normed[rows, :] = low
            proj = kdot(low, w[...], nn) + bias_ref[...]
            c, s = cos_ref[rows, :], sin_ref[rows, :]
            for h in range(heads):
                at = slice(h * HEAD_DIM, (h + 1) * HEAD_DIM)
                q = proj[:, at]
                query[rows, at] = ((q * c + pltpu.roll(q, 64, 1) * s) * scale).astype(halves)
                k = proj[:, piece + h * HEAD_DIM : piece + (h + 1) * HEAD_DIM]
                key[rows, at] = (k * c + pltpu.roll(k, 64, 1) * s).astype(halves)
            value[rows, :] = proj[:, 2 * piece :].astype(halves)

    vmem = pl.BlockSpec(memory_space=pltpu.VMEM)
    shape = jax.ShapeDtypeStruct
    return kernel_call(
        kernel,
        (
            shape((width, 3 * piece), halves),
            shape((piece, width), halves),
            shape((length, width), halves),
            shape((length, piece), halves),
            shape((length, piece), halves),
            shape((length, piece), halves),
        ),
        [pl.BlockSpec(memory_space=pltpu.SMEM)]
        + [vmem] * 5
        + [pl.BlockSpec(memory_space=pl.ANY)] * 5,
        (vmem,) * 6,
        0,
        scratch=[pltpu.SemaphoreType.DMA((8 * count,))],
    )(places, tokens, gain, bias, cosine, sine, *blocks)


def attention_mix(core, query, key, value, seg_col, seg_row, out_rows):
    length, piece = query.shape
    width = out_rows.shape[1]
    heads = piece // HEAD_DIM
    tile = 256

    def kernel(core_ref, query, key, value, segc, segr, wout, lse, attended, mine, other):
        for t in range(length // tile):
            rows = pl.ds(t * tile, tile)
            seen = (t + 1) * tile
            place = lax.broadcasted_iota(jnp.int32, (tile, seen), 0) + t * tile
            visible = (lax.broadcasted_iota(jnp.int32, (tile, seen), 1) <= place) & (
                segc[rows, :] == segr[:, :seen]
            )
            for h in range(heads):
                at = slice(h * HEAD_DIM, (h + 1) * HEAD_DIM)
                scores = kdot(query[rows, at], key[:seen, at], nt)
                scores = jnp.where(visible, scores, neg_fill)
                top = jnp.max(scores, axis=-1, keepdims=True)
                grown = jnp.exp(scores - top)
                total = jnp.sum(grown, axis=-1, keepdims=True)
                probs = (grown / total).astype(halves)
                attended[rows, at] = kdot(probs, value[:seen, at], nn).astype(halves)
                lse[rows, h : h + 1] = top + jnp.log(total)
            mixed = kdot(attended[rows, :], wout[...], nn).astype(halves)
            k = lax.rem(t + 4 - core_ref[1], 4)
            mine[k], other[k] = ordered(core_ref[0], mixed[: tile // 2], mixed[tile // 2 :])

    vmem = pl.BlockSpec(memory_space=pltpu.VMEM)
    shape = jax.ShapeDtypeStruct
    return kernel_call(
        kernel,
        (
            shape((length, heads), floats),
            shape((length, piece), halves),
            shape((length // tile, tile // 2, width), halves),
            shape((length // tile, tile // 2, width), halves),
        ),
        [pl.BlockSpec(memory_space=pltpu.SMEM)] + [vmem] * 6,
        (vmem,) * 4,
        0,
    )(core, query, key, value, seg_col, seg_row, out_rows)


def attention_backward(
    core, mid_mine, mid_other, tokens, weight, cosine, sine, seg_col, seg_row, out_rows,
    query, key, value, lse, attended,
):
    length, width = tokens.shape
    piece = out_rows.shape[0]
    heads = piece // HEAD_DIM
    scale = 1.0 / math.sqrt(HEAD_DIM)
    tile = 256

    def kernel(
        core_ref, mid_m, mid_o, tok, w, cos_ref, sin_ref, segc, segr, wout, q_ref, k_ref, v_ref, lse_ref,
        att_ref, proj_grad, mine, other, gain_part, bias_part, out_part, key_grad, value_grad, out_grad,
    ):
        out_grad[...] = jnp.zeros_like(out_grad)
        key_grad[...] = jnp.zeros_like(key_grad)
        value_grad[...] = jnp.zeros_like(value_grad)
        for t in range(length // tile):
            rows = pl.ds(t * tile, tile)
            seen = (t + 1) * tile
            place = lax.broadcasted_iota(jnp.int32, (tile, seen), 0) + t * tile
            visible = (lax.broadcasted_iota(jnp.int32, (tile, seen), 1) <= place) & (
                segc[rows, :] == segr[:, :seen]
            )
            k = lax.rem(t + 4 - core_ref[1], 4)
            mid = jnp.concatenate(ordered(core_ref[0], mid_m[k], mid_o[k]))
            grad = kdot(mid, wout[...], nt).astype(halves)
            out_grad[...] += kdot(att_ref[rows, :], mid, tn)
            c, s = cos_ref[rows, :], sin_ref[rows, :]
            for h in range(heads):
                at = slice(h * HEAD_DIM, (h + 1) * HEAD_DIM)
                query = q_ref[rows, at]
                scores = kdot(query, k_ref[:seen, at], nt)
                probs = jnp.where(visible, jnp.exp(scores - lse_ref[rows, h : h + 1]), 0.0)
                prob_grad = kdot(grad[:, at], v_ref[:seen, at], nt)
                delta = jnp.sum(probs * prob_grad, axis=-1, keepdims=True)
                score_grad = (probs * (prob_grad - delta)).astype(halves)
                q_grad = kdot(score_grad, k_ref[:seen, at], nn) * scale
                proj_grad[rows, at] = (q_grad * c - pltpu.roll(q_grad, 64, 1) * s).astype(halves)
                key_grad[:seen, at] += kdot(score_grad, query, tn)
                value_grad[:seen, at] += kdot(probs.astype(halves), grad[:, at], tn)
        gains = jnp.zeros((1, width), floats)
        biases = jnp.zeros((1, 3 * piece), floats)
        for t in range(length // tile):
            rows = pl.ds(t * tile, tile)
            c, s = cos_ref[rows, :], sin_ref[rows, :]
            for h in range(heads):
                at = slice(h * HEAD_DIM, (h + 1) * HEAD_DIM)
                k_grad = key_grad[rows, at]
                proj_grad[rows, piece + h * HEAD_DIM : piece + (h + 1) * HEAD_DIM] = (
                    k_grad * c - pltpu.roll(k_grad, 64, 1) * s
                ).astype(halves)
            proj_grad[rows, 2 * piece :] = value_grad[rows, :].astype(halves)
            grads = proj_grad[rows, :]
            biases = biases + jnp.sum(grads.astype(floats), axis=0, keepdims=True)
            part = kdot(grads, w[...], nt)
            x = tok[rows, :].astype(floats)
            stat = lax.rsqrt(jnp.mean(x * x, axis=-1, keepdims=True) + eps_norm)
            gains = gains + jnp.sum(part * (x * stat), axis=0, keepdims=True)
            k = lax.rem(t + 4 - core_ref[1], 4)
            part = part.astype(halves)
            mine[k], other[k] = ordered(core_ref[0], part[: tile // 2], part[tile // 2 :])
        out_part[...] = out_grad[...].astype(halves)
        gain_part[...] = gains
        bias_part[...] = biases

    vmem = pl.BlockSpec(memory_space=pltpu.VMEM)
    shape = jax.ShapeDtypeStruct
    return kernel_call(
        kernel,
        (
            shape((length, 3 * piece), halves),
            shape((length // tile, tile // 2, width), halves),
            shape((length // tile, tile // 2, width), halves),
            shape((1, width), floats),
            shape((1, 3 * piece), floats),
            shape((piece, width), halves),
        ),
        [pl.BlockSpec(memory_space=pltpu.SMEM)] + [vmem] * 14,
        (vmem,) * 6,
        2 * length * width * 5 * piece + 2 * length * length * 5 * piece,
        scratch=[
            pltpu.VMEM((length, piece), floats),
            pltpu.VMEM((length, piece), floats),
            pltpu.VMEM((piece, width), floats),
        ],
    )(
        core, mid_mine, mid_other, tokens, weight, cosine, sine, seg_col, seg_row, out_rows,
        query, key, value, lse, attended,
    )


def expert_pass(slot_row, gate_row, rows_in, grads_in, up, downs, places, capacity):
    pairs, half, width = rows_in[0].shape
    rows_each = downs[0].shape[0]
    ff = rows_each * len(downs)
    pair = 2 * half
    count = pairs * capacity
    wide = 2 * ff
    chunk = 256
    chunks = wide // chunk

    def kernel(place_ref, slot_ref, gate_ref, x_mine, x_other, g_mine, g_other, up_hbm, *refs):
        downs_hbm, refs = refs[: len(downs)], refs[len(downs) :]
        out, in_grad, up_grad, down_grad, *refs = refs
        x, g, w_up, w_down, pre, slot_in, slot_grad, hidden, pre_grad, stage, result, *sems = refs
        row_sems, up_sems, down_sems, stage_sems, result_sems = sems
        row_loads = []
        for p in range(pairs):
            for i, (source, target) in enumerate(((x_mine, x), (x_other, x), (g_mine, g), (g_other, g))):
                rows = pl.ds(p * pair + (i % 2) * half, half)
                row_loads.append(
                    pltpu.make_async_copy(source.at[p], target.at[rows], row_sems.at[4 * p + i])
                )
        loads = [
            pltpu.make_async_copy(
                up_hbm.at[place_ref[len(downs)], pl.ds(j * chunk, chunk)],
                w_up.at[pl.ds(j * chunk, chunk)],
                up_sems.at[j],
            )
            for j in range(width // chunk)
        ]
        down_loads = [
            pltpu.make_async_copy(
                block,
                w_down.at[pl.ds(pl.multiple_of(place_ref[i] * rows_each, 16), rows_each)],
                down_sems.at[i],
            )
            for i, block in enumerate(downs_hbm)
        ]
        for load in row_loads + loads + down_loads:
            load.start()
        for p in range(pairs):
            for load in row_loads[4 * p : 4 * p + 4]:
                load.wait()
            rows = pl.ds(p * pair, pair)
            slots = pl.ds(p * capacity, capacity)
            picks = lax.broadcasted_iota(jnp.int32, (capacity, pair), 0) == slot_ref[p]
            pick = jnp.where(picks, 1.0, 0.0).astype(halves)
            gates = jnp.sum(jnp.where(picks, gate_ref[p], 0.0), axis=-1, keepdims=True)
            slot_in[slots, :] = kdot(pick, x[rows, :], nn).astype(halves)
            slot_grad[slots, :] = (kdot(pick, g[rows, :], nn) * gates).astype(halves)
        for load in loads:
            load.wait()
        for j in range(chunks):
            at = pl.ds(j * chunk, chunk)
            pre[:, at] = kdot(slot_in[...], w_up[:, at], nn)
        for load in down_loads:
            load.wait()
        start = 0
        while start < ff:
            size = min(chunk, ff - start)
            at = slice(start, start + size)
            up_at = slice(ff + start, ff + start + size)
            grad = kdot(slot_grad[...], w_down[at, :], nt)
            gate_pre, up_pre = pre[:, at], pre[:, up_at]
            sigma = jax.nn.sigmoid(gate_pre)
            act = gate_pre * sigma
            hidden[:, at] = (act * up_pre).astype(halves)
            pre_grad[:, at] = (grad * up_pre * sigma * (1.0 + gate_pre * (1.0 - sigma))).astype(halves)
            pre_grad[:, up_at] = (grad * act).astype(halves)
            start += size
        stores, results = [], []

        def store(value, buffers, sems, target, first):
            slot = len(stores) % 3
            if len(stores) > 2:
                stores[-3].wait()
            rows, columns = value.shape
            buffers[slot, :rows, :columns] = value.astype(halves)
            stores.append(
                pltpu.make_async_copy(
                    buffers.at[slot, pl.ds(0, rows), pl.ds(0, columns)],
                    target.at[pl.ds(first, rows)],
                    sems.at[slot],
                )
            )
            stores[-1].start()

        for j in range(width // chunk):
            at = pl.ds(j * chunk, chunk)
            store(kdot(slot_in[:, at], pre_grad[...], tn), stage, stage_sems, up_grad, j * chunk)
        start = 0
        while start < ff:
            size = min(chunk, ff - start)
            at = slice(start, start + size)
            store(kdot(hidden[:, at], slot_grad[...], tn), stage, stage_sems, down_grad, start)
            start += size
        for copy in stores[-3:]:
            copy.wait()
        for j in range(2):
            rows = pl.ds(j * (count // 2), count // 2)
            for i, target in enumerate((out, in_grad)):
                if i == 0:
                    value = kdot(hidden[rows, :], w_down[...], nn)
                else:
                    value = kdot(pre_grad[rows, :], w_up[...], nt)
                result[2 * j + i] = value.astype(halves)
                copy = pltpu.make_async_copy(
                    result.at[2 * j + i], target.at[rows], result_sems.at[2 * j + i]
                )
                copy.start()
                results.append(copy)
        for copy in results:
            copy.wait()

    vmem = pl.BlockSpec(memory_space=pltpu.VMEM)
    hbm = pl.BlockSpec(memory_space=pl.ANY)
    shape = jax.ShapeDtypeStruct
    dma = pltpu.SemaphoreType.DMA
    return kernel_call(
        kernel,
        (
            shape((count, width), halves),
            shape((count, width), halves),
            shape((width, wide), halves),
            shape((ff, width), halves),
        ),
        [pl.BlockSpec(memory_space=pltpu.SMEM)] + [vmem] * 2 + [hbm] * (5 + len(downs)),
        (hbm,) * 4,
        2 * count * width * ff * 9,
        scratch=[
            pltpu.VMEM((pairs * pair, width), halves),
            pltpu.VMEM((pairs * pair, width), halves),
            pltpu.VMEM((width, wide), halves),
            pltpu.VMEM((ff, width), halves),
            pltpu.VMEM((count, wide), floats),
            pltpu.VMEM((count, width), halves),
            pltpu.VMEM((count, width), halves),
            pltpu.VMEM((count, ff), halves),
            pltpu.VMEM((count, wide), halves),
            pltpu.VMEM((3, chunk, wide), halves),
            pltpu.VMEM((4, count // 2, width), halves),
            dma((4 * pairs,)),
            dma((width // chunk,)),
            dma((len(downs),)),
            dma((3,)),
            dma((4,)),
        ],
    )(places, slot_row, gate_row, *rows_in, *grads_in, up, *downs)


def shared_pass(core, slot_col, gate_col, rows_in, grads_in, up, down, vector, expert_out, expert_grad):
    pairs, half, width = rows_in[0].shape
    tile = 2 * half
    length = pairs * tile
    all_units = up.shape[2]
    units = (all_units // 2 + 127) // 128 * 128
    cut = 2 * units - all_units
    capacity = expert_out.shape[0] * tile // length

    def kernel(
        core_ref, slot_ref, gate_ref, x_mine, x_other, g_mine, g_other, up_hbm, down_hbm, vec_ref, eout_ref,
        egrad_ref, ffn_mine, ffn_other, out_mine, out_other, pre_grad, hidden, shared_grad, logit,
        up_ref, down_ref, sems,
    ):
        @pl.when(pl.program_id(0) == 0)
        def _():
            first = pl.multiple_of(core_ref[0] * (units - cut), 128)
            copies = [
                pltpu.make_async_copy(
                    up_hbm.at[at, :, pl.ds(first, units)],
                    up_ref.at[:, pl.ds(at * units, units)],
                    sems.at[at],
                )
                for at in range(2)
            ]
            copies.append(
                pltpu.make_async_copy(down_hbm.at[pl.ds(first, units)], down_ref, sems.at[2])
            )
            for copy in copies:
                copy.start()
            for copy in copies:
                copy.wait()

        unit = lax.broadcasted_iota(jnp.int32, (tile, units), 1)
        ours = (unit >= cut) | (core_ref[0] == 0)
        x = jnp.concatenate([x_mine[0], x_other[0]])
        pre = kdot(x, up_ref[...], nn)
        gate_shared = jax.nn.sigmoid(
            jnp.sum(x.astype(floats) * vec_ref[...], axis=-1, keepdims=True)
        )
        grads = jnp.concatenate([g_mine[0], g_other[0]]).astype(floats)
        low_grad = (gate_shared * grads).astype(halves)
        shared_grad[...] = low_grad
        grad = jnp.where(ours, kdot(low_grad, down_ref[...], nt), 0.0)
        gate_pre, up_pre = pre[:, :units], pre[:, units:]
        sigma = jax.nn.sigmoid(gate_pre)
        act = gate_pre * sigma
        hid = jnp.where(ours, act * up_pre, 0.0).astype(halves)
        hidden[...] = hid
        pre_grad[:, :units] = (grad * up_pre * sigma * (1.0 + gate_pre * (1.0 - sigma))).astype(halves)
        pre_grad[:, units:] = (grad * act).astype(halves)
        picks = lax.broadcasted_iota(jnp.int32, (tile, capacity), 1) == slot_ref[...]
        pick = jnp.where(picks, 1.0, 0.0).astype(halves)
        ffn = kdot(pre_grad[...], up_ref[...], nt) + kdot(pick, egrad_ref[...], nn)
        ffn_mine[0], ffn_other[0] = ffn[:half].astype(halves), ffn[half:].astype(halves)
        shared_out = kdot(hid, down_ref[...], nn)
        logit[...] = jnp.sum(grads * shared_out, axis=-1, keepdims=True)
        out = gate_shared * shared_out + gate_ref[...] * kdot(pick, eout_ref[...], nn)
        out_mine[0], out_other[0] = out[:half].astype(halves), out[half:].astype(halves)

    shape = jax.ShapeDtypeStruct
    rows = lambda n: pl.BlockSpec((tile, n), lambda i: (i, 0))
    whole = lambda a: pl.BlockSpec(a.shape, lambda i: (0,) * a.ndim)
    slots = pl.BlockSpec((capacity, width), lambda i: (i, 0))
    halfs = pl.BlockSpec((1, half, width), lambda i: (i, 0, 0))
    half_shape = shape((pairs, half, width), halves)
    return kernel_call(
        kernel,
        (half_shape,) * 4
        + (
            shape((length, 2 * units), halves),
            shape((length, units), halves),
            shape((length, width), halves),
            shape((length, 1), floats),
        ),
        [
            pl.BlockSpec(memory_space=pltpu.SMEM),
            rows(1), rows(1), halfs, halfs, halfs, halfs,
            pl.BlockSpec(memory_space=pl.ANY),
            pl.BlockSpec(memory_space=pl.ANY),
            whole(vector), slots, slots,
        ],
        (halfs,) * 4 + (rows(2 * units), rows(units), rows(width), rows(1)),
        2 * length * width * units * 6,
        grid=(pairs,),
        scratch=[
            pltpu.VMEM((width, 2 * units), halves),
            pltpu.VMEM((units, width), halves),
            pltpu.SemaphoreType.DMA((3,)),
        ],
    )(core, slot_col, gate_col, *rows_in, *grads_in, up, down, vector, expert_out, expert_grad)


def weight_grad(*pairs):
    tile = 256
    lefts = [left if isinstance(left, tuple) else (left,) for left, _ in pairs]
    rights = [right for _, right in pairs]
    rows = lefts[0][0].shape[-1]
    depth = rights[0].shape[0]
    steps = [right.shape[1] // tile for right in rights]
    starts = [sum(steps[:i]) for i in range(len(steps))]

    def kernel(*refs):
        out, turned = refs[-2:]
        step = pl.program_id(0)
        at = 0
        for i, left in enumerate(lefts):
            left_refs, right_ref = refs[at : at + len(left)], refs[at + len(left)]
            at += len(left) + 1

            @pl.when(step == starts[i])
            def _():
                if len(left_refs) == 1:
                    turned[...] = left_refs[0][...].T
                else:
                    each = left_refs[0].shape[1]
                    for block in range(depth // each):
                        part = left_refs[block % 2][block // 2]
                        turned[:, block * each : (block + 1) * each] = part.T

            @pl.when((step >= starts[i]) & (step < starts[i] + steps[i]))
            def _():
                out[...] = kdot(turned[...], right_ref[...], nn).astype(halves)

    specs, arrays = [], []
    for left, right, start, count in zip(lefts, rights, starts, steps):
        specs += [pl.BlockSpec(part.shape, lambda j, n=part.ndim: (0,) * n) for part in left]
        specs.append(
            pl.BlockSpec(
                (depth, tile), lambda j, a=start, n=count: (0, jnp.clip(j - a, 0, n - 1))
            )
        )
        arrays += [*left, right]
    return kernel_call(
        kernel,
        jax.ShapeDtypeStruct((rows, sum(steps) * tile), halves),
        specs,
        pl.BlockSpec((rows, tile), lambda j: (0, j)),
        2 * depth * rows * sum(steps) * tile,
        grid=(sum(steps),),
        scratch=[pltpu.VMEM((rows, depth), halves)],
    )(*arrays)


def head_cut(qkv_weight, out_weight, vectors, ids, orders, gates):
    count = lax.axis_size(group)
    rows, wide = qkv_weight.shape
    width = wide // 3
    piece = width // count
    tokens, choices = ids.shape

    def kernel(weight_ref, ids_ref, orders_ref, gates_ref, vectors_ref, out):
        for g in range(count):
            for at in range(3):
                out[g, :, at * piece : (at + 1) * piece] = weight_ref[
                    :, at * width + g * piece : at * width + (g + 1) * piece
                ]
        order = orders_ref[...]
        gate = gates_ref[...]
        first = gate.astype(halves).astype(floats)
        second = (gate - first).astype(halves).astype(floats)
        parts = (ids_ref[...], order // 16, order % 16, first, second, gate - first - second)
        fill = jnp.zeros((tokens, 128 - choices * len(parts)), floats)
        turned = jnp.concatenate([part.astype(floats) for part in parts] + [fill], axis=1).T
        tile = jnp.concatenate(
            [turned[: choices * len(parts)], vectors_ref[...], jnp.zeros((32, 128), floats)]
        ).astype(halves)
        for g in range(count):
            out[g, :, 3 * piece :] = tile

    stacked = jnp.concatenate([vector.reshape(-1, rows).astype(floats) for vector in vectors])
    stacked = jnp.pad(stacked, ((0, 8 - stacked.shape[0]), (0, 128 - rows)))
    vmem = pl.BlockSpec(memory_space=pltpu.VMEM)
    cut = kernel_call(
        kernel,
        jax.ShapeDtypeStruct((count, rows, 3 * piece + 128), halves),
        [vmem] * 5,
        vmem,
        0,
    )(qkv_weight, ids, orders, gates, stacked)
    cut = lax.all_to_all(cut, group, split_axis=0, concat_axis=0, tiled=True)
    out = out_weight.reshape(rows, count, piece).transpose(1, 0, 2)
    return jnp.concatenate([cut, out], axis=-1)


def head_vectors(blocks, places):
    count, rows, wide = blocks[0].shape
    piece = (wide - 128) // 4
    half = count // 2
    whole = lambda out, at: out.at[:, at]
    low = lambda out, at: out.at[pl.ds(0, half), at]
    high = lambda out, at: out.at[pl.ds(half, half), at]
    packed = place_blocks(
        blocks, places, (count, 4, rows, 128), [whole] * 3 + [low, high], (3 * piece, 128)
    )
    lines = packed[..., 24:30, :rows].astype(floats)
    vectors = [lines[..., at, :].reshape(-1) for at in range(3)]
    vectors.append(lines[..., 3:, :].reshape(-1))
    return vectors


def rows_weights(qkv_weight, out_weight):
    return (
        lax.all_gather(qkv_weight, every, axis=0, tiled=True),
        lax.all_gather(out_weight, every, axis=0, tiled=True),
    )


def rows_forward(own_tokens, gain, bias, weights, seq_ids):
    weight, out_weight = weights
    tok_count, width = own_tokens.shape
    seq_len = seq_ids.shape[0]
    head_groups = HEADS // group_heads
    block_place = lax.axis_index(group)
    positions = block_place * tok_count + jnp.arange(tok_count, dtype=jnp.int32)
    cosine, sine = rope_tables(positions, HEAD_DIM // 2)
    scale = 1.0 / math.sqrt(HEAD_DIM)
    tokens = own_tokens.astype(floats)
    stat = lax.rsqrt(jnp.mean(tokens * tokens, axis=-1, keepdims=True) + eps_norm)
    unit = tokens * stat
    normed = (unit * gain).astype(halves)
    projected = dot(normed, weight) + bias
    raw = projected.reshape(tok_count, 3, HEADS, HEAD_DIM)
    query = (rotate(raw[:, 0], cosine, sine) * scale).astype(halves)
    key = rotate(raw[:, 1], cosine, sine).astype(halves)
    value = raw[:, 2].astype(halves)

    def by_group(array):
        return array.reshape(tok_count, head_groups, group_heads, HEAD_DIM).transpose(1, 0, 2, 3)

    query_groups = by_group(query)
    key_all = lax.all_gather(by_group(key), group, axis=1, tiled=True)
    value_all = lax.all_gather(by_group(value), group, axis=1, tiled=True)
    query_ids = lax.dynamic_slice_in_dim(seq_ids, block_place * tok_count, tok_count)
    key_places = jnp.arange(seq_len, dtype=jnp.int32)
    visible = (key_places[None, :] <= positions[:, None]) & (seq_ids[None, :] == query_ids[:, None])

    def attend_group(pieces):
        q_part, k_part, v_part = pieces
        scores = jnp.einsum("qhd,khd->hqk", q_part, k_part, preferred_element_type=floats)
        scores = jnp.where(visible[None], scores, neg_fill)
        top_score = jnp.max(scores, axis=-1, keepdims=True)
        grown = jnp.exp(scores - top_score)
        total = jnp.sum(grown, axis=-1, keepdims=True)
        probs_low = (grown / total).astype(halves)
        mixed = jnp.einsum("hqk,khd->qhd", probs_low, v_part, preferred_element_type=floats)
        return (mixed, top_score + jnp.log(total))

    mixed_groups, log_totals = lax.map(attend_group, (query_groups, key_all, value_all))
    attended = mixed_groups.transpose(1, 0, 2, 3).reshape(tok_count, width).astype(halves)
    saved = (normed, unit, query_groups, key_all, value_all, log_totals, attended, cosine, sine, visible)
    return dot(attended, out_weight), saved


def rows_backward(weights, saved, mid_low):
    weight, out_weight = weights
    normed, unit, query_groups, key_all, value_all, log_totals, attended, cosine, sine, visible = saved
    tok_count, width = mid_low.shape
    head_groups = HEADS // group_heads
    scale = 1.0 / math.sqrt(HEAD_DIM)
    attended_grad = dot_nt(mid_low, out_weight).astype(halves)
    grad_groups = attended_grad.reshape(tok_count, head_groups, group_heads, HEAD_DIM).transpose(
        1, 0, 2, 3
    )

    def attend_back(pieces):
        q_part, k_part, v_part, g_part, log_part = pieces
        scores = jnp.einsum("qhd,khd->hqk", q_part, k_part, preferred_element_type=floats)
        scores = jnp.where(visible[None], scores, neg_fill)
        probs = jnp.exp(scores - log_part)
        prob_grad = jnp.einsum("qhd,khd->hqk", g_part, v_part, preferred_element_type=floats)
        delta = jnp.sum(probs * prob_grad, axis=-1, keepdims=True)
        score_grad = (probs * (prob_grad - delta)).astype(halves)
        q_grad = jnp.einsum("hqk,khd->qhd", score_grad, k_part, preferred_element_type=floats)
        k_grad = jnp.einsum("hqk,qhd->khd", score_grad, q_part, preferred_element_type=floats)
        v_grad = jnp.einsum(
            "hqk,qhd->khd", probs.astype(halves), g_part, preferred_element_type=floats
        )
        return (q_grad, k_grad, v_grad)

    query_grads, key_grads, value_grads = lax.map(
        attend_back, (query_groups, key_all, value_all, grad_groups, log_totals)
    )
    key_grad = lax.psum_scatter(key_grads, group, scatter_dimension=1, tiled=True)
    value_grad = lax.psum_scatter(value_grads, group, scatter_dimension=1, tiled=True)

    def by_head(array):
        return array.transpose(1, 0, 2, 3).reshape(tok_count, HEADS, HEAD_DIM)

    proj_grad = jnp.concatenate(
        [
            rotate_back(by_head(query_grads) * scale, cosine, sine).reshape(tok_count, width),
            rotate_back(by_head(key_grad), cosine, sine).reshape(tok_count, width),
            by_head(value_grad).reshape(tok_count, width),
        ],
        axis=-1,
    ).astype(halves)
    bias_part = jnp.sum(proj_grad.astype(floats), axis=0)
    attn_in_grad = dot_nt(proj_grad, weight)
    gain_part = jnp.sum(attn_in_grad * unit, axis=0)
    qkv_out = lax.psum_scatter(dot_tn(normed, proj_grad), every, scatter_dimension=0, tiled=True)
    out_out = lax.psum_scatter(dot_tn(attended, mid_low), every, scatter_dimension=0, tiled=True)
    return attn_in_grad, gain_part, bias_part, qkv_out, out_out


def routing_of(expert_ids, slot_order, gate_weights, count, mark):
    tok_count, topk = expert_ids.shape[1:]
    routing = [expert_ids[0].reshape(-1), slot_order[0, 0], gate_weights[0].reshape(-1)]
    routing = jnp.concatenate([v.astype(floats) for v in routing]).reshape(1, -1, 128)
    routing = jnp.broadcast_to(routing, (count,) + routing.shape[1:])
    routing = lax.all_to_all(after(routing, mark), group, split_axis=0, concat_axis=0, tiled=True)
    routing = routing.reshape(count, 3, tok_count, topk)
    return routing[:, 0], routing[:, 1], routing[:, 2]


def slots_of(routes, index, capacity):
    pair_expert, pair_order, pair_gate = routes
    chosen = pair_expert == index.astype(floats)
    has_pair = jnp.any(chosen, axis=-1)
    order = jnp.sum(jnp.where(chosen, pair_order, 0.0), axis=-1)
    gate = jnp.sum(jnp.where(chosen, pair_gate, 0.0), axis=-1)
    earlier = has_pair[:, None, :] & (order[:, None, :] < order[:, :, None])
    rank = jnp.sum(earlier.astype(jnp.int32), axis=-1)
    kept = has_pair & (rank < capacity)
    return rank, kept, jnp.where(kept, gate, 0.0)


def small_sums(parts, lengths, mark):
    devices = lax.axis_size(every)
    packed = jnp.concatenate([part.reshape(devices, -1) for part in parts], axis=1)
    packed = jnp.pad(after(packed, mark), ((0, 0), (0, -packed.shape[1] % 128)))
    packed = lax.all_to_all(
        packed.reshape(devices, -1, 128), every, split_axis=0, concat_axis=0, tiled=True
    )
    sums = jnp.sum(packed, axis=0).reshape(-1)
    out, at = [], 0
    for size in lengths:
        out.append(sums[at : at + size])
        at += size
    return out


def norm_backward(grad_out, grads, gain, unit, stat):
    unit_grad = grads * gain
    return grad_out + stat * (unit_grad - unit * jnp.mean(unit_grad * unit, axis=-1, keepdims=True))


def halves_of(array, axis, which):
    size = array.shape[axis] // 2
    return lax.dynamic_slice_in_dim(array, which * size, size, axis)


def entry(array, which):
    return lax.dynamic_index_in_dim(array, which, 0, keepdims=False)


def shards_by_heads(
    tokens,
    cotangent,
    segments,
    expert_ids,
    slot_order,
    gate_weights,
    qkv_weight,
    qkv_bias,
    out_weight,
    norm_attn,
    norm_ffn,
    shared_gate_up,
    shared_down,
    shared_gate,
    expert_gate_up,
    expert_down,
):
    count = lax.axis_size(group)
    core = lax.axis_index("context")
    place = lax.axis_index("dp")
    index = lax.axis_index(group)
    tok_count, width = tokens.shape[1:]
    pairs = tok_count * expert_ids.shape[2]
    experts = expert_gate_up.shape[0] * lax.axis_size("expert")
    capacity = (9 * pairs + 8 * experts - 1) // (8 * experts)
    length = count * tok_count
    core_at = jnp.stack([core, lax.axis_index("expert")]).astype(jnp.int32)
    vectors = [norm_attn, norm_ffn, shared_gate, qkv_bias]
    lengths = [vector.shape[0] for vector in vectors]
    own_tokens = tokens[0]
    resid_in = own_tokens.astype(floats)

    both = ("context", "dp")
    shared_dn = lax.all_gather(shared_down, both, axis=1, tiled=True)
    ed_first = entry(expert_down, core)
    ed_second = other_core(entry(expert_down, 1 - core))
    ed_first_x, ed_first_y = near_blocks(ed_first)
    cut = after(
        head_cut(
            qkv_weight,
            out_weight,
            vectors,
            expert_ids[0],
            slot_order.reshape(tok_count, -1),
            gate_weights[0],
        ),
        ed_first_x,
        ed_first_y,
        ed_second,
    )
    all_tokens = lax.all_gather(after(own_tokens, cut, shared_dn), group, axis=0, tiled=True)
    cut_x, cut_y = near_blocks(cut)
    half = count // 2
    cut_far = dp_step(cut_x[:half], 2), dp_step(cut_y[half:], 1)
    blocks = [cut, cut_x, cut_y, *cut_far]
    places = [place, place ^ 1, place ^ 2, place ^ 3, place ^ 3]
    gain_attn, gain_ffn, gate_vector, bias = head_vectors(blocks, places)
    grads_mine = line_blocks(after(cotangent[0], all_tokens))
    expert_up = lax.all_gather(after(expert_gate_up, cut_x, cut_y), both, axis=1, tiled=True)
    piece = width // count
    inverse = rope_base ** (-2.0 * np.arange(HEAD_DIM // 2) / HEAD_DIM)
    angle = np.arange(length)[:, None] * inverse[None, :]
    cosine = np.concatenate([np.cos(angle), np.cos(angle)], axis=-1).astype(np.float32)
    sine = np.concatenate([-np.sin(angle), np.sin(angle)], axis=-1).astype(np.float32)
    seg_row = segments.astype(jnp.int32)
    seg_col = seg_row.reshape(length, 1)
    own_bias = lax.dynamic_index_in_dim(bias.reshape(3, count, piece), index, 1, keepdims=False)
    weight, out_rows, normed, query, key, value = attention_project(
        jnp.stack(places).astype(jnp.int32),
        all_tokens,
        gain_attn.reshape(1, width),
        blocks,
        own_bias.reshape(1, 3 * piece),
        cosine,
        sine,
    )
    ed_first_far = dp_step(after(ed_first_x, *cut_far), 2)
    ed_second_x, ed_second_y = near_blocks(after(ed_second, *cut_far))
    lse, attended, mine, other = attention_mix(
        core_at, after(query, *grads_mine, ed_first_far, ed_second_x, ed_second_y), key, value, seg_col, seg_row, out_rows
    )
    grads_mine = jnp.stack(grads_mine)

    slot_row, gate_row, slot_col, gate_col = slot_table(
        jnp.stack([after(core, query), lax.axis_index("expert"), index]).astype(jnp.int32),
        cut[:, :24, 3 * piece : 3 * piece + 128].astype(floats),
        capacity,
    )
    other = other_core(after(other, slot_row, slot_col, gate_row, gate_col))
    ed_second_far = dp_step(ed_second_y, 1)
    mixed = line_sum(mine, other)
    shared_up = lax.all_gather(after(shared_gate_up, attended), both, axis=1, tiled=True)

    resid_mid = resid_in + mixed
    stat_ffn = lax.rsqrt(jnp.mean(resid_mid * resid_mid, axis=-1, keepdims=True) + eps_norm)
    unit_ffn = resid_mid * stat_ffn
    normed_ffn = (unit_ffn * gain_ffn).astype(halves)
    grad_out = cotangent[0].astype(floats)
    all_grads = (grads_mine, other_core(after(grads_mine, mine)))
    normed_mine = line_gather(normed_ffn, ed_second_far, all_grads[1])
    all_normed = (normed_mine, other_core(normed_mine))

    expert_out, expert_grad, eu_term, ed_term = expert_pass(
        slot_row,
        gate_row,
        all_normed,
        all_grads,
        expert_up,
        [ed_first, ed_first_x, ed_first_y, ed_first_far]
        + [ed_second, ed_second_x, ed_second_y, ed_second_far],
        jnp.stack(
            [4 * which + (place ^ step) for which in (core, 1 - core) for step in range(4)] + [core]
        ).astype(jnp.int32),
        2 * capacity,
    )
    ffn_mine, ffn_other, out_mine, out_other, sh_pre_grad, sh_hidden, sh_grad, logit_part = shared_pass(
        core_at,
        slot_col,
        gate_col,
        (after(all_normed[0], eu_term, ed_term), all_normed[1]),
        all_grads,
        shared_up,
        shared_dn,
        gate_vector.reshape(1, width),
        expert_out,
        expert_grad,
    )
    ffn_other = other_core(ffn_other)
    eu_sum = sum_weight(eu_term)

    ffn_grad = line_sum(ffn_mine, ffn_other)
    logit_part = further_on(logit_part.reshape(-1, 2, tok_count), True)
    logit_sums = lax.all_to_all(
        after(logit_part.reshape(count, 1, tok_count), ffn_other),
        group,
        split_axis=0,
        concat_axis=0,
        tiled=True,
    )
    own_gate = jax.nn.sigmoid(
        jnp.sum(normed_ffn.astype(floats) * gate_vector, axis=-1, keepdims=True)
    )
    logit_grad = jnp.sum(logit_sums, axis=0).reshape(tok_count, 1) * own_gate * (1.0 - own_gate)
    ffn_grad = ffn_grad + logit_grad * gate_vector
    gain_ffn_part = jnp.sum(ffn_grad * unit_ffn, axis=0)
    gate_vector_part = jnp.sum(logit_grad * normed_ffn.astype(floats), axis=0)
    mid_grad = norm_backward(grad_out, ffn_grad, gain_ffn, unit_ffn, stat_ffn)
    mid_low = mid_grad.astype(halves)
    sh_term = weight_grad((all_normed, after(sh_pre_grad, mid_low)), (sh_grad, sh_hidden))
    sh_sum = sum_weight(sh_term)

    out_got = other_core(out_other)
    mid_mine = line_gather(mid_low, eu_sum, out_got, sh_term)
    mid_other = other_core(mid_mine)
    proj_grad, mine, other, gain_attn_part, bias_part, out_part = attention_backward(
        core_at, mid_mine, mid_other, all_tokens, weight, cosine, sine, seg_col, seg_row, out_rows,
        query, key, value, lse, attended,
    )
    other = other_core(other)
    rows = other
    small = small_sums(
        [
            gain_attn_part,
            gain_ffn_part,
            gate_vector_part,
            lax.dynamic_update_slice(
                jnp.zeros((3, count, piece), floats), bias_part.reshape(3, 1, piece), (0, index, 0)
            ),
        ],
        lengths,
        rows,
    )
    attn_in_grad = line_sum(mine, other, *small)
    weight_part = weight_grad((normed, after(proj_grad, other))).reshape(count, -1, 3 * piece)
    out_part = out_part.reshape(-1, count, piece).transpose(1, 0, 2)
    ed_sum = sum_weight(after(ed_term, weight_part))
    total = lax.psum_scatter(
        jnp.concatenate([weight_part, out_part], axis=-1), "dp", scatter_dimension=1, tiled=True
    )
    qkv_total = lax.all_to_all(
        after(total[..., : 3 * piece], attn_in_grad), group, split_axis=0, concat_axis=0, tiled=True
    )
    each = qkv_weight.shape[0]
    qkv_out = (
        qkv_total.reshape(count, each, 3, piece)
        .transpose(1, 2, 0, 3)
        .reshape(each, 3 * width)
        .astype(floats)
    )
    out_weight_out = total[..., 3 * piece :].transpose(1, 0, 2).reshape(each, width).astype(floats)
    layer_sum = resid_mid + line_sum(out_mine, after(out_got, attn_in_grad))
    stat_attn = lax.rsqrt(jnp.mean(resid_in * resid_in, axis=-1, keepdims=True) + eps_norm)
    unit_attn = resid_in * stat_attn
    input_grad = norm_backward(mid_grad, attn_in_grad, gain_attn, unit_attn, stat_attn)

    eu_sum, ed_sum = after(eu_sum, rows), after(ed_sum, attn_in_grad)
    sh_sum = after(sh_sum, attn_in_grad)
    got = other_core(entry(sh_sum, 1 - core))
    shared_up_out, shared_down_out = unpack_shared(
        core_at, sh_sum, got, shared_gate_up.shape[2]
    )
    gain_attn_out, gain_ffn_out, gate_vector_out, bias_out = small
    return (
        layer_sum.astype(halves)[None],
        input_grad[None],
        qkv_out,
        bias_out,
        out_weight_out,
        gain_attn_out,
        gain_ffn_out,
        shared_up_out,
        shared_down_out,
        gate_vector_out,
        jnp.stack(cores_in_order(eu_sum)).astype(floats),
        jnp.stack(cores_in_order(ed_sum)).astype(floats),
    )


def shards_by_rows(
    tokens,
    cotangent,
    segments,
    expert_ids,
    slot_order,
    gate_weights,
    qkv_weight,
    qkv_bias,
    out_weight,
    norm_attn,
    norm_ffn,
    shared_gate_up,
    shared_down,
    shared_gate,
    expert_gate_up,
    expert_down,
):
    count = lax.axis_size(group)
    core = lax.axis_index("context")
    index = lax.axis_index(group)
    tok_count, width = tokens.shape[1:]
    pairs = tok_count * expert_ids.shape[2]
    experts = expert_gate_up.shape[0] * lax.axis_size("expert")
    capacity = (9 * pairs + 8 * experts - 1) // (8 * experts)
    length = count * tok_count
    vectors = [norm_attn, norm_ffn, shared_gate, qkv_bias]
    lengths = [vector.shape[0] for vector in vectors]
    payload = jnp.concatenate([vector.astype(floats) for vector in vectors])
    small = spread(jnp.pad(payload, (0, -payload.shape[0] % 128)))
    gathered = []
    for at, size in enumerate(lengths):
        first = sum(lengths[:at])
        gathered.append(small[:, first : first + size].reshape(-1))
    gain_attn, gain_ffn, gate_vector, bias = gathered
    routes = routing_of(expert_ids, slot_order, gate_weights, count, small)

    resid_in = tokens[0].astype(floats)
    weights = rows_weights(qkv_weight, out_weight)
    mixed, saved = rows_forward(tokens[0], gain_attn, bias, weights, segments[0])

    def gate_up_half(which):
        part = halves_of(shared_gate_up, 2, which)
        return jnp.concatenate([part[0], part[1]], axis=-1)

    def down_half(which):
        return halves_of(shared_down, 0, which).T

    expert_up = gather_rows(both_cores(entry(expert_gate_up, core), entry(expert_gate_up, 1 - core)))
    expert_dn = gather_rows(both_cores(entry(expert_down, core), entry(expert_down, 1 - core)))
    shared_up = gather_rows(both_cores(gate_up_half(core), gate_up_half(1 - core)))
    shared_dn = gather_rows(both_cores(down_half(core), down_half(1 - core)))
    ff_width = expert_dn.shape[0]
    units = shared_dn.shape[1]

    resid_mid = resid_in + mixed
    stat_ffn = lax.rsqrt(jnp.mean(resid_mid * resid_mid, axis=-1, keepdims=True) + eps_norm)
    unit_ffn = resid_mid * stat_ffn
    normed_ffn = (unit_ffn * gain_ffn).astype(halves)
    grad_out = cotangent[0].astype(floats)
    all_grads = gather_cores(gather_line(cotangent[0]))
    all_normed = gather_cores(gather_line(normed_ffn))

    rank, kept, gate = slots_of(routes, index, capacity)
    slots = jnp.arange(capacity, dtype=jnp.int32)
    select = (rank[:, None, :] == slots[None, :, None]) & kept[:, None, :]
    slot_gate = jnp.sum(jnp.where(select, gate[:, None, :], 0.0), axis=-1).reshape(-1, 1)
    select = select.astype(halves)

    def to_slots(rows):
        rows = rows.reshape(count, tok_count, width)
        got = jnp.einsum("brt,btd->brd", select, rows, preferred_element_type=floats)
        return got.reshape(count * capacity, width)

    def from_slots(rows):
        rows = rows.reshape(count, capacity, width)
        got = jnp.einsum("brt,brd->btd", select, rows, preferred_element_type=floats)
        return got.reshape(length, width)

    slot_in = to_slots(all_normed).astype(halves)
    slot_grad = (to_slots(all_grads) * slot_gate).astype(halves)
    expert_pre = dot(slot_in, expert_up)
    expert_g, expert_u = expert_pre[:, :ff_width], expert_pre[:, ff_width:]
    expert_hidden = (jax.nn.silu(expert_g) * expert_u).astype(halves)
    hidden_grad = dot_nt(slot_grad, expert_dn)
    expert_pre_grad = jnp.concatenate(
        silu_parts(hidden_grad, expert_g, expert_u), axis=-1
    ).astype(halves)
    expert_out = dot(expert_hidden, expert_dn).astype(halves)
    slot_in_grad = dot_nt(expert_pre_grad, expert_up).astype(halves)
    eu_sum = sum_weight(dot_tn(slot_in, expert_pre_grad).astype(halves))
    ed_sum = sum_weight(dot_tn(expert_hidden, slot_grad).astype(halves))

    shared_pre = dot(all_normed, shared_up)
    shared_g, shared_u = shared_pre[:, :units], shared_pre[:, units:]
    shared_hidden = (jax.nn.silu(shared_g) * shared_u).astype(halves)
    gate_shared = jax.nn.sigmoid(
        jnp.sum(all_normed.astype(floats) * gate_vector, axis=-1, keepdims=True)
    )
    shared_grad = (gate_shared * all_grads.astype(floats)).astype(halves)
    hidden_grad = dot(shared_grad, shared_dn)
    shared_pre_grad = jnp.concatenate(
        silu_parts(hidden_grad, shared_g, shared_u), axis=-1
    ).astype(halves)
    shared_part = dot_nt(shared_hidden, shared_dn)
    logit_part = jnp.sum(all_grads.astype(floats) * shared_part, axis=-1)
    su_sum = sum_weight(dot_tn(all_normed, shared_pre_grad).astype(halves))
    sd_sum = sum_weight(dot_tn(shared_grad, shared_hidden).astype(halves))
    ffn_part = dot_nt(shared_pre_grad, shared_up) + from_slots(slot_in_grad)
    out_part = gate_shared * shared_part + gate.reshape(length, 1) * from_slots(expert_out)

    logit_sums = lax.all_to_all(
        logit_part.reshape(count, 1, tok_count), group, split_axis=0, concat_axis=0, tiled=True
    )
    own_gate = jax.nn.sigmoid(
        jnp.sum(normed_ffn.astype(floats) * gate_vector, axis=-1, keepdims=True)
    )
    logit_grad = jnp.sum(logit_sums, axis=0).reshape(tok_count, 1) * own_gate * (1.0 - own_gate)

    def own_sum(part):
        part = part.reshape(-1, 2, tok_count, width)
        mine = lax.dynamic_index_in_dim(part, core, 1, keepdims=False)
        other = lax.dynamic_index_in_dim(part, 1 - core, 1, keepdims=False)
        return group_sum(mine, other.astype(halves))

    layer_sum = resid_mid + own_sum(out_part)
    ffn_grad = own_sum(ffn_part) + logit_grad * gate_vector
    gain_ffn_part = jnp.sum(ffn_grad * unit_ffn, axis=0)
    gate_vector_part = jnp.sum(logit_grad * normed_ffn.astype(floats), axis=0)
    mid_grad = norm_backward(grad_out, ffn_grad, gain_ffn, unit_ffn, stat_ffn)
    mid_low = mid_grad.astype(halves)

    attn_in_grad, gain_attn_part, bias_part, qkv_out, out_weight_out = rows_backward(
        weights, saved, mid_low
    )
    stat_attn = lax.rsqrt(jnp.mean(resid_in * resid_in, axis=-1, keepdims=True) + eps_norm)
    unit_attn = resid_in * stat_attn
    input_grad = norm_backward(mid_grad, attn_in_grad, gain_attn, unit_attn, stat_attn)
    shared_up_out = jnp.concatenate(
        [
            array.reshape(-1, 2, units).transpose(1, 0, 2) for array in cores_in_order(su_sum)
        ],
        axis=-1,
    )
    gain_attn_out, gain_ffn_out, gate_vector_out, bias_out = small_sums(
        [gain_attn_part, gain_ffn_part, gate_vector_part, bias_part], lengths, attn_in_grad
    )
    return (
        layer_sum.astype(halves)[None],
        input_grad[None],
        qkv_out,
        bias_out,
        out_weight_out,
        gain_attn_out,
        gain_ffn_out,
        shared_up_out.astype(floats),
        jnp.concatenate(cores_in_order(sd_sum), axis=-1).T.astype(floats),
        gate_vector_out,
        jnp.stack(cores_in_order(eu_sum)).astype(floats),
        jnp.stack(cores_in_order(ed_sum)).astype(floats),
    )


def shards(*arrays):
    if HEADS % lax.axis_size(group) == 0 and lax.axis_size("dp") == 4 and lax.axis_size("expert") == 4:
        return shards_by_heads(*arrays)
    return shards_by_rows(*arrays)


def solution(mesh):
    placed = (
        P("dp", ("expert", "context"), None),
        P("dp", ("expert", "context"), None),
        P("dp", None),
        P("dp", ("expert", "context"), None),
        P("dp", ("expert", "context"), None),
        P("dp", ("expert", "context"), None),
        P(("expert", "context", "dp"), None),
        P(("expert", "context", "dp")),
        P(("expert", "context", "dp"), None),
        P(("expert", "context", "dp")),
        P(("expert", "context", "dp")),
        P(None, ("context", "dp"), "expert"),
        P("expert", ("context", "dp")),
        P(("expert", "context", "dp")),
        P("expert", ("context", "dp"), None),
        P("expert", ("context", "dp"), None),
    )
    return jax.shard_map(
        shards,
        mesh=mesh,
        in_specs=placed,
        out_specs=(
            P("dp", ("expert", "context"), None),
            P("dp", ("expert", "context"), None),
            P(("expert", "context", "dp"), None),
            P(("expert", "context", "dp")),
            P(("expert", "context", "dp"), None),
            P(("expert", "context", "dp")),
            P(("expert", "context", "dp")),
            P(None, ("context", "dp"), "expert"),
            P("expert", ("context", "dp")),
            P(("expert", "context", "dp")),
            P("expert", ("context", "dp"), None),
            P("expert", ("context", "dp"), None),
        ),
        check_vma=False,
    )
```
